256 devices in a mesh: gx: 32 (over z, x), gy: 8 (over y, core).
Axes of the slice: x: 4, y: 4, z: 8, core: 2. Of those that a mesh axis runs over, the one named last changes fastest.
Arguments:
- populations: float32 [19, 512, 128, 128], P(None, 'gx', 'gy'), as said below
- relax_matrix: float32 [19, 19], replicated, as said below
- grain_state: float32 [32, 8, 4, 128], P('gx', 'gy'), as said below
- link_cell: int32 [32, 8, 16384], P('gx', 'gy'), may hold values from 0 to 32671, as said below
- link_dir: int32 [32, 8, 16384], P('gx', 'gy'), may hold values from 0 to 18, as said below
- link_grain: int32 [32, 8, 16384], P('gx', 'gy'), may hold values from 0 to 1151, as said below
- contact_self: int32 [32, 8, 512], P('gx', 'gy'), may hold values from 0 to 128, as said below
- contact_peer: int32 [32, 8, 512], P('gx', 'gy'), may hold values from 0 to 1151, as said below
- contact_normal: float32 [32, 8, 3, 512], P('gx', 'gy'), may hold values from -4 to 4
- contact_gap: float32 [32, 8, 512], P('gx', 'gy'), may hold values from -3 to 3
Outputs:
- populations_next: float32 [19, 512, 128, 128], P(None, 'gx', 'gy')
- grain_force: float32 [32, 8, 3, 128], P('gx', 'gy')
- grain_velocity: float32 [32, 8, 3, 128], P('gx', 'gy')
- contact_impulse: float32 [32, 8, 512], P('gx', 'gy')
The draws below stay inside these ranges and needn't reach their ends.
Inputs may be any that keep to these rules, and one draw needn't show every extreme that they name: `populations`: positive in every cell and direction. `relax_matrix`: diagonal entries 0.8 to 1.7; off-diagonal entries of magnitude at most 0.1. `grain_state`: row 3 lies between 0.1 and 1. `link_cell`: A local cell number (x * 16 + y) * 128 + z of the block's own cells, with z below 32. `link_dir`: direction 0 marks an empty slot; the live slots of a block come first. `link_grain`: encoded as a block offset dx, dy in -1, 0, 1 and a slot. `contact_self`: the value 128 marks an empty slot; the live slots of a block come first. `contact_peer`: encoded as a block offset dx, dy in -1, 0, 1 and a slot; never the contact's own grain.
All inputs are finite; a program needn't handle non-finite values.
Results may differ from the reference program's by a relative error of at most 0.00023.
Values sent between devices are 32-bit elements; how exact they have to be, the bound alone decides.
No kernel may reach another device: no remote copies, remote signals or barrier semaphores. Data moves between devices by JAX's collectives and lax.ppermute only.
A program may use at most 64 MiB of HBM per device.

```python
import jax
import jax.numpy as jnp
from jax import lax

CX = 16
CY = 16
CZ = 128
GRAIN_DEV = 128
LINK_DEV = 16384
CONT_DEV = 512
SWEEPS = 4
NX = 512
NY = 128
GRAINS = 32768
N_GX = 32
N_GY = 8


lattice_weights = [1.0 / 3.0] + [1.0 / 18.0] * 6 + [1.0 / 36.0] * 12


def draw_populations(key, part):
    key = jax.random.fold_in(key, 1)
    weight = jnp.array(lattice_weights, jnp.float32)[:, None, None, None]
    return weight * jnp.exp(0.3 * jax.random.normal(key, (19, NX, NY, CZ), jnp.float32))


def draw_relax_matrix(key, part):
    key = jax.random.fold_in(key, 2)
    first_key, second_key = jax.random.split(key)
    diagonal = jax.random.uniform(first_key, (19,), jnp.float32, 0.8, 1.6)
    offdiag = jax.random.uniform(second_key, (19, 19), jnp.float32, -0.08, 0.08)
    identity = (lax.broadcasted_iota(jnp.int32, (19, 19), 0) == lax.broadcasted_iota(jnp.int32, (19, 19), 1)).astype(jnp.float32)
    return offdiag * (1.0 - identity) + identity * diagonal[:, None]


def draw_grain_state(key, part):
    key = jax.random.fold_in(key, 3)
    first_key, second_key = jax.random.split(key)
    speeds = 0.5 * jax.random.normal(first_key, (N_GX, N_GY, 3, GRAIN_DEV), jnp.float32)
    inverse = jnp.exp(jax.random.uniform(second_key, (N_GX, N_GY, 1, GRAIN_DEV), jnp.float32, -2.302585, 0.0))
    return jnp.concatenate([speeds, inverse], axis=2)


def link_tables(key):
    keys = jax.random.split(jax.random.fold_in(key, 40), 7)
    blocks = N_GX * N_GY
    counts = jax.random.randint(keys[0], (blocks,), LINK_DEV // 4, LINK_DEV + 1)
    fullest = jax.random.randint(keys[1], (), 0, blocks)
    counts = jnp.where(jnp.arange(blocks) == fullest, LINK_DEV, counts)
    slot_pos = lax.broadcasted_iota(jnp.int32, (blocks, LINK_DEV), 1)
    live = slot_pos < counts[:, None]
    coord_x = jax.random.randint(keys[2], (blocks, LINK_DEV), 0, CX)
    coord_y = jax.random.randint(keys[3], (blocks, LINK_DEV), 0, CY)
    coord_z = jax.random.randint(keys[4], (blocks, LINK_DEV), 0, CZ // 4)
    cells = (coord_x * CY + coord_y) * CZ + coord_z
    dirs = jnp.where(live, jax.random.randint(keys[5], (blocks, LINK_DEV), 1, 19), 0)
    grains = jax.random.randint(keys[6], (blocks, LINK_DEV), 0, 9 * GRAIN_DEV)
    shape = (N_GX, N_GY, LINK_DEV)
    return (cells.reshape(shape), dirs.reshape(shape), grains.reshape(shape))


def draw_link_cell(key, part):
    return link_tables(key)[0]


def draw_link_dir(key, part):
    return link_tables(key)[1]


def draw_link_grain(key, part):
    return link_tables(key)[2]


def contact_tables(key):
    keys = jax.random.split(jax.random.fold_in(key, 50), 4)
    blocks = N_GX * N_GY
    counts = jax.random.randint(keys[0], (blocks,), CONT_DEV // 2, CONT_DEV + 1)
    fullest = jax.random.randint(keys[1], (), 0, blocks)
    counts = jnp.where(jnp.arange(blocks) == fullest, CONT_DEV, counts)
    slot_pos = lax.broadcasted_iota(jnp.int32, (blocks, CONT_DEV), 1)
    live = slot_pos < counts[:, None]
    own_slot = jax.random.randint(keys[2], (blocks, CONT_DEV), 0, GRAIN_DEV)
    peers = jax.random.randint(keys[3], (blocks, CONT_DEV), 0, 9 * GRAIN_DEV)
    clash = peers == 4 * GRAIN_DEV + own_slot
    peers = jnp.where(clash, (peers + GRAIN_DEV) % (9 * GRAIN_DEV), peers)
    own_slot = jnp.where(live, own_slot, GRAIN_DEV)
    shape = (N_GX, N_GY, CONT_DEV)
    return (own_slot.reshape(shape), peers.reshape(shape))


def draw_contact_self(key, part):
    return contact_tables(key)[0]


def draw_contact_peer(key, part):
    return contact_tables(key)[1]


def level_of(key, dims, shards, low, high):
    gain = 1.0
    for position, blocks in shards:
        heights = jax.random.uniform(jax.random.fold_in(jax.random.fold_in(key, 6), position), (blocks,), jnp.float32, low / len(shards), high / len(shards))
        gain = gain * jnp.repeat(jnp.exp(heights), dims[position] // blocks).reshape((-1,) + (1,) * (len(dims) - 1 - position))
    return gain


def centred(rng, extent, spread, reach, cuts=(), dtype=jnp.bfloat16):
    drawn = spread * jax.random.normal(rng, extent, jnp.float32)
    if cuts:
        drawn = drawn * level_of(rng, extent, cuts, -0.22, 0.18)
    return jnp.clip(drawn, -reach, reach).astype(dtype)


def setup_inputs(seed: int = 0) -> dict:
    streams_of = jax.random.split(jax.random.key(seed), 11)
    populations = draw_populations(jax.random.fold_in(streams_of[10], 71), 0)
    relax_matrix = draw_relax_matrix(jax.random.fold_in(streams_of[10], 71), 0)
    grain_state = draw_grain_state(jax.random.fold_in(streams_of[10], 71), 0)
    link_cell = draw_link_cell(jax.random.fold_in(streams_of[10], 71), 0)
    link_dir = draw_link_dir(jax.random.fold_in(streams_of[10], 71), 0)
    link_grain = draw_link_grain(jax.random.fold_in(streams_of[10], 71), 0)
    contact_self = draw_contact_self(jax.random.fold_in(streams_of[10], 71), 0)
    contact_peer = draw_contact_peer(jax.random.fold_in(streams_of[10], 71), 0)
    contact_normal = centred(streams_of[8], (N_GX, N_GY, 3, CONT_DEV), 0.6, 4.0, ((0, 32), (1, 8)), jnp.float32)
    contact_gap = centred(streams_of[9], (N_GX, N_GY, CONT_DEV), 0.3, 3.0, ((0, 32), (1, 8)), jnp.float32)
    return {"populations": populations, "relax_matrix": relax_matrix, "grain_state": grain_state, "link_cell": link_cell, "link_dir": link_dir, "link_grain": link_grain, "contact_self": contact_self, "contact_peer": contact_peer, "contact_normal": contact_normal, "contact_gap": contact_gap}


lattice_dirs = [[0, 0, 0], [1, 0, 0], [-1, 0, 0], [0, 1, 0], [0, -1, 0], [0, 0, 1], [0, 0, -1],
                [1, 1, 0], [-1, -1, 0], [1, -1, 0], [-1, 1, 0], [1, 0, 1], [-1, 0, -1], [1, 0, -1],
                [-1, 0, 1], [0, 1, 1], [0, -1, -1], [0, 1, -1], [0, -1, 1]]
lattice_weights = [1.0 / 3.0] + [1.0 / 18.0] * 6 + [1.0 / 36.0] * 12
opposite_list = [0, 2, 1, 4, 3, 6, 5, 8, 7, 10, 9, 12, 11, 14, 13, 16, 15, 18, 17]
under_relax = 0.5
highest = lax.Precision.HIGHEST


def lattice_tables():
    velocity = jnp.array(lattice_dirs, jnp.float32).T
    weight = jnp.array(lattice_weights, jnp.float32)
    return velocity, weight


def opposite(dirs):
    return jnp.where(dirs == 0, 0, jnp.where(dirs % 2 == 1, dirs + 1, dirs - 1))


def collide(flat, relax_matrix):
    velocity, weight = lattice_tables()
    density = jnp.sum(flat, axis=0)
    momentum = jnp.dot(velocity, flat, precision=highest)
    speed = momentum / density
    along = jnp.dot(velocity.T, speed, precision=highest)
    square = jnp.sum(speed * speed, axis=0)
    equilibrium = weight[:, None] * density * (1.0 + 3.0 * along + 4.5 * along * along - 1.5 * square)
    return flat - jnp.dot(relax_matrix, flat - equilibrium, precision=highest)


def global_grain(frame_index, block_x, block_y):
    frame_pos = frame_index // GRAIN_DEV
    owner_x = (block_x + frame_pos // 3 - 1) % N_GX
    owner_y = (block_y + frame_pos % 3 - 1) % N_GY
    return (owner_x * N_GY + owner_y) * GRAIN_DEV + frame_index % GRAIN_DEV


def reference(populations, relax_matrix, grain_state, link_cell, link_dir, link_grain, contact_self, contact_peer, contact_normal, contact_gap):
    moved = jnp.moveaxis(populations, 1, 0)

    def collide_slab(slab):
        return collide(slab.reshape(19, NY * CZ), relax_matrix).reshape(19, NY, CZ)

    collided = jnp.moveaxis(lax.map(collide_slab, moved), 0, 1)
    read_rows = []
    for stream_dir in range(19):
        step_x, step_y, step_z = lattice_dirs[stream_dir]
        pulled = jnp.roll(collided[stream_dir], (step_x, step_y), axis=(0, 1))
        mirror = collided[opposite_list[stream_dir]]
        if step_z == 1:
            pulled = jnp.concatenate([mirror[:, :, :1], pulled[:, :, :-1]], axis=2)
        elif step_z == -1:
            pulled = jnp.concatenate([pulled[:, :, 1:], mirror[:, :, -1:]], axis=2)
        read_rows.append(pulled)
    read = jnp.stack(read_rows)

    velocity, weight = lattice_tables()
    block_x = lax.broadcasted_iota(jnp.int32, link_cell.shape, 0)
    block_y = lax.broadcasted_iota(jnp.int32, link_cell.shape, 1)
    coord_x = block_x * CX + link_cell // (CY * CZ)
    coord_y = block_y * CY + (link_cell // CZ) % CY
    coord_z = link_cell % CZ
    outgoing = collided[link_dir, coord_x, coord_y, coord_z]
    incoming = read[opposite(link_dir), coord_x, coord_y, coord_z]
    push = velocity[:, link_dir] * (outgoing + incoming)[None]
    targets = global_grain(link_grain, block_x, block_y).reshape(-1)
    force_rows = []
    for component in range(3):
        force_rows.append(jax.ops.segment_sum(push[component].reshape(-1), targets, num_segments=GRAINS))
    force_flat = jnp.stack(force_rows)
    grain_force = force_flat.reshape(3, N_GX, N_GY, GRAIN_DEV).transpose(1, 2, 0, 3)

    speed_flat = grain_state[:, :, 0:3].transpose(2, 0, 1, 3).reshape(3, GRAINS)
    inverse_mass = grain_state[:, :, 3].reshape(GRAINS)
    free_flat = speed_flat + inverse_mass[None] * force_flat

    cblock_x = lax.broadcasted_iota(jnp.int32, contact_self.shape, 0)
    cblock_y = lax.broadcasted_iota(jnp.int32, contact_self.shape, 1)
    live = (contact_self < GRAIN_DEV).reshape(-1)
    own_slot = jnp.minimum(contact_self, GRAIN_DEV - 1)
    grain_a = ((cblock_x * N_GY + cblock_y) * GRAIN_DEV + own_slot).reshape(-1)
    grain_b = global_grain(contact_peer, cblock_x, cblock_y).reshape(-1)
    normals = contact_normal.transpose(2, 0, 1, 3).reshape(3, -1)
    gaps = contact_gap.reshape(-1)
    both = jnp.concatenate([grain_a, grain_b])
    impulse = jnp.zeros(gaps.shape, jnp.float32)
    current = free_flat
    for sweep_idx in range(SWEEPS):
        closing = jnp.sum(normals * (current[:, grain_b] - current[:, grain_a]), axis=0) + gaps
        denom = inverse_mass[grain_a] + inverse_mass[grain_b]
        impulse = jnp.where(live, jnp.maximum(0.0, impulse - under_relax * closing / denom), 0.0)
        kicks = jnp.concatenate([-impulse[None] * normals, impulse[None] * normals], axis=1)
        total_rows = []
        for component in range(3):
            total_rows.append(jax.ops.segment_sum(kicks[component], both, num_segments=GRAINS))
        current = free_flat + inverse_mass[None] * jnp.stack(total_rows)
    grain_velocity = current.reshape(3, N_GX, N_GY, GRAIN_DEV).transpose(1, 2, 0, 3)
    contact_impulse = impulse.reshape(contact_self.shape)
    return read, grain_force, grain_velocity, contact_impulse
```

```python
import jax
import jax.numpy as jnp
from jax import lax
from jax.experimental import pallas as pl
from jax.experimental.pallas import tpu as pltpu
from jax.sharding import PartitionSpec as P

SWEEPS = 4
DIRS = [
    [0, 0, 0],
    [1, 0, 0],
    [-1, 0, 0],
    [0, 1, 0],
    [0, -1, 0],
    [0, 0, 1],
    [0, 0, -1],
    [1, 1, 0],
    [-1, -1, 0],
    [1, -1, 0],
    [-1, 1, 0],
    [1, 0, 1],
    [-1, 0, -1],
    [1, 0, -1],
    [-1, 0, 1],
    [0, 1, 1],
    [0, -1, -1],
    [0, 1, -1],
    [0, -1, 1],
]
OPP = [0, 2, 1, 4, 3, 6, 5, 8, 7, 10, 9, 12, 11, 14, 13, 16, 15, 18, 17]
WEIGHT = [1.0 / 3.0] + [1.0 / 18.0] * 6 + [1.0 / 36.0] * 12
XP = [1, 7, 9, 11, 13]
XM = [2, 8, 10, 12, 14]
YP = [3, 7, 10, 15, 17]
YM = [4, 8, 9, 16, 18]
LOW = 32
highest = lax.Precision.HIGHEST
f32 = jnp.float32
bf16 = jnp.bfloat16
VMEM = pltpu.VMEM


def whole(shape):
    return pl.BlockSpec(shape, lambda *_: (0,) * len(shape))


def lanes_of(shape):
    return lax.broadcasted_iota(jnp.int32, shape, len(shape) - 1)


def split3(v):
    hi = v.astype(bf16)
    rest = v - hi.astype(f32)
    mid = rest.astype(bf16)
    low = (rest - mid.astype(f32)).astype(bf16)
    return hi, mid, low


def collide_kernel(
    relax_ref, pop_ref, centre_ref, table_ref, yhi_ref, ylo_ref, xhi_ref, xlo_ref, rs, pad
):
    step = pl.program_id(0)
    steps = pl.num_programs(0)
    block_x = pop_ref.shape[1]
    size_y = pop_ref.shape[2]
    size_x = pad.shape[1] - 2

    @pl.when(step == 0)
    def _():
        for j in range(19):
            rs[j] = jnp.broadcast_to(relax_ref[:, j : j + 1], (19, 128))
        zero = jnp.zeros((size_x + 2, 8, 128), f32)
        for q in YP + YM:
            pad[q, :, 0:8] = zero
            pad[q, :, 8 + size_y :] = zero
        for q in XP + XM:
            pad[q, 0] = jnp.zeros(pad.shape[2:], f32)
            pad[q, size_x + 1] = jnp.zeros(pad.shape[2:], f32)

    def one_row(x, carry):
        f = [pop_ref[q, x] for q in range(19)]
        rho = f[0]
        for q in range(1, 19):
            rho = rho + f[q]
        speeds = []
        inverse = 1.0 / rho
        for axis in range(3):
            total = None
            for q in range(1, 19, 2):
                sign = DIRS[q][axis]
                if sign:
                    diff = f[q] - f[q + 1] if sign > 0 else f[q + 1] - f[q]
                    total = diff if total is None else total + diff
            speeds.append(total * inverse)
        ux, uy, uz = speeds
        base = 1.0 - 1.5 * (ux * ux + uy * uy + uz * uz)
        neq = [f[0] - WEIGHT[0] * rho * base]
        for q in range(1, 19, 2):
            along = None
            for axis in range(3):
                sign = DIRS[q][axis]
                if sign:
                    if along is None:
                        along = speeds[axis]
                    else:
                        along = along + speeds[axis] if sign > 0 else along - speeds[axis]
            scale = WEIGHT[q] * rho
            even = scale * (base + 4.5 * (along * along))
            odd = scale * (3.0 * along)
            neq.append(f[q] - (even + odd))
            neq.append(f[q + 1] - (even - odd))
        for q in range(19):
            parts = [None, None]
            for j in range(19):
                term = rs[j, q : q + 1, :] * neq[j]
                parts[j % 2] = term if parts[j % 2] is None else parts[j % 2] + term
            out = f[q] - (parts[0] + parts[1])
            centre_ref[q, x] = out
            pad[q, 1 + step * block_x + x, 8 : 8 + size_y] = out
        return carry

    lax.fori_loop(0, block_x, one_row, 0)

    @pl.when(step == steps - 1)
    def _():
        for k in range(5):
            yhi_ref[k * size_x : (k + 1) * size_x] = pad[YP[k], 1 : 1 + size_x, 7 + size_y, :]
            ylo_ref[k * size_x : (k + 1) * size_x] = pad[YM[k], 1 : 1 + size_x, 8, :]
            xhi_ref[k * size_y : (k + 1) * size_y] = pad[XP[k], size_x, 8 : 8 + size_y, :]
            xlo_ref[k * size_y : (k + 1) * size_y] = pad[XM[k], 1, 8 : 8 + size_y, :]
        lane = lanes_of((size_y, 128))

        def pack(xh, carry):
            for d in range(1, 19):
                q = OPP[d]
                dx, dy, dz = DIRS[d]
                for half in range(2):
                    acc = None
                    for k in range(4):
                        x = xh * 8 + half * 4 + k
                        own = pad[d, 1 + x, 8 : 8 + size_y, :]
                        other = pad[q, 1 + x + dx, 8 + dy : 8 + dy + size_y, :]
                        if dz:
                            other = pltpu.roll(other, (-dz) % 128, 1)
                        if dz == -1:
                            other = jnp.where(lane == 0, own, other)
                        pair = own + other
                        if k:
                            pair = jnp.where(lane >= LOW * k, pltpu.roll(pair, LOW * k, 1), acc)
                        acc = pair
                    start = pl.multiple_of((d - 1) * 2 * size_y + xh * size_y, size_y)
                    hi = acc.astype(bf16)
                    lo = (acc - hi.astype(f32)).astype(bf16)
                    table_ref[pl.ds(start, size_y), 128 * half : 128 * half + 128] = hi
                    table_ref[pl.ds(start, size_y), 256 + 128 * half : 384 + 128 * half] = lo
            return carry

        lax.fori_loop(0, size_x // 8, pack, 0)


def collide(populations, relax_matrix):
    _, size_x, size_y, size_z = populations.shape
    block_x = 4
    face = jax.ShapeDtypeStruct((5 * size_y, size_z), f32)
    table_rows = 18 * (size_x // 8) * size_y
    return pl.pallas_call(
        collide_kernel,
        grid=(size_x // block_x,),
        in_specs=[
            whole((19, 19)),
            pl.BlockSpec((19, block_x, size_y, size_z), lambda i: (0, i, 0, 0)),
        ],
        out_specs=[
            pl.BlockSpec((19, block_x, size_y, size_z), lambda i: (0, i, 0, 0)),
            whole((table_rows, 512)),
        ]
        + [whole(face.shape)] * 4,
        out_shape=[
            jax.ShapeDtypeStruct(populations.shape, f32),
            jax.ShapeDtypeStruct((table_rows, 512), bf16),
        ]
        + [face] * 4,
        scratch_shapes=[
            VMEM((19, 19, 128), f32),
            VMEM((19, size_x + 2, size_y + 16, size_z), f32),
        ],
        compiler_params=pltpu.CompilerParams(vmem_limit_bytes=40 << 20),
        cost_estimate=pl.CostEstimate(flops=40_000_000, bytes_accessed=6_000_000, transcendentals=0),
        name="collide",
    )(relax_matrix, populations)


CHUNK = 512


def pick(table_ref, rows, column, entry, chunk):
    depth = table_ref.shape[1] // 2
    hot = (lax.broadcasted_iota(jnp.int32, (depth, chunk), 0) == column).astype(f32).astype(bf16)
    hot = jnp.concatenate([hot, hot], axis=0)
    offset = entry - lax.broadcasted_iota(jnp.int32, (8, chunk), 0)
    acc = jnp.zeros((8, chunk), f32)
    tile = min(rows, 192)
    for begin in range(0, rows, tile):
        found = jnp.dot(table_ref[begin : begin + tile, :], hot, preferred_element_type=f32)
        for j in range(0, tile, 8):
            acc = jnp.where(offset == begin + j, found[j : j + 8], acc)
    return jnp.sum(acc, axis=0, keepdims=True)


def link_kernel(table_ref, cell_ref, dir_ref, value_ref):
    rows = table_ref.shape[0]

    def one_chunk(i, carry):
        cell = cell_ref[pl.ds(i, 1), :]
        direction = dir_ref[pl.ds(i, 1), :]
        x = cell >> 11
        y = (cell >> 7) & 15
        z = cell & 31
        column = (x & 7) * 32 + z
        entry = (direction - 1) * 32 + (x >> 3) * 16 + y
        value_ref[pl.ds(i, 1), :] = pick(table_ref, rows, column, entry, CHUNK)
        return carry

    lax.fori_loop(0, cell_ref.shape[0], one_chunk, 0, unroll=4)


def interior_links(table, cells, dirs):
    links = cells.size
    shape = (links // CHUNK, CHUNK)
    return pl.pallas_call(
        link_kernel,
        in_specs=[whole(table.shape), whole(shape), whole(shape)],
        out_specs=whole(shape),
        grid=(1,),
        out_shape=jax.ShapeDtypeStruct(shape, f32),
        compiler_params=pltpu.CompilerParams(vmem_limit_bytes=40 << 20),
        cost_estimate=pl.CostEstimate(
            flops=10_000_000_000, bytes_accessed=1_000_000, transcendentals=0
        ),
        name="interior_links",
    )(table, cells.reshape(shape), dirs.reshape(shape))


def member(direction, dirs):
    out = jnp.zeros(direction.shape, jnp.int32)
    for k, d in enumerate(dirs):
        out = jnp.where(direction == d, k + 1, out)
    return out


def scatter_kernel(
    value_ref, cell_ref, dir_ref, grain_ref, xlow_ref, xhigh_ref, ylow_ref, yhigh_ref, out_ref, table
):
    size = 16
    lane = lanes_of((size, 128))
    for side in range(2):
        for j in range(10):
            d = (XP + XM)[j] if side == 0 else (YP + YM)[j]
            q = OPP[d]
            dx, dy, dz = DIRS[d]
            along = dy if side == 0 else dx
            if side == 0:
                ref = xhigh_ref if j < 5 else xlow_ref
                k = (XM if j < 5 else XP).index(q)
                if along == 0:
                    face = ref[k * size : (k + 1) * size]
                elif along == 1:
                    face = jnp.concatenate(
                        [ref[k * size + 1 : (k + 1) * size], ref[5 * size + 1 : 5 * size + 2]], axis=0
                    )
                else:
                    face = jnp.concatenate(
                        [ref[5 * size : 5 * size + 1], ref[k * size : (k + 1) * size - 1]], axis=0
                    )
            else:
                ref = yhigh_ref if j < 5 else ylow_ref
                k = (YM if j < 5 else YP).index(q)
                blank = jnp.zeros((1, 128), f32)
                if along == 0:
                    face = ref[k * size : (k + 1) * size]
                elif along == 1:
                    face = jnp.concatenate([ref[k * size + 1 : (k + 1) * size], blank], axis=0)
                else:
                    face = jnp.concatenate([blank, ref[k * size : (k + 1) * size - 1]], axis=0)
            if dz:
                face = pltpu.roll(face, (-dz) % 128, 1)
            if dz == -1:
                face = jnp.where(lane == 0, 0.0, face)
            spot = (j % 8) * LOW
            shift = spot % 128
            if shift:
                face = pltpu.roll(face, shift, 1)
            row = 16 * (2 * side + j // 8)
            half = spot // 128 * 128
            keep = (lane >= shift) & (lane < shift + LOW)
            face = jnp.where(keep, face, 0.0)
            hi = face.astype(bf16)
            lo = (face - hi.astype(f32)).astype(bf16)
            rows = slice(row, row + 16)
            for piece, part in ((0, hi), (1, lo)):
                cols = slice(256 * piece + half, 256 * piece + half + 128)
                if shift:
                    table[rows, cols] = table[rows, cols] + part
                else:
                    table[rows, cols] = part
        for piece in range(2):
            table[16 * (2 * side + 1) : 16 * (2 * side + 2), 256 * piece + 128 : 256 * piece + 256] = (
                jnp.zeros((16, 128), bf16)
            )

    def one_chunk(i, acc):
        cell = cell_ref[pl.ds(i, 1), :]
        direction = dir_ref[pl.ds(i, 1), :]
        grain = grain_ref[pl.ds(i, 1), :]
        x = cell >> 11
        y = (cell >> 7) & 15
        z = cell & 31
        xup, xdown = member(direction, XP), member(direction, XM)
        yup, ydown = member(direction, YP), member(direction, YM)
        jx = jnp.where(
            (x == 15) & (xup > 0), xup, jnp.where((x == 0) & (xdown > 0), xdown + 5, 0)
        )
        jy = jnp.where(
            (y == 15) & (yup > 0), yup, jnp.where((y == 0) & (ydown > 0), ydown + 5, 0)
        )
        which = jnp.where(jx > 0, jx, jy) - 1
        column = (which & 7) * 32 + z
        entry = jnp.where(jx > 0, y, jnp.where(jy > 0, 32 + x, -64)) + (which >> 3) * 16
        value = value_ref[pl.ds(i, 1), :] + pick(table, 64, column, entry, CHUNK)
        sign_x = jnp.where(xup > 0, 1.0, 0.0) - jnp.where(xdown > 0, 1.0, 0.0)
        sign_y = jnp.where(yup > 0, 1.0, 0.0) - jnp.where(ydown > 0, 1.0, 0.0)
        zup = (direction == 5) | (direction == 11) | (direction == 14) | (direction == 15) | (direction == 18)
        zdown = (direction == 6) | (direction == 12) | (direction == 13) | (direction == 16) | (direction == 17)
        sign_z = jnp.where(zup, 1.0, 0.0) - jnp.where(zdown, 1.0, 0.0)
        frame = grain >> 7
        slot = grain & 127
        frame_hit = lax.broadcasted_iota(jnp.int32, (16, CHUNK), 0) == frame
        terms = []
        for part in split3(value):
            for sign in (sign_x, sign_y, sign_z):
                scaled = part.astype(f32) * sign
                terms.append(jnp.where(frame_hit, scaled, 0.0).astype(bf16))
        terms = jnp.concatenate(terms, axis=0)
        hot = (lax.broadcasted_iota(jnp.int32, (128, CHUNK), 0) == slot).astype(f32).astype(bf16)
        return acc + lax.dot_general(
            terms, hot, (((1,), (1,)), ((), ())), preferred_element_type=f32
        )

    acc = lax.fori_loop(0, cell_ref.shape[0], one_chunk, jnp.zeros((144, 128), f32))
    total = acc[0:48] + (acc[48:96] + acc[96:144])
    out_ref[...] = jnp.concatenate(
        [total[0:9], total[16:25], total[32:41], jnp.zeros((5, 128), f32)], axis=0
    )


def link_sums(values, cells, dirs, grains, xlow, xhigh, ylow, yhigh):
    shape = values.shape
    args = (
        values,
        cells.reshape(shape),
        dirs.reshape(shape),
        grains.reshape(shape),
        xlow,
        xhigh,
        ylow,
        yhigh,
    )
    return pl.pallas_call(
        scatter_kernel,
        grid=(1,),
        in_specs=[whole(a.shape) for a in args],
        out_specs=whole((32, 128)),
        out_shape=jax.ShapeDtypeStruct((32, 128), f32),
        scratch_shapes=[VMEM((64, 512), bf16)],
        compiler_params=pltpu.CompilerParams(vmem_limit_bytes=40 << 20),
        cost_estimate=pl.CostEstimate(
            flops=2_000_000_000, bytes_accessed=500_000, transcendentals=0
        ),
        name="link_sums",
    )(*args)


def stream_kernel(centre_ref, xlow_ref, xhigh_ref, ylow_ref, yhigh_ref, out_ref, pad):
    step = pl.program_id(0)
    block_x = out_ref.shape[1]
    size_x, size_y = centre_ref.shape[1], centre_ref.shape[2]

    @pl.when(step == 0)
    def _():
        for q in range(19):
            pad[q, 1 : 1 + size_x, 8 : 8 + size_y] = centre_ref[q]
        for k in range(5):
            pad[YP[k], 1 : 1 + size_x, 7, :] = ylow_ref[k * size_x : (k + 1) * size_x]
            pad[YM[k], 1 : 1 + size_x, 8 + size_y, :] = yhigh_ref[k * size_x : (k + 1) * size_x]
            pad[XP[k], 0, 8 : 8 + size_y, :] = xlow_ref[k * size_y : (k + 1) * size_y]
            pad[XM[k], 1 + size_x, 8 : 8 + size_y, :] = xhigh_ref[k * size_y : (k + 1) * size_y]
        base = 5 * size_y
        for q, row in ((7, 7), (9, 8 + size_y)):
            pad[q, 0, row : row + 1, :] = xlow_ref[base + (row > 8) : base + (row > 8) + 1]
        for q, row in ((10, 7), (8, 8 + size_y)):
            pad[q, 1 + size_x, row : row + 1, :] = xhigh_ref[base + (row > 8) : base + (row > 8) + 1]

    lane = lanes_of((size_y, 128))

    def one_row(i, carry):
        x = step * block_x + i
        for q in range(19):
            dx, dy, dz = DIRS[q]
            moved = pad[q, 1 + x - dx, 8 - dy : 8 - dy + size_y, :]
            if dz:
                moved = pltpu.roll(moved, dz % 128, 1)
                wall = 0 if dz == 1 else 127
                moved = jnp.where(lane == wall, pad[OPP[q], 1 + x, 8 : 8 + size_y, :], moved)
            out_ref[q, i] = moved
        return carry

    lax.fori_loop(0, block_x, one_row, 0)


def passed(centre, xlow, xhigh, ylow, yhigh):
    _, size_x, size_y, size_z = centre.shape
    block_x = 4
    return pl.pallas_call(
        stream_kernel,
        grid=(size_x // block_x,),
        in_specs=[whole(a.shape) for a in (centre, xlow, xhigh, ylow, yhigh)],
        out_specs=pl.BlockSpec((19, block_x, size_y, size_z), lambda i: (0, i, 0, 0)),
        out_shape=jax.ShapeDtypeStruct(centre.shape, f32),
        scratch_shapes=[VMEM((19, size_x + 2, size_y + 16, size_z), f32)],
        compiler_params=pltpu.CompilerParams(vmem_limit_bytes=40 << 20),
        cost_estimate=pl.CostEstimate(flops=10_000_000, bytes_accessed=6_000_000, transcendentals=0),
        name="passed",
    )(centre, xlow, xhigh, ylow, yhigh)


def across(v, by):
    return pltpu.roll(v, by % 8, 0) if by % 8 else v


def look_up(table, index):
    return jnp.take_along_axis(table, index, axis=1)


def fold(sums_ref, stride):
    out = []
    for dxi in range(3):
        for c in range(3):
            total = None
            for dyi in range(3):
                row = sums_ref[:, c * stride + 3 * dxi + dyi, :]
                row = across(row, dyi - 1)
                total = row if total is None else total + row
            out.append(total)
    return out


def column_index(contact, t):
    own = contact(0, t).astype(jnp.int32)
    peer = contact(1, t).astype(jnp.int32)
    return own, peer & 127, peer >> 7


def peer_tables(read):
    tables = {}
    for dxi in range(3):
        base = read(dxi - 1)
        for dyi in range(3):
            tables[3 * dxi + dyi] = across(base, 1 - dyi)
    return tables


def pick_peer(tables, slot, frame):
    found = jnp.zeros(slot.shape, f32)
    for k in range(9):
        found = jnp.where(frame == k, look_up(tables[k], slot), found)
    return found


def one_column(contact, vel, denom, impulse, store_impulse, sums_ref):
    shape = (8, 128)
    indices = [column_index(contact, t) for t in range(4)]
    closing = [contact(5, t) for t in range(4)]
    for c in range(3):
        tables = peer_tables(lambda j: vel(j, c))
        for t in range(4):
            own, slot, frame = indices[t]
            gap = pick_peer(tables, slot, frame) - look_up(vel(0, c), jnp.minimum(own, 127))
            closing[t] = closing[t] + contact(2 + c, t) * gap
    kicks = []
    for t in range(4):
        new = jnp.maximum(0.0, impulse(t) - 0.5 * closing[t] / denom(t))
        new = jnp.where(indices[t][0] < 128, new, 0.0)
        store_impulse(t, new)
        kicks.append([split3(new * contact(2 + c, t)) for c in range(3)])
    slots_of = lax.broadcasted_iota(jnp.int32, (128, 512), 0)
    frames_of = lax.broadcasted_iota(jnp.int32, (16, 512), 0)

    def line(parts, y):
        return jnp.concatenate([p[y : y + 1, :] for p in parts], axis=1)

    for y in range(8):
        slot = line([indices[t][1] for t in range(4)], y)
        frame = line([indices[t][2] for t in range(4)], y)
        own = line([indices[t][0] for t in range(4)], y)
        hot_peer = (slots_of == slot).astype(f32).astype(bf16)
        hot_own = (slots_of == own).astype(f32).astype(bf16)
        hit = frames_of == frame
        rows = [
            line([kicks[t][c][piece].astype(f32) for t in range(4)], y)
            for piece in range(3)
            for c in range(3)
        ]
        terms = jnp.concatenate([jnp.where(hit, r, 0.0).astype(bf16) for r in rows], axis=0)
        nt = (((1,), (1,)), ((), ()))
        found = lax.dot_general(terms, hot_peer, nt, preferred_element_type=f32)
        mine = jnp.concatenate(rows + [jnp.zeros((7, 512), f32)], axis=0).astype(bf16)
        mine = lax.dot_general(mine, hot_own, nt, preferred_element_type=f32)
        found = found[0:48] + (found[48:96] + found[96:144])
        mine = mine[0:3] + (mine[3:6] + mine[6:9])
        sums_ref[y, 0:48] = found
        for c in range(3):
            sums_ref[y, 16 * c + 9 : 16 * c + 10] = mine[c : c + 1]


def column_kicks(sums_ref):
    out = fold(sums_ref, 16)
    for c in range(3):
        out[3 + c] = out[3 + c] - sums_ref[:, 16 * c + 9, :]
    return out


def fold_kernel(frames_ref, out_ref):
    for k, row in enumerate(fold(frames_ref, 9)):
        out_ref[k] = row


def prep_kernel(own_ref, low1_ref, high1_ref, low3_ref, high3_ref, contact_ref, grain_ref, denom_ref):
    contact_ref[0] = low3_ref[0:24]
    contact_ref[1] = low1_ref[0:24]
    contact_ref[2] = own_ref[0:24]
    contact_ref[3] = high1_ref[0:24]
    contact_ref[4] = high3_ref[0:24]
    grain_ref[0] = low3_ref[28:32]
    grain_ref[1] = low3_ref[24:28]
    grain_ref[2] = low1_ref[24:28]
    grain_ref[3] = own_ref[24:28]
    grain_ref[4] = high1_ref[24:28]
    grain_ref[5] = high3_ref[24:28]
    grain_ref[6] = high3_ref[28:32]

    def column(j, carry):
        contact = lambda f, t: contact_ref[j, 4 * f + t]
        mass = lambda k: grain_ref[j + 1 + k, 3]
        tables = peer_tables(mass)
        for t in range(4):
            own, slot, frame = column_index(contact, t)
            denom_ref[j, t] = pick_peer(tables, slot, frame) + look_up(
                mass(0), jnp.minimum(own, 127)
            )
        return carry

    lax.fori_loop(0, 5, column, 0)


def two_sweeps(contact_ref, grain_ref, denom_ref, base_ref, vel_ref, impulse_ref, sums_ref, kick_ref):
    def sweep(j):
        one_column(
            lambda f, t: contact_ref[j, 4 * f + t],
            lambda k, c: vel_ref[j + 1 + k, c],
            lambda t: denom_ref[j, t],
            lambda t: impulse_ref[j, t],
            lambda t, v: impulse_ref.__setitem__((j, t), v),
            sums_ref,
        )
        for k, row in enumerate(column_kicks(sums_ref)):
            kick_ref[j, k] = row

    def column(j, carry):
        sweep(j)
        return carry

    lax.fori_loop(0, 5, column, 0)
    for j in range(1, 4):
        for c in range(3):
            total = kick_ref[j, 3 + c] + (kick_ref[j - 1, 6 + c] + kick_ref[j + 1, c])
            vel_ref[j + 1, c] = base_ref[j + 1, c] + grain_ref[j + 1, 3] * total
    lax.fori_loop(2, 3, column, 0)


def gather_totals(own_ref, low1_ref, high1_ref, low3_ref, high3_ref, store):
    def rows(j, dxi, c):
        k = 3 * dxi + c
        if j == 0:
            return own_ref[k]
        if abs(j) == 1:
            return (high1_ref if j > 0 else low1_ref)[k]
        ref = high3_ref if j > 0 else low3_ref
        if abs(j) == 2:
            return ref[k]
        if abs(j) == 3:
            return ref[9 + k]
        return ref[18 + c]

    for j in range(-3, 4):
        for c in range(3):
            store(j + 3, c, rows(j, 1, c) + (rows(j - 1, 2, c) + rows(j + 1, 0, c)))


def row_of(v, y):
    hit = lax.broadcasted_iota(jnp.int32, (8, 128), 0) == y
    return jnp.sum(jnp.where(hit, v, 0.0), axis=0, keepdims=True)


def first_kernel(
    place_ref, own_ref, low1_ref, high1_ref, low3_ref, high3_ref, contact_ref, grain_ref, denom_ref,
    force_ref, free_ref, send_ref, vel, impulse, sums, kick,
):
    y = place_ref[0]

    def store(j, c, total):
        if j == 3:
            force_ref[c : c + 1] = row_of(total, y)
        free_ref[j, c] = grain_ref[j, c] + grain_ref[j, 3] * total
        vel[j, c] = free_ref[j, c]

    gather_totals(own_ref, low1_ref, high1_ref, low3_ref, high3_ref, store)
    impulse[...] = jnp.zeros(impulse.shape, f32)
    two_sweeps(contact_ref, grain_ref, denom_ref, free_ref, vel, impulse, sums, kick)
    send_ref[0:9] = kick[2]
    send_ref[9:13] = impulse[2]


def second_kernel(
    place_ref, own_ref, low1_ref, high1_ref, low3_ref, high3_ref, contact_ref, grain_ref, denom_ref,
    free_ref, kicks_ref, impulse_ref, base_ref, vel, impulse, sums, kick,
):
    y = place_ref[0]

    def store(j, c, total):
        vel[j, c] = free_ref[j, c] + grain_ref[j, 3] * total

    gather_totals(own_ref, low1_ref, high1_ref, low3_ref, high3_ref, store)
    impulse[0] = low3_ref[21:25]
    impulse[1] = low1_ref[9:13]
    impulse[2] = own_ref[9:13]
    impulse[3] = high1_ref[9:13]
    impulse[4] = high3_ref[21:25]
    two_sweeps(contact_ref, grain_ref, denom_ref, free_ref, vel, impulse, sums, kick)
    for k in range(9):
        kicks_ref[k : k + 1] = row_of(kick[2, k], y)
    for t in range(4):
        impulse_ref[t : t + 1] = row_of(impulse[2, t], y)
    for c in range(3):
        base_ref[c : c + 1] = row_of(free_ref[3, c], y)
    base_ref[3:4] = row_of(grain_ref[3, 3], y)


def vmem_call(kernel, outs, args, scratch=(), flops=1_000_000, place=None):
    specs = [pl.BlockSpec(memory_space=VMEM) for _ in args]
    if place is not None:
        args = (place,) + tuple(args)
        specs = [pl.BlockSpec(memory_space=pltpu.SMEM)] + specs
    return pl.pallas_call(
        kernel,
        in_specs=specs,
        out_specs=[pl.BlockSpec(memory_space=VMEM) for _ in outs],
        out_shape=[jax.ShapeDtypeStruct(s, f32) for s in outs],
        scratch_shapes=list(scratch),
        compiler_params=pltpu.CompilerParams(vmem_limit_bytes=24 << 20),
        cost_estimate=pl.CostEstimate(flops=flops, bytes_accessed=500_000, transcendentals=0),
        name=kernel.__name__,
    )(*args)


def shift(value, axis, by):
    size = lax.axis_size(axis)
    return lax.ppermute(value, axis, [(i, (i + by) % size) for i in range(size)])


def both_ways(to_low, to_high, axis, by):
    return shift(to_high, axis, by), shift(to_low, axis, -by)


def whole_column(rows):
    size = lax.axis_size("gy")
    spread = jnp.broadcast_to(rows[None], (size,) + rows.shape)
    return lax.all_to_all(spread, "gy", 0, 0)


def per_device(
    populations,
    relax_matrix,
    grain_state,
    link_cell,
    link_dir,
    link_grain,
    contact_self,
    contact_peer,
    contact_normal,
    contact_gap,
):
    size_y = populations.shape[2]
    place = lax.axis_index("gy").astype(jnp.int32).reshape(1)

    static = jnp.concatenate(
        [
            contact_self.reshape(4, 128).astype(f32),
            contact_peer.reshape(4, 128).astype(f32),
            contact_normal.reshape(12, 128),
            contact_gap.reshape(4, 128),
            grain_state.reshape(4, 128),
        ],
        axis=0,
    )
    static0 = whole_column(static).transpose(1, 0, 2)

    centre, table, yhi, ylo, xhi, xlo = collide(populations, relax_matrix)
    ylow, yhigh = both_ways(ylo, yhi, "gy", 1)
    corner = lambda lists, k, x: lists[k * size_y + x : k * size_y + x + 1]
    last = populations.shape[1] - 1
    blank = jnp.zeros((6, 128), f32)
    to_high = jnp.concatenate([xhi, corner(ylow, 1, last), corner(yhigh, 2, last), blank], axis=0)
    to_low = jnp.concatenate([xlo, corner(ylow, 2, 0), corner(yhigh, 1, 0), blank], axis=0)
    xlow, xhigh = both_ways(to_low, to_high, "gx", 1)
    static_low, static_high = both_ways(static0, static0, "gx", 1)
    static_low3, static_high3 = both_ways(
        jnp.concatenate([static_low, static0[24:28]], axis=0),
        jnp.concatenate([static_high, static0[24:28]], axis=0),
        "gx",
        3,
    )
    contacts, grains, denom = vmem_call(
        prep_kernel,
        [(5, 24, 8, 128), (7, 4, 8, 128), (5, 4, 8, 128)],
        (static0, static_low, static_high, static_low3, static_high3),
    )

    values = interior_links(table, link_cell, link_dir)
    frames = link_sums(values, link_cell, link_dir, link_grain, xlow, xhigh, ylow, yhigh)
    populations_next = passed(centre, xlow, xhigh, ylow, yhigh)

    (force0,) = vmem_call(fold_kernel, [(9, 8, 128)], (whole_column(frames),))
    force_low, force_high = both_ways(force0, force0, "gx", 1)
    force_low3, force_high3 = both_ways(
        jnp.concatenate([force_low, force0, force_high[0:3]], axis=0),
        jnp.concatenate([force_high, force0, force_low[6:9]], axis=0),
        "gx",
        3,
    )
    scratch = [
        VMEM((7, 3, 8, 128), f32),
        VMEM((5, 4, 8, 128), f32),
        VMEM((8, 48, 128), f32),
        VMEM((5, 9, 8, 128), f32),
    ]
    force, free, sent0 = vmem_call(
        first_kernel,
        [(3, 128), (7, 3, 8, 128), (13, 8, 128)],
        (force0, force_low, force_high, force_low3, force_high3, contacts, grains, denom),
        scratch,
        place=place,
    )

    sent_low, sent_high = both_ways(sent0, sent0, "gx", 1)
    sent_low3, sent_high3 = both_ways(
        jnp.concatenate([sent_low[0:9], sent0[0:9], sent_high[0:3], sent_low[9:13]], axis=0),
        jnp.concatenate([sent_high[0:9], sent0[0:9], sent_low[6:9], sent_high[9:13]], axis=0),
        "gx",
        3,
    )
    kicks, impulse, base = vmem_call(
        second_kernel,
        [(9, 128), (4, 128), (4, 128)],
        (sent0, sent_low, sent_high, sent_low3, sent_high3, contacts, grains, denom, free),
        scratch,
        place=place,
    )
    from_low, from_high = both_ways(kicks[0:3], kicks[6:9], "gx", 1)
    velocity = base[0:3] + base[3:4] * (kicks[3:6] + (from_low + from_high))
    return (
        populations_next,
        force[None, None],
        velocity[None, None],
        impulse.reshape(contact_self.shape),
    )


def solution(mesh):
    placed = (
        P(None, "gx", "gy", None),
        P(),
        P("gx", "gy", None, None),
        P("gx", "gy", None),
        P("gx", "gy", None),
        P("gx", "gy", None),
        P("gx", "gy", None),
        P("gx", "gy", None),
        P("gx", "gy", None, None),
        P("gx", "gy", None),
    )
    return jax.shard_map(
        per_device,
        mesh=mesh,
        in_specs=placed,
        out_specs=(
            P(None, "gx", "gy", None),
            P("gx", "gy", None, None),
            P("gx", "gy", None, None),
            P("gx", "gy", None),
        ),
        check_vma=False,
    )
```

```python
import jax
import jax.numpy as jnp
from jax import lax
from jax.experimental import pallas as pl
from jax.experimental.pallas import tpu as pltpu
from jax.sharding import PartitionSpec as P

SWEEPS = 4
DIRS = [
    [0, 0, 0],
    [1, 0, 0],
    [-1, 0, 0],
    [0, 1, 0],
    [0, -1, 0],
    [0, 0, 1],
    [0, 0, -1],
    [1, 1, 0],
    [-1, -1, 0],
    [1, -1, 0],
    [-1, 1, 0],
    [1, 0, 1],
    [-1, 0, -1],
    [1, 0, -1],
    [-1, 0, 1],
    [0, 1, 1],
    [0, -1, -1],
    [0, 1, -1],
    [0, -1, 1],
]
OPP = [0, 2, 1, 4, 3, 6, 5, 8, 7, 10, 9, 12, 11, 14, 13, 16, 15, 18, 17]
WEIGHT = [1.0 / 3.0] + [1.0 / 18.0] * 6 + [1.0 / 36.0] * 12
XP = [1, 7, 9, 11, 13]
XM = [2, 8, 10, 12, 14]
YP = [3, 7, 10, 15, 17]
YM = [4, 8, 9, 16, 18]
CANON = [1, 3, 5, 7, 9, 11, 14, 15, 18]
WALL = [6, 12, 13, 16, 17]
LOW = 32
highest = lax.Precision.HIGHEST
f32 = jnp.float32
bf16 = jnp.bfloat16
VMEM = pltpu.VMEM


def whole(shape):
    return pl.BlockSpec(shape, lambda *_: (0,) * len(shape))


def lanes_of(shape):
    return lax.broadcasted_iota(jnp.int32, shape, len(shape) - 1)


def split3(v):
    hi = v.astype(bf16)
    rest = v - hi.astype(f32)
    mid = rest.astype(bf16)
    low = (rest - mid.astype(f32)).astype(bf16)
    return hi, mid, low


def collide_kernel(
    relax_ref, pop_ref, centre_ref, table_ref, yhi_ref, ylo_ref, xhi_ref, xlo_ref, rs, pad
):
    step = pl.program_id(0)
    steps = pl.num_programs(0)
    block_x = pop_ref.shape[1]
    size_y = pop_ref.shape[2]
    size_x = pad.shape[1] - 2

    @pl.when(step == 0)
    def _():
        for j in range(19):
            column = jnp.broadcast_to(relax_ref[:, j : j + 1], (19, 128))
            for q in range(19):
                rs[j, q] = jnp.broadcast_to(column[q : q + 1], (8, 128))
        zero = jnp.zeros((size_x + 2, 8, 128), f32)
        for q in YP + YM:
            pad[q, :, 0:8] = zero
            pad[q, :, 8 + size_y :] = zero
        for q in XP + XM:
            pad[q, 0] = jnp.zeros(pad.shape[2:], f32)
            pad[q, size_x + 1] = jnp.zeros(pad.shape[2:], f32)

    def one_row(x, carry):
        f = [pop_ref[q, x] for q in range(19)]
        rho = f[0]
        for q in range(1, 19):
            rho = rho + f[q]
        speeds = []
        inverse = 1.0 / rho
        for axis in range(3):
            total = None
            for q in range(1, 19, 2):
                sign = DIRS[q][axis]
                if sign:
                    diff = f[q] - f[q + 1] if sign > 0 else f[q + 1] - f[q]
                    total = diff if total is None else total + diff
            speeds.append(total * inverse)
        ux, uy, uz = speeds
        base = 1.0 - 1.5 * (ux * ux + uy * uy + uz * uz)
        neq = [f[0] - WEIGHT[0] * rho * base]
        for q in range(1, 19, 2):
            along = None
            for axis in range(3):
                sign = DIRS[q][axis]
                if sign:
                    if along is None:
                        along = speeds[axis]
                    else:
                        along = along + speeds[axis] if sign > 0 else along - speeds[axis]
            scale = WEIGHT[q] * rho
            even = scale * (base + 4.5 * (along * along))
            odd = scale * (3.0 * along)
            neq.append(f[q] - (even + odd))
            neq.append(f[q + 1] - (even - odd))
        for q in range(19):
            parts = [None, None]
            for j in range(19):
                term = (neq[j].reshape(2, 8, 128) * rs[j, q][None]).reshape(16, 128)
                parts[j % 2] = term if parts[j % 2] is None else parts[j % 2] + term
            out = f[q] - (parts[0] + parts[1])
            centre_ref[q, x] = out
            pad[q, 1 + step * block_x + x, 8 : 8 + size_y] = out
        return carry

    lax.fori_loop(0, block_x, one_row, 0)

    @pl.when(step == steps - 1)
    def _():
        for k in range(5):
            yhi_ref[k * size_x : (k + 1) * size_x] = pad[YP[k], 1 : 1 + size_x, 7 + size_y, :]
            ylo_ref[k * size_x : (k + 1) * size_x] = pad[YM[k], 1 : 1 + size_x, 8, :]
            xhi_ref[k * size_y : (k + 1) * size_y] = pad[XP[k], size_x, 8 : 8 + size_y, :]
            xlo_ref[k * size_y : (k + 1) * size_y] = pad[XM[k], 1, 8 : 8 + size_y, :]
        lane = lanes_of((size_y, 128))

        def put(row, half, value):
            hi = value.astype(bf16)
            lo = (value - hi.astype(f32)).astype(bf16)
            rows = pl.ds(pl.multiple_of(row, size_y), size_y)
            table_ref[rows, 128 * half : 128 * half + 128] = hi
            table_ref[rows, 256 + 128 * half : 384 + 128 * half] = lo

        def pack(xh, carry):
            for half in range(2):
                for i, d in enumerate(CANON):
                    q = OPP[d]
                    dx, dy, dz = DIRS[d]
                    acc = None
                    for k in range(4):
                        x = xh * 8 + half * 4 + k
                        other = pad[q, 1 + x + dx, 8 + dy : 8 + dy + size_y, :]
                        if dz:
                            other = pltpu.roll(other, 127, 1)
                        pair = pad[d, 1 + x, 8 : 8 + size_y, :] + other
                        if k:
                            pair = jnp.where(lane >= LOW * k, pltpu.roll(pair, LOW * k, 1), acc)
                        acc = pair
                    put(i * 2 * size_y + xh * size_y, half, acc)
                acc = jnp.zeros((size_y, 128), f32)
                for k in range(4):
                    x = xh * 8 + half * 4 + k
                    for i, d in enumerate(WALL):
                        own = 2.0 * pad[d, 1 + x, 8 : 8 + size_y, :]
                        spot = LOW * k + i
                        if spot:
                            own = pltpu.roll(own, spot, 1)
                        acc = jnp.where(lane == spot, own, acc)
                put(len(CANON) * 2 * size_y + xh * size_y, half, acc)
            return carry

        lax.fori_loop(0, size_x // 8, pack, 0)


def collide(populations, relax_matrix):
    _, size_x, size_y, size_z = populations.shape
    block_x = 4
    face = jax.ShapeDtypeStruct((5 * size_y, size_z), f32)
    table_rows = 10 * (size_x // 8) * size_y
    return pl.pallas_call(
        collide_kernel,
        grid=(size_x // block_x,),
        in_specs=[
            whole((19, 19)),
            pl.BlockSpec((19, block_x, size_y, size_z), lambda i: (0, i, 0, 0)),
        ],
        out_specs=[
            pl.BlockSpec((19, block_x, size_y, size_z), lambda i: (0, i, 0, 0)),
            whole((table_rows, 512)),
        ]
        + [whole(face.shape)] * 4,
        out_shape=[
            jax.ShapeDtypeStruct(populations.shape, f32),
            jax.ShapeDtypeStruct((table_rows, 512), bf16),
        ]
        + [face] * 4,
        scratch_shapes=[
            VMEM((19, 19, 8, 128), f32),
            VMEM((19, size_x + 2, size_y + 16, size_z), f32),
        ],
        compiler_params=pltpu.CompilerParams(vmem_limit_bytes=60 << 20),
        cost_estimate=pl.CostEstimate(flops=40_000_000, bytes_accessed=6_000_000, transcendentals=0),
        name="collide",
    )(relax_matrix, populations)


CHUNK = 512


def pick(table_ref, column, entry):
    rows, depth = table_ref.shape[0], table_ref.shape[1] // 2
    chunk = column.shape[1]
    hot = (lax.broadcasted_iota(jnp.int32, (depth, chunk), 0) == column).astype(f32).astype(bf16)
    hot = jnp.concatenate([hot, hot], axis=0)
    offset = entry - lax.broadcasted_iota(jnp.int32, (8, chunk), 0)
    acc = jnp.zeros((8, chunk), f32)
    found = jnp.dot(table_ref[...], hot, preferred_element_type=f32)
    for j in range(0, rows, 8):
        acc = jnp.where(offset == j, found[j : j + 8], acc)
    return jnp.sum(acc, axis=0, keepdims=True)


def member(direction, dirs, first=1, step=1):
    out = jnp.zeros(direction.shape, jnp.int32)
    for k, d in enumerate(dirs):
        out = jnp.where(direction == d, first + step * k, out)
    return out


def sides(direction):
    return (
        member(direction, XP),
        member(direction, XM),
        member(direction, YP),
        member(direction, YM),
    )


def tile_of(ref, k):
    start = pl.multiple_of(k * 1024, 1024)
    return jnp.concatenate(
        [ref[0, :, pl.ds(start + 128 * s, 128)] for s in range(8)], axis=0
    )


def line_of(ref, i):
    return jnp.concatenate([ref[pl.ds(4 * i + k, 1), :] for k in range(4)], axis=1)


def link_kernel(table_ref, cell_ref, dir_ref, value_ref, column, entry):
    def index(k, carry):
        cell, direction = tile_of(cell_ref, k), tile_of(dir_ref, k)
        xup, xdown, yup, ydown = sides(direction)
        forward = member(direction, CANON)
        backward = member(direction, [OPP[d] for d in CANON])
        wall = member(direction, WALL)
        back = (backward > 0).astype(jnp.int32)
        x = (cell >> 11) + back * ((xup > 0).astype(jnp.int32) - (xdown > 0).astype(jnp.int32))
        y = ((cell >> 7) & 15) + back * (
            (yup > 0).astype(jnp.int32) - (ydown > 0).astype(jnp.int32)
        )
        z = cell & 31
        bottom = (wall > 0) & (z == 0)
        z = z - (wall > 0).astype(jnp.int32)
        which = forward + backward - 1
        inside = (x >= 0) & (x < 16) & (y >= 0) & (y < 16) & (which >= 0)
        place = which * 32 + (x >> 3) * 16 + y
        base = cell >> 11
        under = 288 + (base >> 3) * 16 + ((cell >> 7) & 15)
        rows = pl.ds(pl.multiple_of(k * 8, 8), 8)
        column[rows, :] = jnp.where(bottom, (base & 7) * 32 + wall - 1, (x & 7) * 32 + (z & 31))
        entry[rows, :] = jnp.where(bottom, under, jnp.where(inside, place, -8))
        return carry

    lax.fori_loop(0, 16, index, 0)

    def one_chunk(i, carry):
        found = pick(table_ref, line_of(column, i), line_of(entry, i))
        for k in range(4):
            value_ref[pl.ds(4 * i + k, 1), :] = found[:, 128 * k : 128 * k + 128]
        return carry

    lax.fori_loop(0, 32, one_chunk, 0, unroll=8)


def interior_links(table, cells, dirs):
    shape = (128, 128)
    return pl.pallas_call(
        link_kernel,
        in_specs=[pl.BlockSpec(memory_space=VMEM)] * 3,
        out_specs=pl.BlockSpec(memory_space=VMEM),
        out_shape=jax.ShapeDtypeStruct(shape, f32),
        scratch_shapes=[VMEM(shape, jnp.int32)] * 2,
        compiler_params=pltpu.CompilerParams(vmem_limit_bytes=24 << 20),
        cost_estimate=pl.CostEstimate(
            flops=6_000_000_000, bytes_accessed=1_000_000, transcendentals=0
        ),
        name="interior_links",
    )(table, cells, dirs)


def scatter_kernel(
    value_ref, cell_ref, dir_ref, grain_ref,
    xlow_ref, xhigh_ref, ylow_ref, yhigh_ref,
    ownx_low_ref, ownx_high_ref, owny_low_ref, owny_high_ref,
    self_ref, peer_ref, normal_ref, gap_ref, state_ref,
    out_ref,
    table, column, entry, frames, slots, signs,
):
    size = 16
    lane = lanes_of((size, 128))
    for side in range(2):
        for group in range(3):
            acc = jnp.zeros((size, 128), f32)
            for j in range(4 * group, min(4 * group + 4, 10)):
                d = (XP + XM)[j] if side == 0 else (YP + YM)[j]
                q = OPP[d]
                dx, dy, dz = DIRS[d]
                high = j < 5
                if side == 0:
                    along = dy
                    ref = xhigh_ref if high else xlow_ref
                    mine = ownx_high_ref if high else ownx_low_ref
                    k = (XM if high else XP).index(q)
                    ends = ref[5 * size : 5 * size + 1], ref[5 * size + 1 : 5 * size + 2]
                else:
                    along = dx
                    ref = yhigh_ref if high else ylow_ref
                    mine = owny_high_ref if high else owny_low_ref
                    k = (YM if high else YP).index(q)
                    ends = (jnp.zeros((1, 128), f32),) * 2
                face = ref[k * size : (k + 1) * size]
                if along == 1:
                    face = jnp.concatenate([face[1:], ends[1]], axis=0)
                elif along == -1:
                    face = jnp.concatenate([ends[0], face[:-1]], axis=0)
                if dz:
                    face = pltpu.roll(face, (-dz) % 128, 1)
                if d not in CANON:
                    face = face + mine[(j % 5) * size : (j % 5 + 1) * size]
                if dz == -1:
                    face = jnp.where(lane == 0, 0.0, face)
                shift = (j % 4) * LOW
                if shift:
                    face = pltpu.roll(face, shift, 1)
                acc = jnp.where((lane >= shift) & (lane < shift + LOW), face, acc)
            hi = acc.astype(bf16)
            lo = (acc - hi.astype(f32)).astype(bf16)
            row = 16 * (3 * side + group)
            table[row : row + 16, 0:128] = hi
            table[row : row + 16, 128:256] = lo

    def index(k, carry):
        cell, direction, grain = tile_of(cell_ref, k), tile_of(dir_ref, k), tile_of(grain_ref, k)
        xup, xdown, yup, ydown = sides(direction)
        zup = member(direction, [5, 11, 14, 15, 18], 1, 0)
        zdown = member(direction, WALL, 1, 0)
        x, y, z = cell >> 11, (cell >> 7) & 15, cell & 31
        jx = jnp.where(
            (x == 15) & (xup > 0), xup, jnp.where((x == 0) & (xdown > 0), xdown + 5, 0)
        )
        jy = jnp.where(
            (y == 15) & (yup > 0), yup, jnp.where((y == 0) & (ydown > 0), ydown + 5, 0)
        )
        which = jnp.where(jx > 0, jx, jy) - 1
        rows = pl.ds(pl.multiple_of(k * 8, 8), 8)
        column[rows, :] = (which & 3) * 32 + z
        place = (which >> 2) * 16 + jnp.where(jx > 0, y, 48 + x)
        entry[rows, :] = jnp.where(which >= 0, place, -8)
        frames[rows, :] = grain >> 7
        slots[rows, :] = grain & 127
        for c, (up, down) in enumerate(((xup, xdown), (yup, ydown), (zup, zdown))):
            signs[c, rows, :] = (up > 0).astype(f32) - (down > 0).astype(f32)
        return carry

    lax.fori_loop(0, 16, index, 0)
    frames_of = lax.broadcasted_iota(jnp.int32, (16, CHUNK), 0)
    slots_of = lax.broadcasted_iota(jnp.int32, (128, CHUNK), 0)

    def one_chunk(i, acc):
        value = line_of(value_ref, i) + pick(table, line_of(column, i), line_of(entry, i))
        hit = frames_of == line_of(frames, i)
        sign = [line_of(signs.at[c], i) for c in range(3)]
        terms = []
        for part in split3(value):
            part = part.astype(f32)
            for c in range(3):
                terms.append(jnp.where(hit, part * sign[c], 0.0).astype(bf16))
        hot = (slots_of == line_of(slots, i)).astype(f32).astype(bf16)
        return acc + lax.dot_general(
            jnp.concatenate(terms, axis=0), hot, (((1,), (1,)), ((), ())), preferred_element_type=f32
        )

    acc = lax.fori_loop(0, 32, one_chunk, jnp.zeros((144, 128), f32), unroll=8)
    total = acc[0:48] + (acc[48:96] + acc[96:144])
    rows = [total[0:9], total[16:25], total[32:41], jnp.zeros((5, 128), f32)]
    for ref in (self_ref, peer_ref):
        rows += [ref[0, :, 128 * t : 128 * t + 128].astype(f32) for t in range(4)]
    for c in range(3):
        rows += [normal_ref[0, c, :, 128 * t : 128 * t + 128] for t in range(4)]
    rows += [gap_ref[0, :, 128 * t : 128 * t + 128] for t in range(4)]
    rows += [state_ref[0, 0], jnp.zeros((4, 128), f32)]
    message = jnp.concatenate(rows, axis=0)
    for k in range(8):
        out_ref[k] = message


def link_sums(values, links, halos, faces, contacts):
    args = (values,) + links + halos + faces + contacts
    square = (128, 128)
    return pl.pallas_call(
        scatter_kernel,
        in_specs=[pl.BlockSpec(memory_space=VMEM)] * len(args),
        out_specs=pl.BlockSpec(memory_space=VMEM),
        out_shape=jax.ShapeDtypeStruct((8, 64, 128), f32),
        scratch_shapes=[VMEM((96, 256), bf16)]
        + [VMEM(square, jnp.int32)] * 4
        + [VMEM((3,) + square, f32)],
        compiler_params=pltpu.CompilerParams(vmem_limit_bytes=24 << 20),
        cost_estimate=pl.CostEstimate(
            flops=2_000_000_000, bytes_accessed=500_000, transcendentals=0
        ),
        name="link_sums",
    )(*args)


def stream_kernel(centre_ref, xlow_ref, xhigh_ref, ylow_ref, yhigh_ref, out_ref, pad):
    step = pl.program_id(0)
    block_x = out_ref.shape[1]
    size_x, size_y = centre_ref.shape[1], centre_ref.shape[2]

    @pl.when(step == 0)
    def _():
        for q in range(19):
            pad[q, 1 : 1 + size_x, 8 : 8 + size_y] = centre_ref[q]
        for k in range(5):
            pad[YP[k], 1 : 1 + size_x, 7, :] = ylow_ref[k * size_x : (k + 1) * size_x]
            pad[YM[k], 1 : 1 + size_x, 8 + size_y, :] = yhigh_ref[k * size_x : (k + 1) * size_x]
            pad[XP[k], 0, 8 : 8 + size_y, :] = xlow_ref[k * size_y : (k + 1) * size_y]
            pad[XM[k], 1 + size_x, 8 : 8 + size_y, :] = xhigh_ref[k * size_y : (k + 1) * size_y]
        base = 5 * size_y
        for q, row in ((7, 7), (9, 8 + size_y)):
            pad[q, 0, row : row + 1, :] = xlow_ref[base + (row > 8) : base + (row > 8) + 1]
        for q, row in ((10, 7), (8, 8 + size_y)):
            pad[q, 1 + size_x, row : row + 1, :] = xhigh_ref[base + (row > 8) : base + (row > 8) + 1]

    lane = lanes_of((size_y, 128))

    def one_row(i, carry):
        x = step * block_x + i
        for q in range(19):
            dx, dy, dz = DIRS[q]
            moved = pad[q, 1 + x - dx, 8 - dy : 8 - dy + size_y, :]
            if dz:
                moved = pltpu.roll(moved, dz % 128, 1)
                wall = 0 if dz == 1 else 127
                moved = jnp.where(lane == wall, pad[OPP[q], 1 + x, 8 : 8 + size_y, :], moved)
            out_ref[q, i] = moved
        return carry

    lax.fori_loop(0, block_x, one_row, 0)


def passed(centre, xlow, xhigh, ylow, yhigh):
    _, size_x, size_y, size_z = centre.shape
    block_x = 4
    return pl.pallas_call(
        stream_kernel,
        grid=(size_x // block_x,),
        in_specs=[whole(a.shape) for a in (centre, xlow, xhigh, ylow, yhigh)],
        out_specs=pl.BlockSpec((19, block_x, size_y, size_z), lambda i: (0, i, 0, 0)),
        out_shape=jax.ShapeDtypeStruct(centre.shape, f32),
        scratch_shapes=[VMEM((19, size_x + 2, size_y + 16, size_z), f32)],
        compiler_params=pltpu.CompilerParams(vmem_limit_bytes=40 << 20),
        cost_estimate=pl.CostEstimate(flops=10_000_000, bytes_accessed=6_000_000, transcendentals=0),
        name="passed",
    )(centre, xlow, xhigh, ylow, yhigh)


def across(v, by):
    return pltpu.roll(v, by % 8, 0) if by % 8 else v


def look_up(table, index):
    return jnp.take_along_axis(table, index, axis=1)


def fold(sums_ref, stride):
    out = []
    for dxi in range(3):
        for c in range(3):
            total = None
            for dyi in range(3):
                row = sums_ref[:, c * stride + 3 * dxi + dyi, :]
                row = across(row, dyi - 1)
                total = row if total is None else total + row
            out.append(total)
    return out


def column_index(contact, t):
    own = contact(0, t).astype(jnp.int32)
    peer = contact(1, t).astype(jnp.int32)
    return own, peer & 127, peer >> 7


def peer_tables(read):
    tables = {}
    for dxi in range(3):
        base = read(dxi - 1)
        for dyi in range(3):
            tables[3 * dxi + dyi] = across(base, 1 - dyi)
    return tables


def pick_peer(tables, slot, frame):
    found = jnp.zeros(slot.shape, f32)
    for k in range(9):
        found = jnp.where(frame == k, look_up(tables[k], slot), found)
    return found


def one_column(contact, vel, denom, impulse, store_impulse, sums_ref):
    shape = (8, 128)
    indices = [column_index(contact, t) for t in range(4)]
    closing = [contact(5, t) for t in range(4)]
    for c in range(3):
        tables = peer_tables(lambda j: vel(j, c))
        for t in range(4):
            own, slot, frame = indices[t]
            gap = pick_peer(tables, slot, frame) - look_up(vel(0, c), jnp.minimum(own, 127))
            closing[t] = closing[t] + contact(2 + c, t) * gap
    kicks = []
    for t in range(4):
        new = jnp.maximum(0.0, impulse(t) - 0.5 * closing[t] / denom(t))
        new = jnp.where(indices[t][0] < 128, new, 0.0)
        store_impulse(t, new)
        kicks.append([split3(new * contact(2 + c, t)) for c in range(3)])
    slots_of = lax.broadcasted_iota(jnp.int32, (128, 512), 0)
    frames_of = lax.broadcasted_iota(jnp.int32, (16, 512), 0)

    def line(parts, y):
        return jnp.concatenate([p[y : y + 1, :] for p in parts], axis=1)

    for y in range(8):
        slot = line([indices[t][1] for t in range(4)], y)
        frame = line([indices[t][2] for t in range(4)], y)
        own = line([indices[t][0] for t in range(4)], y)
        hot_peer = (slots_of == slot).astype(f32).astype(bf16)
        hot_own = (slots_of == own).astype(f32).astype(bf16)
        hit = frames_of == frame
        rows = [
            line([kicks[t][c][piece].astype(f32) for t in range(4)], y)
            for piece in range(3)
            for c in range(3)
        ]
        terms = jnp.concatenate([jnp.where(hit, r, 0.0).astype(bf16) for r in rows], axis=0)
        nt = (((1,), (1,)), ((), ()))
        found = lax.dot_general(terms, hot_peer, nt, preferred_element_type=f32)
        mine = jnp.concatenate(rows + [jnp.zeros((7, 512), f32)], axis=0).astype(bf16)
        mine = lax.dot_general(mine, hot_own, nt, preferred_element_type=f32)
        found = found[0:48] + (found[48:96] + found[96:144])
        mine = mine[0:3] + (mine[3:6] + mine[6:9])
        sums_ref[y, 0:48] = found
        for c in range(3):
            sums_ref[y, 16 * c + 9 : 16 * c + 10] = mine[c : c + 1]


def column_kicks(sums_ref):
    out = fold(sums_ref, 16)
    for c in range(3):
        out[3 + c] = out[3 + c] - sums_ref[:, 16 * c + 9, :]
    return out


def fold_kernel(frames_ref, out_ref):
    for k, row in enumerate(fold(frames_ref, 9)):
        out_ref[k] = row
    for r in range(28):
        out_ref[9 + r] = frames_ref[:, 32 + r, :]


def far_kernel(own_ref, low_ref, high_ref, to_low_ref, to_high_ref):
    for out_ref, near_ref, behind_ref, rows in (
        (to_low_ref, low_ref, high_ref, slice(0, 3)),
        (to_high_ref, high_ref, low_ref, slice(6, 9)),
    ):
        out_ref[0:9] = near_ref[0:9]
        out_ref[9:18] = own_ref[0:9]
        out_ref[18:21] = behind_ref[rows]
        if out_ref.shape[0] == 25:
            out_ref[21:25] = near_ref[9:13]
        else:
            out_ref[21:49] = near_ref[9:37]
            out_ref[49:53] = own_ref[33:37]


def prep(own_ref, low1_ref, high1_ref, low3_ref, high3_ref, contact_ref, grain_ref, denom_ref):
    contact_ref[0] = low3_ref[21:45]
    contact_ref[1] = low1_ref[9:33]
    contact_ref[2] = own_ref[9:33]
    contact_ref[3] = high1_ref[9:33]
    contact_ref[4] = high3_ref[21:45]
    grain_ref[0] = low3_ref[49:53]
    grain_ref[1] = low3_ref[45:49]
    grain_ref[2] = low1_ref[33:37]
    grain_ref[3] = own_ref[33:37]
    grain_ref[4] = high1_ref[33:37]
    grain_ref[5] = high3_ref[45:49]
    grain_ref[6] = high3_ref[49:53]

    def column(j, carry):
        contact = lambda f, t: contact_ref[j, 4 * f + t]
        mass = lambda k: grain_ref[j + 1 + k, 3]
        tables = peer_tables(mass)
        for t in range(4):
            own, slot, frame = column_index(contact, t)
            denom_ref[j, t] = pick_peer(tables, slot, frame) + look_up(
                mass(0), jnp.minimum(own, 127)
            )
        return carry

    lax.fori_loop(0, 5, column, 0)


def two_sweeps(contact_ref, grain_ref, denom_ref, base_ref, vel_ref, impulse_ref, sums_ref, kick_ref):
    def sweep(j):
        one_column(
            lambda f, t: contact_ref[j, 4 * f + t],
            lambda k, c: vel_ref[j + 1 + k, c],
            lambda t: denom_ref[j, t],
            lambda t: impulse_ref[j, t],
            lambda t, v: impulse_ref.__setitem__((j, t), v),
            sums_ref,
        )
        for k, row in enumerate(column_kicks(sums_ref)):
            kick_ref[j, k] = row

    def column(j, carry):
        sweep(j)
        return carry

    lax.fori_loop(0, 5, column, 0)
    for j in range(1, 4):
        for c in range(3):
            total = kick_ref[j, 3 + c] + (kick_ref[j - 1, 6 + c] + kick_ref[j + 1, c])
            vel_ref[j + 1, c] = base_ref[j + 1, c] + grain_ref[j + 1, 3] * total
    lax.fori_loop(2, 3, column, 0)


def gather_totals(own_ref, low1_ref, high1_ref, low3_ref, high3_ref, store):
    def rows(j, dxi, c):
        k = 3 * dxi + c
        if j == 0:
            return own_ref[k]
        if abs(j) == 1:
            return (high1_ref if j > 0 else low1_ref)[k]
        ref = high3_ref if j > 0 else low3_ref
        if abs(j) == 2:
            return ref[k]
        if abs(j) == 3:
            return ref[9 + k]
        return ref[18 + c]

    for j in range(-3, 4):
        for c in range(3):
            store(j + 3, c, rows(j, 1, c) + (rows(j - 1, 2, c) + rows(j + 1, 0, c)))


def row_of(v, y):
    hit = lax.broadcasted_iota(jnp.int32, (8, 128), 0) == y
    return jnp.sum(jnp.where(hit, v, 0.0), axis=0, keepdims=True)


def first_kernel(
    place_ref, own_ref, low1_ref, high1_ref, low3_ref, high3_ref,
    force_ref, free_ref, send_ref, contact_ref, grain_ref, denom_ref, vel, impulse, sums, kick,
):
    y = place_ref[0]
    prep(own_ref, low1_ref, high1_ref, low3_ref, high3_ref, contact_ref, grain_ref, denom_ref)

    def store(j, c, total):
        if j == 3:
            force_ref[0, c] = row_of(total, y)
        free_ref[j, c] = grain_ref[j, c] + grain_ref[j, 3] * total
        vel[j, c] = free_ref[j, c]

    gather_totals(own_ref, low1_ref, high1_ref, low3_ref, high3_ref, store)
    impulse[...] = jnp.zeros(impulse.shape, f32)
    two_sweeps(contact_ref, grain_ref, denom_ref, free_ref, vel, impulse, sums, kick)
    send_ref[0:9] = kick[2]
    send_ref[9:13] = impulse[2]


def second_kernel(
    place_ref, own_ref, low1_ref, high1_ref, low3_ref, high3_ref, contact_ref, grain_ref, denom_ref,
    free_ref, kicks_ref, impulse_ref, base_ref, vel, impulse, sums, kick,
):
    y = place_ref[0]

    def store(j, c, total):
        vel[j, c] = free_ref[j, c] + grain_ref[j, 3] * total

    gather_totals(own_ref, low1_ref, high1_ref, low3_ref, high3_ref, store)
    impulse[0] = low3_ref[21:25]
    impulse[1] = low1_ref[9:13]
    impulse[2] = own_ref[9:13]
    impulse[3] = high1_ref[9:13]
    impulse[4] = high3_ref[21:25]
    two_sweeps(contact_ref, grain_ref, denom_ref, free_ref, vel, impulse, sums, kick)
    for k in range(9):
        kicks_ref[k : k + 1] = row_of(kick[2, k], y)
    for t in range(4):
        impulse_ref[0, :, 128 * t : 128 * t + 128] = row_of(impulse[2, t], y)
    for c in range(3):
        base_ref[c : c + 1] = row_of(free_ref[3, c], y)
    base_ref[3:4] = row_of(grain_ref[3, 3], y)


def final_kernel(base_ref, kicks_ref, low_ref, high_ref, out_ref):
    total = kicks_ref[3:6] + (low_ref[...] + high_ref[...])
    speed = base_ref[0:3] + base_ref[3:4] * total
    for c in range(3):
        out_ref[0, c] = speed[c : c + 1]


def edge_kernel(xhi_ref, xlo_ref, ylow_ref, yhigh_ref, to_low_ref, to_high_ref):
    size = 16
    last = size - 1
    for out_ref, face_ref, first, second in (
        (to_high_ref, xhi_ref, size + last, 2 * size + last),
        (to_low_ref, xlo_ref, 2 * size, size),
    ):
        out_ref[0:80] = face_ref[...]
        corners = [ylow_ref[first : first + 1], yhigh_ref[second : second + 1]]
        out_ref[80:88] = jnp.concatenate(corners + [jnp.zeros((6, 128), f32)], axis=0)


def vmem_call(kernel, outs, args, scratch=(), flops=1_000_000, place=None):
    specs = [pl.BlockSpec(memory_space=VMEM) for _ in args]
    if place is not None:
        args = (place,) + tuple(args)
        specs = [pl.BlockSpec(memory_space=pltpu.SMEM)] + specs
    return pl.pallas_call(
        kernel,
        in_specs=specs,
        out_specs=[pl.BlockSpec(memory_space=VMEM) for _ in outs],
        out_shape=[jax.ShapeDtypeStruct(s, f32) for s in outs],
        scratch_shapes=list(scratch),
        compiler_params=pltpu.CompilerParams(vmem_limit_bytes=24 << 20),
        cost_estimate=pl.CostEstimate(flops=flops, bytes_accessed=500_000, transcendentals=0),
        name=kernel.__name__,
    )(*args)


def shift(value, axis, by):
    size = lax.axis_size(axis)
    return lax.ppermute(value, axis, [(i, (i + by) % size) for i in range(size)])


def both_ways(to_low, to_high, axis, by):
    return shift(to_high, axis, by), shift(to_low, axis, -by)


def per_device(
    populations,
    relax_matrix,
    grain_state,
    link_cell,
    link_dir,
    link_grain,
    contact_self,
    contact_peer,
    contact_normal,
    contact_gap,
):
    place = lax.axis_index("gy").astype(jnp.int32).reshape(1)
    links = (link_cell, link_dir, link_grain)
    contacts = (
        contact_self,
        contact_peer,
        contact_normal.transpose(0, 2, 1, 3),
        contact_gap,
        grain_state,
    )

    centre, table, yhi, ylo, xhi, xlo = collide(populations, relax_matrix)
    ylow, yhigh = both_ways(ylo, yhi, "gy", 1)
    to_low, to_high = vmem_call(edge_kernel, [(88, 128)] * 2, (xhi, xlo, ylow, yhigh))
    xlow, xhigh = both_ways(to_low, to_high, "gx", 1)
    values = interior_links(table, link_cell, link_dir)
    halos = (xlow, xhigh, ylow, yhigh)
    spread = link_sums(values, links, halos, (xlo, xhi, ylo, yhi), contacts)
    populations_next = passed(centre, *halos)

    own = lax.all_to_all(spread, "gy", 0, 0)
    (own,) = vmem_call(fold_kernel, [(37, 8, 128)], (own,))
    low, high = both_ways(own, own, "gx", 1)
    far = vmem_call(far_kernel, [(53, 8, 128)] * 2, (own, low, high))
    low3, high3 = both_ways(*far, "gx", 3)
    scratch = [
        VMEM((7, 3, 8, 128), f32),
        VMEM((5, 4, 8, 128), f32),
        VMEM((8, 48, 128), f32),
        VMEM((5, 9, 8, 128), f32),
    ]
    force, free, own, *static = vmem_call(
        first_kernel,
        [
            (1, 3, 1, 128),
            (7, 3, 8, 128),
            (13, 8, 128),
            (5, 24, 8, 128),
            (7, 4, 8, 128),
            (5, 4, 8, 128),
        ],
        (own, low, high, low3, high3),
        scratch,
        place=place,
    )

    low, high = both_ways(own, own, "gx", 1)
    far = vmem_call(far_kernel, [(25, 8, 128)] * 2, (own, low, high))
    low3, high3 = both_ways(*far, "gx", 3)
    kicks, impulse, base = vmem_call(
        second_kernel,
        [(9, 128), (1, 1, 512), (4, 128)],
        (own, low, high, low3, high3, *static, free),
        scratch,
        place=place,
    )
    from_low, from_high = both_ways(kicks[0:3], kicks[6:9], "gx", 1)
    (velocity,) = vmem_call(final_kernel, [(1, 3, 1, 128)], (base, kicks, from_low, from_high))
    return (
        populations_next,
        force.transpose(0, 2, 1, 3),
        velocity.transpose(0, 2, 1, 3),
        impulse,
    )


def solution(mesh):
    placed = (
        P(None, "gx", "gy", None),
        P(),
        P("gx", "gy", None, None),
        P("gx", "gy", None),
        P("gx", "gy", None),
        P("gx", "gy", None),
        P("gx", "gy", None),
        P("gx", "gy", None),
        P("gx", "gy", None, None),
        P("gx", "gy", None),
    )
    return jax.shard_map(
        per_device,
        mesh=mesh,
        in_specs=placed,
        out_specs=(
            P(None, "gx", "gy", None),
            P("gx", "gy", None, None),
            P("gx", "gy", None, None),
            P("gx", "gy", None),
        ),
        check_vma=False,
    )
```

```python
import functools

import jax
import jax.numpy as jnp
from jax import lax
from jax.experimental import pallas as pl
from jax.experimental.pallas import tpu as pltpu
from jax.sharding import PartitionSpec as P

SWEEPS = 4
DIRS = [
    [0, 0, 0],
    [1, 0, 0],
    [-1, 0, 0],
    [0, 1, 0],
    [0, -1, 0],
    [0, 0, 1],
    [0, 0, -1],
    [1, 1, 0],
    [-1, -1, 0],
    [1, -1, 0],
    [-1, 1, 0],
    [1, 0, 1],
    [-1, 0, -1],
    [1, 0, -1],
    [-1, 0, 1],
    [0, 1, 1],
    [0, -1, -1],
    [0, 1, -1],
    [0, -1, 1],
]
OPP = [0, 2, 1, 4, 3, 6, 5, 8, 7, 10, 9, 12, 11, 14, 13, 16, 15, 18, 17]
WEIGHT = [1.0 / 3.0] + [1.0 / 18.0] * 6 + [1.0 / 36.0] * 12
XP = [1, 7, 9, 11, 13]
XM = [2, 8, 10, 12, 14]
YP = [3, 7, 10, 15, 17]
YM = [4, 8, 9, 16, 18]
CANON = [1, 3, 5, 7, 9, 11, 14, 15, 18]
WALL = [6, 12, 13, 16, 17]
LOW = 32
highest = lax.Precision.HIGHEST
f32 = jnp.float32
bf16 = jnp.bfloat16
VMEM = pltpu.VMEM


def whole(shape):
    return pl.BlockSpec(shape, lambda *_: (0,) * len(shape))


def lanes_of(shape):
    return lax.broadcasted_iota(jnp.int32, shape, len(shape) - 1)


def split3(v):
    hi = v.astype(bf16)
    rest = v - hi.astype(f32)
    mid = rest.astype(bf16)
    low = (rest - mid.astype(f32)).astype(bf16)
    return hi, mid, low


PIECES = 4


def collide_kernel(
    relax_hbm, pop_hbm, centre_hbm, table_ref, yhi_ref, ylo_ref, xhi_ref, xlo_ref,
    relax, rs, pop, pad, in_sem, out_sem,
):
    size_x, size_y = pop.shape[1], pop.shape[2]
    piece_x = size_x // PIECES

    def arriving(i):
        part = pl.ds(i * piece_x, piece_x)
        return pltpu.make_async_copy(pop_hbm.at[:, part], pop.at[:, part], in_sem.at[i])

    def leaving(i):
        part = pl.ds(i * piece_x, piece_x)
        inner = pl.ds(1 + i * piece_x, piece_x)
        return pltpu.make_async_copy(
            pad.at[:, inner, 8 : 8 + size_y], centre_hbm.at[:, part], out_sem.at[i]
        )

    matrix = pltpu.make_async_copy(relax_hbm, relax, in_sem.at[PIECES])
    matrix.start()
    for i in range(PIECES):
        arriving(i).start()
    zero = jnp.zeros((size_x + 2, 8, 128), f32)
    for q in YP + YM:
        pad[q, :, 0:8] = zero
        pad[q, :, 8 + size_y :] = zero
    for q in XP + XM:
        pad[q, 0] = jnp.zeros(pad.shape[2:], f32)
        pad[q, size_x + 1] = jnp.zeros(pad.shape[2:], f32)
    matrix.wait()
    for j in range(19):
        column = jnp.broadcast_to(relax[:, j : j + 1], (19, 128))
        for q in range(19):
            rs[j, q] = jnp.broadcast_to(column[q : q + 1], (8, 128))

    def one_row(x, carry):
        f = [pop[q, x] for q in range(19)]
        rho = f[0]
        for q in range(1, 19):
            rho = rho + f[q]
        speeds = []
        inverse = 1.0 / rho
        for axis in range(3):
            total = None
            for q in range(1, 19, 2):
                sign = DIRS[q][axis]
                if sign:
                    diff = f[q] - f[q + 1] if sign > 0 else f[q + 1] - f[q]
                    total = diff if total is None else total + diff
            speeds.append(total * inverse)
        ux, uy, uz = speeds
        base = 1.0 - 1.5 * (ux * ux + uy * uy + uz * uz)
        neq = [f[0] - WEIGHT[0] * rho * base]
        for q in range(1, 19, 2):
            along = None
            for axis in range(3):
                sign = DIRS[q][axis]
                if sign:
                    if along is None:
                        along = speeds[axis]
                    else:
                        along = along + speeds[axis] if sign > 0 else along - speeds[axis]
            scale = WEIGHT[q] * rho
            even = scale * (base + 4.5 * (along * along))
            odd = scale * (3.0 * along)
            neq.append(f[q] - (even + odd))
            neq.append(f[q + 1] - (even - odd))
        for q in range(19):
            parts = [None, None]
            for j in range(19):
                term = (neq[j].reshape(2, 8, 128) * rs[j, q][None]).reshape(16, 128)
                parts[j % 2] = term if parts[j % 2] is None else parts[j % 2] + term
            out = f[q] - (parts[0] + parts[1])
            pad[q, 1 + x, 8 : 8 + size_y] = out
        return carry

    def one_piece(i, carry):
        arriving(i).wait()
        lax.fori_loop(i * piece_x, (i + 1) * piece_x, one_row, 0)
        leaving(i).start()
        return carry

    lax.fori_loop(0, PIECES, one_piece, 0)
    for k in range(5):
        yhi_ref[k * size_x : (k + 1) * size_x] = pad[YP[k], 1 : 1 + size_x, 7 + size_y, :]
        ylo_ref[k * size_x : (k + 1) * size_x] = pad[YM[k], 1 : 1 + size_x, 8, :]
        xhi_ref[k * size_y : (k + 1) * size_y] = pad[XP[k], size_x, 8 : 8 + size_y, :]
        xlo_ref[k * size_y : (k + 1) * size_y] = pad[XM[k], 1, 8 : 8 + size_y, :]

    cells = size_x * size_y
    nt = (((1,), (1,)), ((), ()))

    def put(row, count, terms, chooser):
        hi = terms.astype(bf16)
        lo = (terms - hi.astype(f32)).astype(bf16)
        pair = lax.dot_general(chooser, hi, nt, preferred_element_type=f32)
        pair = pair + lax.dot_general(chooser, lo, nt, preferred_element_type=f32)
        hi = pair.astype(bf16)
        table_ref[row : row + count, 0:cells] = hi
        table_ref[row : row + count, cells:] = (pair - hi.astype(f32)).astype(bf16)

    for dz in range(2):
        row = lax.broadcasted_iota(jnp.int32, (LOW, 256), 0)
        col = lanes_of((LOW, 256))
        chooser = ((col == row) | (col == row + 128 + dz)).astype(f32).astype(bf16)
        for i, d in enumerate(CANON):
            dx, dy, climb = DIRS[d]
            if climb == dz:
                own = pad[d, 1 : 1 + size_x, 8 : 8 + size_y, :]
                other = pad[
                    OPP[d], 1 + dx : 1 + dx + size_x, 8 + dy : 8 + dy + size_y, :
                ]
                terms = [v.reshape(cells, 128) for v in (own, other)]
                put(LOW * i, LOW, jnp.concatenate(terms, axis=1), chooser)
    row = lax.broadcasted_iota(jnp.int32, (16, 640), 0)
    chooser = jnp.where(lanes_of((16, 640)) == 128 * row, 2.0, 0.0).astype(bf16)
    terms = [pad[d, 1 : 1 + size_x, 8 : 8 + size_y, :].reshape(cells, 128) for d in WALL]
    put(LOW * len(CANON), 16, jnp.concatenate(terms, axis=1), chooser)
    for i in range(PIECES):
        leaving(i).wait()


def collide(populations, relax_matrix):
    _, size_x, size_y, size_z = populations.shape
    face = jax.ShapeDtypeStruct((5 * size_y, size_z), f32)
    table = jax.ShapeDtypeStruct((LOW * len(CANON) + 16, 2 * size_x * size_y), bf16)
    return pl.pallas_call(
        collide_kernel,
        in_specs=[pl.BlockSpec(memory_space=pltpu.HBM)] * 2,
        out_specs=[pl.BlockSpec(memory_space=pltpu.HBM)] + [pl.BlockSpec(memory_space=VMEM)] * 5,
        out_shape=[jax.ShapeDtypeStruct(populations.shape, f32), table] + [face] * 4,
        scratch_shapes=[
            VMEM((19, 19), f32),
            VMEM((19, 19, 8, 128), f32),
            VMEM(populations.shape, f32),
            VMEM((19, size_x + 2, size_y + 16, size_z), f32),
            pltpu.SemaphoreType.DMA((PIECES + 1,)),
            pltpu.SemaphoreType.DMA((PIECES,)),
        ],
        compiler_params=pltpu.CompilerParams(vmem_limit_bytes=51 << 20),
        cost_estimate=pl.CostEstimate(flops=40_000_000, bytes_accessed=6_000_000, transcendentals=0),
        name="collide",
    )(relax_matrix, populations)


CHUNK = 512


def hot_rows(count, line):
    shape = (16, line.shape[1])
    offset = jnp.broadcast_to(line, shape) - lax.broadcasted_iota(jnp.int32, shape, 0)
    offset = offset.astype(jnp.int16)
    one, zero = jnp.ones(shape, bf16), jnp.zeros(shape, bf16)
    return jnp.concatenate(
        [jnp.where(offset == jnp.int16(b), one, zero) for b in range(0, count, 16)], axis=0
    )


def pick(table_ref, column, entry):
    rows, depth = table_ref.shape[0], table_ref.shape[1] // 2
    chunk = column.shape[1]
    hot = hot_rows(depth, column)
    hot = jnp.concatenate([hot, hot], axis=0)
    offset = entry - lax.broadcasted_iota(jnp.int32, (8, chunk), 0)
    acc = jnp.zeros((8, chunk), f32)
    found = jnp.dot(table_ref[...], hot, preferred_element_type=f32)
    for j in range(0, rows, 8):
        acc = jnp.where(offset == j, found[j : j + 8], acc)
    return jnp.sum(acc, axis=0, keepdims=True)


def member(direction, dirs, first=1, step=1):
    out = jnp.zeros(direction.shape, jnp.int32)
    for k, d in enumerate(dirs):
        out = jnp.where(direction == d, first + step * k, out)
    return out


def sides(direction):
    return (
        member(direction, XP),
        member(direction, XM),
        member(direction, YP),
        member(direction, YM),
    )


def tile_of(ref, k):
    start = pl.multiple_of(k * 1024, 1024)
    return jnp.concatenate(
        [ref[0, :, pl.ds(start + 128 * s, 128)] for s in range(8)], axis=0
    )


def line_of(ref, i):
    return jnp.concatenate([ref[pl.ds(4 * i + k, 1), :] for k in range(4)], axis=1)


def link_kernel(half, table_ref, cell_ref, dir_ref, value_ref, column, entry):
    def index(k, carry):
        cell, direction = tile_of(cell_ref, 8 * half + k), tile_of(dir_ref, 8 * half + k)
        xup, xdown, yup, ydown = sides(direction)
        forward = member(direction, CANON)
        backward = member(direction, [OPP[d] for d in CANON])
        wall = member(direction, WALL)
        back = (backward > 0).astype(jnp.int32)
        x = (cell >> 11) + back * ((xup > 0).astype(jnp.int32) - (xdown > 0).astype(jnp.int32))
        y = ((cell >> 7) & 15) + back * (
            (yup > 0).astype(jnp.int32) - (ydown > 0).astype(jnp.int32)
        )
        z = cell & 31
        bottom = (wall > 0) & (z == 0)
        z = z - (wall > 0).astype(jnp.int32)
        which = forward + backward - 1
        inside = (x >= 0) & (x < 16) & (y >= 0) & (y < 16) & (which >= 0)
        rows = pl.ds(pl.multiple_of(k * 8, 8), 8)
        column[rows, :] = jnp.where(bottom, cell >> 7, x * 16 + y)
        entry[rows, :] = jnp.where(bottom, 287 + wall, jnp.where(inside, which * 32 + z, -8))
        return carry

    lax.fori_loop(0, 8, index, 0)

    def one_chunk(i, carry):
        found = pick(table_ref, line_of(column, i), line_of(entry, i))
        for k in range(4):
            value_ref[pl.ds(4 * i + k, 1), :] = found[:, 128 * k : 128 * k + 128]
        return carry

    lax.fori_loop(0, 16, one_chunk, 0, unroll=8)


def interior_links(half, table, cells, dirs):
    shape = (64, 128)
    return pl.pallas_call(
        functools.partial(link_kernel, half),
        in_specs=[pl.BlockSpec(memory_space=VMEM)] * 3,
        out_specs=pl.BlockSpec(memory_space=VMEM),
        out_shape=jax.ShapeDtypeStruct(shape, f32),
        scratch_shapes=[VMEM(shape, jnp.int32)] * 2,
        compiler_params=pltpu.CompilerParams(vmem_limit_bytes=24 << 20),
        cost_estimate=pl.CostEstimate(
            flops=6_000_000_000, bytes_accessed=1_000_000, transcendentals=0
        ),
        name="interior_links",
    )(table, cells, dirs)


def scatter_kernel(
    first_ref, second_ref, cell_ref, dir_ref, grain_ref,
    xlow_ref, xhigh_ref, ylow_ref, yhigh_ref,
    ownx_low_ref, ownx_high_ref, owny_low_ref, owny_high_ref,
    self_ref, peer_ref, normal_ref, gap_ref, state_ref,
    out_ref,
    table, column, entry, frames, slots, signs,
):
    size = 16
    lane = lanes_of((size, 128))
    for side in range(2):
        for group in range(3):
            acc = jnp.zeros((size, 128), f32)
            for j in range(4 * group, min(4 * group + 4, 10)):
                d = (XP + XM)[j] if side == 0 else (YP + YM)[j]
                q = OPP[d]
                dx, dy, dz = DIRS[d]
                high = j < 5
                if side == 0:
                    along = dy
                    ref = xhigh_ref if high else xlow_ref
                    mine = ownx_high_ref if high else ownx_low_ref
                    k = (XM if high else XP).index(q)
                    ends = ref[5 * size : 5 * size + 1], ref[5 * size + 1 : 5 * size + 2]
                else:
                    along = dx
                    ref = yhigh_ref if high else ylow_ref
                    mine = owny_high_ref if high else owny_low_ref
                    k = (YM if high else YP).index(q)
                    ends = (jnp.zeros((1, 128), f32),) * 2
                face = ref[k * size : (k + 1) * size]
                if along == 1:
                    face = jnp.concatenate([face[1:], ends[1]], axis=0)
                elif along == -1:
                    face = jnp.concatenate([ends[0], face[:-1]], axis=0)
                if dz:
                    face = pltpu.roll(face, (-dz) % 128, 1)
                if d not in CANON:
                    face = face + mine[(j % 5) * size : (j % 5 + 1) * size]
                if dz == -1:
                    face = jnp.where(lane == 0, 0.0, face)
                shift = (j % 4) * LOW
                if shift:
                    face = pltpu.roll(face, shift, 1)
                acc = jnp.where((lane >= shift) & (lane < shift + LOW), face, acc)
            hi = acc.astype(bf16)
            lo = (acc - hi.astype(f32)).astype(bf16)
            row = 16 * (3 * side + group)
            table[row : row + 16, 0:128] = hi
            table[row : row + 16, 128:256] = lo

    def index(k, carry):
        cell, direction, grain = tile_of(cell_ref, k), tile_of(dir_ref, k), tile_of(grain_ref, k)
        xup, xdown, yup, ydown = sides(direction)
        zup = member(direction, [5, 11, 14, 15, 18], 1, 0)
        zdown = member(direction, WALL, 1, 0)
        x, y, z = cell >> 11, (cell >> 7) & 15, cell & 31
        jx = jnp.where(
            (x == 15) & (xup > 0), xup, jnp.where((x == 0) & (xdown > 0), xdown + 5, 0)
        )
        jy = jnp.where(
            (y == 15) & (yup > 0), yup, jnp.where((y == 0) & (ydown > 0), ydown + 5, 0)
        )
        which = jnp.where(jx > 0, jx, jy) - 1
        rows = pl.ds(pl.multiple_of(k * 8, 8), 8)
        column[rows, :] = (which & 3) * 32 + z
        place = (which >> 2) * 16 + jnp.where(jx > 0, y, 48 + x)
        entry[rows, :] = jnp.where(which >= 0, place, -8)
        frames[rows, :] = grain >> 7
        slots[rows, :] = grain & 127
        for c, (up, down) in enumerate(((xup, xdown), (yup, ydown), (zup, zdown))):
            signs[c, rows, :] = (up > 0).astype(f32) - (down > 0).astype(f32)
        return carry

    lax.fori_loop(0, 16, index, 0)
    frames_of = lax.broadcasted_iota(jnp.int32, (16, CHUNK), 0)

    def one_chunk(value_ref, before, k, acc):
        i = before + k
        value = line_of(value_ref, k) + pick(table, line_of(column, i), line_of(entry, i))
        hit = frames_of == line_of(frames, i)
        sign = [line_of(signs.at[c], i) for c in range(3)]
        terms = []
        for part in split3(value):
            part = part.astype(f32)
            for c in range(3):
                terms.append(jnp.where(hit, part * sign[c], 0.0).astype(bf16))
        hot = hot_rows(128, line_of(slots, i))
        return acc + lax.dot_general(
            jnp.concatenate(terms, axis=0), hot, (((1,), (1,)), ((), ())), preferred_element_type=f32
        )

    acc = jnp.zeros((144, 128), f32)
    for before, value_ref in ((0, first_ref), (16, second_ref)):
        acc = lax.fori_loop(
            0, 16, functools.partial(one_chunk, value_ref, before), acc, unroll=True
        )
    total = acc[0:48] + (acc[48:96] + acc[96:144])
    rows = [total[0:9], total[16:25], total[32:41], jnp.zeros((5, 128), f32)]
    for ref in (self_ref, peer_ref):
        rows += [ref[0, :, 128 * t : 128 * t + 128].astype(f32) for t in range(4)]
    for c in range(3):
        rows += [normal_ref[0, c, :, 128 * t : 128 * t + 128] for t in range(4)]
    rows += [gap_ref[0, :, 128 * t : 128 * t + 128] for t in range(4)]
    rows += [state_ref[0, 0], jnp.zeros((4, 128), f32)]
    message = jnp.concatenate(rows, axis=0)
    for k in range(8):
        out_ref[k] = message


def link_sums(values, links, halos, faces, contacts):
    args = values + links + halos + faces + contacts
    square = (128, 128)
    return pl.pallas_call(
        scatter_kernel,
        in_specs=[pl.BlockSpec(memory_space=VMEM)] * len(args),
        out_specs=pl.BlockSpec(memory_space=VMEM),
        out_shape=jax.ShapeDtypeStruct((8, 64, 128), f32),
        scratch_shapes=[VMEM((96, 256), bf16)]
        + [VMEM(square, jnp.int32)] * 4
        + [VMEM((3,) + square, f32)],
        compiler_params=pltpu.CompilerParams(vmem_limit_bytes=24 << 20),
        cost_estimate=pl.CostEstimate(
            flops=2_000_000_000, bytes_accessed=500_000, transcendentals=0
        ),
        name="link_sums",
    )(*args)


def stream_kernel(centre_ref, xlow_ref, xhigh_ref, ylow_ref, yhigh_ref, out_ref, pad):
    step = pl.program_id(0)
    block_x = out_ref.shape[1]
    size_x, size_y = centre_ref.shape[1], centre_ref.shape[2]

    @pl.when(step == 0)
    def _():
        for q in range(19):
            pad[q, 1 : 1 + size_x, 8 : 8 + size_y] = centre_ref[q]
        for k in range(5):
            pad[YP[k], 1 : 1 + size_x, 7, :] = ylow_ref[k * size_x : (k + 1) * size_x]
            pad[YM[k], 1 : 1 + size_x, 8 + size_y, :] = yhigh_ref[k * size_x : (k + 1) * size_x]
            pad[XP[k], 0, 8 : 8 + size_y, :] = xlow_ref[k * size_y : (k + 1) * size_y]
            pad[XM[k], 1 + size_x, 8 : 8 + size_y, :] = xhigh_ref[k * size_y : (k + 1) * size_y]
        base = 5 * size_y
        for q, row in ((7, 7), (9, 8 + size_y)):
            pad[q, 0, row : row + 1, :] = xlow_ref[base + (row > 8) : base + (row > 8) + 1]
        for q, row in ((10, 7), (8, 8 + size_y)):
            pad[q, 1 + size_x, row : row + 1, :] = xhigh_ref[base + (row > 8) : base + (row > 8) + 1]

    lane = lanes_of((size_y, 128))

    def one_row(i, carry):
        x = step * block_x + i
        for q in range(19):
            dx, dy, dz = DIRS[q]
            moved = pad[q, 1 + x - dx, 8 - dy : 8 - dy + size_y, :]
            if dz:
                moved = pltpu.roll(moved, dz % 128, 1)
                wall = 0 if dz == 1 else 127
                moved = jnp.where(lane == wall, pad[OPP[q], 1 + x, 8 : 8 + size_y, :], moved)
            out_ref[q, i] = moved
        return carry

    lax.fori_loop(0, block_x, one_row, 0)


def passed(centre, xlow, xhigh, ylow, yhigh):
    _, size_x, size_y, size_z = centre.shape
    block_x = 4
    return pl.pallas_call(
        stream_kernel,
        grid=(size_x // block_x,),
        in_specs=[whole(a.shape) for a in (centre, xlow, xhigh, ylow, yhigh)],
        out_specs=pl.BlockSpec((19, block_x, size_y, size_z), lambda i: (0, i, 0, 0)),
        out_shape=jax.ShapeDtypeStruct(centre.shape, f32),
        scratch_shapes=[VMEM((19, size_x + 2, size_y + 16, size_z), f32)],
        compiler_params=pltpu.CompilerParams(vmem_limit_bytes=40 << 20),
        cost_estimate=pl.CostEstimate(flops=10_000_000, bytes_accessed=6_000_000, transcendentals=0),
        name="passed",
    )(centre, xlow, xhigh, ylow, yhigh)


def across(v, by):
    return pltpu.roll(v, by % 8, 0) if by % 8 else v


def look_up(table, index):
    return jnp.take_along_axis(table, index, axis=1)


def fold(sums_ref, stride, dxs):
    out = []
    for k in range(len(dxs)):
        for c in range(3):
            total = None
            for dyi in range(3):
                row = sums_ref[:, c * stride + 3 * k + dyi, :]
                row = across(row, dyi - 1)
                total = row if total is None else total + row
            out.append(total)
    return out


def column_index(contact, t):
    own = contact(0, t).astype(jnp.int32)
    peer = contact(1, t).astype(jnp.int32)
    return own, peer & 127, peer >> 7


def peer_tables(read, dxs):
    tables = {}
    for dxi in dxs:
        base = read(dxi - 1)
        for dyi in range(3):
            tables[3 * dxi + dyi] = across(base, 1 - dyi)
    return tables


def pick_peer(tables, slot, frame):
    found = jnp.zeros(slot.shape, f32)
    for k, table in tables.items():
        found = jnp.where(frame == k, look_up(table, slot), found)
    return found


def one_column(contact, vel, denom, impulse, store_impulse, sums_ref, dxs):
    indices = [column_index(contact, t) for t in range(4)]
    closing = [contact(5, t) for t in range(4)]
    for c in range(3):
        tables = peer_tables(lambda j: vel(j, c), dxs)
        for t in range(4):
            own, slot, frame = indices[t]
            gap = pick_peer(tables, slot, frame) - look_up(vel(0, c), jnp.minimum(own, 127))
            closing[t] = closing[t] + contact(2 + c, t) * gap
    kicks = []
    for t in range(4):
        new = jnp.maximum(0.0, impulse(t) - 0.5 * closing[t] / denom(t))
        new = jnp.where(indices[t][0] < 128, new, 0.0)
        store_impulse(t, new)
        kicks.append([[p.astype(f32) for p in split3(new * contact(2 + c, t))] for c in range(3)])
    every = len(dxs) == 3
    height = 16 if every else 8
    frames_of = lax.broadcasted_iota(jnp.int32, (height, 512), 0) + 3 * dxs[0]
    nt = (((1,), (1,)), ((), ()))

    def line(parts, y):
        return jnp.concatenate([p[y : y + 1, :] for p in parts], axis=1)

    for y in range(8):
        hit = frames_of == line([indices[t][2] for t in range(4)], y)
        hot_peer = hot_rows(128, line([indices[t][1] for t in range(4)], y))
        rows = [
            line([kicks[t][c][piece] for t in range(4)], y) for piece in range(3) for c in range(3)
        ]
        terms = [jnp.where(hit, r, 0.0) for r in rows]
        if not every:
            terms.append(jnp.zeros((8, 512), f32))
        terms = jnp.concatenate(terms, axis=0).astype(bf16)
        found = lax.dot_general(terms, hot_peer, nt, preferred_element_type=f32)
        step = 3 * height
        sums_ref[y, 0:step] = found[0:step] + (found[step : 2 * step] + found[2 * step : 3 * step])
        if every:
            hot_own = hot_rows(128, line([indices[t][0] for t in range(4)], y))
            mine = jnp.concatenate(rows + [jnp.zeros((7, 512), f32)], axis=0).astype(bf16)
            mine = lax.dot_general(mine, hot_own, nt, preferred_element_type=f32)
            mine = mine[0:3] + (mine[3:6] + mine[6:9])
            for c in range(3):
                sums_ref[y, 16 * c + 9 : 16 * c + 10] = mine[c : c + 1]


def fold_kernel(frames_ref, to_low_ref, to_high_ref):
    force = fold(frames_ref, 9, (0, 1, 2))
    for c in range(3):
        to_low_ref[c] = force[3 + c]
        to_low_ref[3 + c] = force[c]
        to_high_ref[c] = force[3 + c]
        to_high_ref[3 + c] = force[6 + c]
    for r in range(28):
        row = frames_ref[:, 32 + r, :]
        to_low_ref[6 + r] = row
        to_high_ref[6 + r] = row


def far_kernel(mine_low_ref, mine_high_ref, low_ref, high_ref, to_low_ref, to_high_ref):
    total = mine_low_ref[0:3] + (low_ref[3:6] + high_ref[3:6])
    to_low_ref[0:3] = total
    to_high_ref[0:3] = total
    to_low_ref[3:] = mine_low_ref[3:]
    to_high_ref[3:] = mine_high_ref[3:]


def totals(mine_low_ref, mine_high_ref, low1_ref, high1_ref, low2_ref, high2_ref):
    return [
        low2_ref[0:3],
        low1_ref[0:3] + (low2_ref[3:6] + mine_low_ref[3:6]),
        mine_low_ref[0:3] + (low1_ref[3:6] + high1_ref[3:6]),
        high1_ref[0:3] + (mine_high_ref[3:6] + high2_ref[3:6]),
        high2_ref[0:3],
    ]


def reach(j):
    return {0: (2,), 4: (0,)}.get(j, (0, 1, 2))


def prep(parts, contact_ref, grain_ref, denom_ref):
    for j, part in enumerate(parts):
        contact_ref[j] = part[6:30]
        grain_ref[j] = part[30:34]
    for j in range(5):
        contact = lambda f, t: contact_ref[j, 4 * f + t]
        mass = lambda k: grain_ref[j + k, 3]
        tables = peer_tables(mass, reach(j))
        for t in range(4):
            own, slot, frame = column_index(contact, t)
            denom_ref[j, t] = pick_peer(tables, slot, frame) + look_up(
                mass(0), jnp.minimum(own, 127)
            )


def two_sweeps(contact_ref, grain_ref, denom_ref, base_ref, vel_ref, impulse_ref, sums_ref, kick_ref):
    def sweep(j):
        dxs = reach(j)
        one_column(
            lambda f, t: contact_ref[j, 4 * f + t],
            lambda k, c: vel_ref[j + k, c],
            lambda t: denom_ref[j, t],
            lambda t: impulse_ref[j, t],
            lambda t, v: impulse_ref.__setitem__((j, t), v),
            sums_ref.at[j],
            dxs,
        )
        rows = fold(sums_ref.at[j], 16 if len(dxs) == 3 else 8, dxs)
        for k, dxi in enumerate(dxs):
            for c in range(3):
                row = rows[3 * k + c]
                if dxi == 1:
                    row = row - sums_ref[j, :, 16 * c + 9, :]
                kick_ref[j, 3 * dxi + c] = row

    for j in range(5):
        sweep(j)
    for j in range(1, 4):
        for c in range(3):
            total = kick_ref[j, 3 + c] + (kick_ref[j - 1, 6 + c] + kick_ref[j + 1, c])
            vel_ref[j, c] = base_ref[j, c] + grain_ref[j, 3] * total
    sweep(2)


def row_of(v, y):
    hit = lax.broadcasted_iota(jnp.int32, (8, 128), 0) == y
    return jnp.sum(jnp.where(hit, v, 0.0), axis=0, keepdims=True)


def first_kernel(
    place_ref, mine_low_ref, mine_high_ref, low1_ref, high1_ref, low2_ref, high2_ref,
    force_ref, free_ref, to_low_ref, to_high_ref, contact_ref, grain_ref, denom_ref,
    vel, impulse, sums, kick,
):
    y = place_ref[0]
    refs = (mine_low_ref, mine_high_ref, low1_ref, high1_ref, low2_ref, high2_ref)
    prep((low2_ref, low1_ref, mine_low_ref, high1_ref, high2_ref), contact_ref, grain_ref, denom_ref)
    for j, total in enumerate(totals(*refs)):
        for c in range(3):
            if j == 2:
                force_ref[0, c] = row_of(total[c], y)
            free = grain_ref[j, c] + grain_ref[j, 3] * total[c]
            free_ref[j, c] = free
            vel[j, c] = free
    impulse[...] = jnp.zeros(impulse.shape, f32)
    two_sweeps(contact_ref, grain_ref, denom_ref, free_ref, vel, impulse, sums, kick)
    to_low_ref[0:3] = kick[2, 3:6]
    to_low_ref[3:6] = kick[2, 0:3]
    to_low_ref[6:10] = impulse[2]
    to_high_ref[0:3] = kick[2, 3:6]
    to_high_ref[3:6] = kick[2, 6:9]
    to_high_ref[6:10] = impulse[2]


def second_kernel(
    place_ref, mine_low_ref, mine_high_ref, low1_ref, high1_ref, low2_ref, high2_ref,
    contact_ref, grain_ref, denom_ref, free_ref,
    to_low_ref, to_high_ref, impulse_ref, base_ref, vel, impulse, sums, kick,
):
    y = place_ref[0]
    refs = (mine_low_ref, mine_high_ref, low1_ref, high1_ref, low2_ref, high2_ref)
    for j, total in enumerate(totals(*refs)):
        for c in range(3):
            vel[j, c] = free_ref[j, c] + grain_ref[j, 3] * total[c]
    for j, ref in enumerate((low2_ref, low1_ref, mine_low_ref, high1_ref, high2_ref)):
        impulse[j] = ref[6:10]
    two_sweeps(contact_ref, grain_ref, denom_ref, free_ref, vel, impulse, sums, kick)
    for t in range(4):
        impulse_ref[0, :, 128 * t : 128 * t + 128] = row_of(impulse[2, t], y)
    mass = row_of(grain_ref[2, 3], y)
    for c in range(3):
        to_low_ref[c : c + 1] = row_of(kick[2, c], y)
        to_high_ref[c : c + 1] = row_of(kick[2, 6 + c], y)
        base_ref[c : c + 1] = row_of(free_ref[2, c], y)
        base_ref[3 + c : 4 + c] = row_of(kick[2, 3 + c], y)
    base_ref[6:7] = mass
    base_ref[7:8] = mass


def final_kernel(base_ref, low_ref, high_ref, out_ref):
    total = base_ref[3:6] + (low_ref[...] + high_ref[...])
    speed = base_ref[0:3] + base_ref[6:7] * total
    for c in range(3):
        out_ref[0, c] = speed[c : c + 1]


def edge_kernel(xhi_ref, xlo_ref, ylow_ref, yhigh_ref, after_ref, to_low_ref, to_high_ref):
    size = 16
    last = size - 1
    for out_ref, face_ref, first, second in (
        (to_high_ref, xhi_ref, size + last, 2 * size + last),
        (to_low_ref, xlo_ref, 2 * size, size),
    ):
        out_ref[0:80] = face_ref[...]
        corners = [ylow_ref[first : first + 1], yhigh_ref[second : second + 1]]
        out_ref[80:88] = jnp.concatenate(corners + [jnp.zeros((6, 128), f32)], axis=0)


def vmem_call(kernel, outs, args, scratch=(), flops=1_000_000, place=None):
    specs = [pl.BlockSpec(memory_space=VMEM) for _ in args]
    if place is not None:
        args = (place,) + tuple(args)
        specs = [pl.BlockSpec(memory_space=pltpu.SMEM)] + specs
    return pl.pallas_call(
        kernel,
        in_specs=specs,
        out_specs=[pl.BlockSpec(memory_space=VMEM) for _ in outs],
        out_shape=[jax.ShapeDtypeStruct(s, f32) for s in outs],
        scratch_shapes=list(scratch),
        compiler_params=pltpu.CompilerParams(vmem_limit_bytes=24 << 20),
        cost_estimate=pl.CostEstimate(flops=flops, bytes_accessed=500_000, transcendentals=0),
        name=kernel.__name__,
    )(*args)


def shift(value, axis, by):
    size = lax.axis_size(axis)
    return lax.ppermute(value, axis, [(i, (i + by) % size) for i in range(size)])


def both_ways(to_low, to_high, axis, by):
    return shift(to_high, axis, by), shift(to_low, axis, -by)


def per_device(
    populations,
    relax_matrix,
    grain_state,
    link_cell,
    link_dir,
    link_grain,
    contact_self,
    contact_peer,
    contact_normal,
    contact_gap,
):
    place = lax.axis_index("gy").astype(jnp.int32).reshape(1)
    links = (link_cell, link_dir, link_grain)
    contacts = (
        contact_self,
        contact_peer,
        contact_normal.transpose(0, 2, 1, 3),
        contact_gap,
        grain_state,
    )

    centre, table, yhi, ylo, xhi, xlo = collide(populations, relax_matrix)
    ylow, yhigh = both_ways(ylo, yhi, "gy", 1)
    first = interior_links(0, table, link_cell, link_dir)
    to_low, to_high = vmem_call(edge_kernel, [(88, 128)] * 2, (xhi, xlo, ylow, yhigh, first))
    xlow, xhigh = both_ways(to_low, to_high, "gx", 1)
    second = interior_links(1, table, link_cell, link_dir)
    halos = (xlow, xhigh, ylow, yhigh)
    spread = link_sums((first, second), links, halos, (xlo, xhi, ylo, yhi), contacts)
    populations_next = passed(centre, *halos)

    spread = lax.all_to_all(spread, "gy", 0, 0)
    mine = vmem_call(fold_kernel, [(34, 8, 128)] * 2, (spread,))
    near = both_ways(*mine, "gx", 1)
    far = both_ways(*vmem_call(far_kernel, [(34, 8, 128)] * 2, (*mine, *near)), "gx", 2)
    scratch = [
        VMEM((5, 3, 8, 128), f32),
        VMEM((5, 4, 8, 128), f32),
        VMEM((5, 8, 48, 128), f32),
        VMEM((5, 9, 8, 128), f32),
    ]
    force, free, *mine_and_static = vmem_call(
        first_kernel,
        [
            (1, 3, 1, 128),
            (5, 3, 8, 128),
            (10, 8, 128),
            (10, 8, 128),
            (5, 24, 8, 128),
            (5, 4, 8, 128),
            (5, 4, 8, 128),
        ],
        (*mine, *near, *far),
        scratch,
        place=place,
    )
    mine, static = mine_and_static[:2], mine_and_static[2:]

    near = both_ways(*mine, "gx", 1)
    far = both_ways(*vmem_call(far_kernel, [(10, 8, 128)] * 2, (*mine, *near)), "gx", 2)
    *mine, impulse, base = vmem_call(
        second_kernel,
        [(3, 128), (3, 128), (1, 1, 512), (8, 128)],
        (*mine, *near, *far, *static, free),
        scratch,
        place=place,
    )
    near = both_ways(*mine, "gx", 1)
    (velocity,) = vmem_call(final_kernel, [(1, 3, 1, 128)], (base, *near))
    return (
        populations_next,
        force.transpose(0, 2, 1, 3),
        velocity.transpose(0, 2, 1, 3),
        impulse,
    )


def solution(mesh):
    placed = (
        P(None, "gx", "gy", None),
        P(),
        P("gx", "gy", None, None),
        P("gx", "gy", None),
        P("gx", "gy", None),
        P("gx", "gy", None),
        P("gx", "gy", None),
        P("gx", "gy", None),
        P("gx", "gy", None, None),
        P("gx", "gy", None),
    )
    return jax.shard_map(
        per_device,
        mesh=mesh,
        in_specs=placed,
        out_specs=(
            P(None, "gx", "gy", None),
            P("gx", "gy", None, None),
            P("gx", "gy", None, None),
            P("gx", "gy", None),
        ),
        check_vma=False,
    )
```

```python
import functools

import jax
import jax.numpy as jnp
from jax import lax
from jax.experimental import pallas as pl
from jax.experimental.pallas import tpu as pltpu
from jax.sharding import PartitionSpec as P

SWEEPS = 4
DIRS = [
    [0, 0, 0],
    [1, 0, 0],
    [-1, 0, 0],
    [0, 1, 0],
    [0, -1, 0],
    [0, 0, 1],
    [0, 0, -1],
    [1, 1, 0],
    [-1, -1, 0],
    [1, -1, 0],
    [-1, 1, 0],
    [1, 0, 1],
    [-1, 0, -1],
    [1, 0, -1],
    [-1, 0, 1],
    [0, 1, 1],
    [0, -1, -1],
    [0, 1, -1],
    [0, -1, 1],
]
OPP = [0, 2, 1, 4, 3, 6, 5, 8, 7, 10, 9, 12, 11, 14, 13, 16, 15, 18, 17]
WEIGHT = [1.0 / 3.0] + [1.0 / 18.0] * 6 + [1.0 / 36.0] * 12
XP = [1, 7, 9, 11, 13]
XM = [2, 8, 10, 12, 14]
YP = [3, 7, 10, 15, 17]
YM = [4, 8, 9, 16, 18]
CANON = [1, 3, 5, 7, 9, 11, 14, 15, 18]
WALL = [6, 12, 13, 16, 17]
LOW = 32
highest = lax.Precision.HIGHEST
f32 = jnp.float32
bf16 = jnp.bfloat16
VMEM = pltpu.VMEM


def whole(shape):
    return pl.BlockSpec(shape, lambda *_: (0,) * len(shape))


def lanes_of(shape):
    return lax.broadcasted_iota(jnp.int32, shape, len(shape) - 1)


def split3(v):
    hi = v.astype(bf16)
    rest = v - hi.astype(f32)
    mid = rest.astype(bf16)
    low = (rest - mid.astype(f32)).astype(bf16)
    return hi, mid, low


PIECES = 4


def collide_kernel(
    relax_hbm, pop_hbm, centre_hbm, table_ref, yhi_ref, ylo_ref, xhi_ref, xlo_ref,
    relax, rs, pop, pad, in_sem, out_sem,
):
    size_x, size_y = pop.shape[1], pop.shape[2]
    piece_x = size_x // PIECES

    def arriving(i):
        part = pl.ds(i * piece_x, piece_x)
        return pltpu.make_async_copy(pop_hbm.at[:, part], pop.at[:, part], in_sem.at[i])

    def leaving(i):
        part = pl.ds(i * piece_x, piece_x)
        inner = pl.ds(1 + i * piece_x, piece_x)
        return pltpu.make_async_copy(
            pad.at[:, inner, 8 : 8 + size_y], centre_hbm.at[:, part], out_sem.at[i]
        )

    matrix = pltpu.make_async_copy(relax_hbm, relax, in_sem.at[PIECES])
    matrix.start()
    for i in range(PIECES):
        arriving(i).start()
    zero = jnp.zeros((size_x + 2, 8, 128), f32)
    for q in YP + YM:
        pad[q, :, 0:8] = zero
        pad[q, :, 8 + size_y :] = zero
    for q in XP + XM:
        pad[q, 0] = jnp.zeros(pad.shape[2:], f32)
        pad[q, size_x + 1] = jnp.zeros(pad.shape[2:], f32)
    matrix.wait()
    for j in range(19):
        column = jnp.broadcast_to(relax[:, j : j + 1], (19, 128))
        for q in range(19):
            rs[j, q] = jnp.broadcast_to(column[q : q + 1], (8, 128))

    def one_row(x, carry):
        f = [pop[q, x] for q in range(19)]
        rho = f[0]
        for q in range(1, 19):
            rho = rho + f[q]
        speeds = []
        inverse = 1.0 / rho
        for axis in range(3):
            total = None
            for q in range(1, 19, 2):
                sign = DIRS[q][axis]
                if sign:
                    diff = f[q] - f[q + 1] if sign > 0 else f[q + 1] - f[q]
                    total = diff if total is None else total + diff
            speeds.append(total * inverse)
        ux, uy, uz = speeds
        base = 1.0 - 1.5 * (ux * ux + uy * uy + uz * uz)
        neq = [f[0] - WEIGHT[0] * rho * base]
        for q in range(1, 19, 2):
            along = None
            for axis in range(3):
                sign = DIRS[q][axis]
                if sign:
                    if along is None:
                        along = speeds[axis]
                    else:
                        along = along + speeds[axis] if sign > 0 else along - speeds[axis]
            scale = WEIGHT[q] * rho
            even = scale * (base + 4.5 * (along * along))
            odd = scale * (3.0 * along)
            neq.append(f[q] - (even + odd))
            neq.append(f[q + 1] - (even - odd))
        for q in range(19):
            parts = [None, None]
            for j in range(19):
                term = (neq[j].reshape(2, 8, 128) * rs[j, q][None]).reshape(16, 128)
                parts[j % 2] = term if parts[j % 2] is None else parts[j % 2] + term
            out = f[q] - (parts[0] + parts[1])
            pad[q, 1 + x, 8 : 8 + size_y] = out
        return carry

    def one_piece(i, carry):
        arriving(i).wait()
        lax.fori_loop(i * piece_x, (i + 1) * piece_x, one_row, 0)
        leaving(i).start()
        return carry

    lax.fori_loop(0, PIECES, one_piece, 0)
    for k in range(5):
        yhi_ref[k * size_x : (k + 1) * size_x] = pad[YP[k], 1 : 1 + size_x, 7 + size_y, :]
        ylo_ref[k * size_x : (k + 1) * size_x] = pad[YM[k], 1 : 1 + size_x, 8, :]
        xhi_ref[k * size_y : (k + 1) * size_y] = pad[XP[k], size_x, 8 : 8 + size_y, :]
        xlo_ref[k * size_y : (k + 1) * size_y] = pad[XM[k], 1, 8 : 8 + size_y, :]

    cells = size_x * size_y
    nt = (((1,), (1,)), ((), ()))

    def put(row, count, terms, chooser):
        hi = terms.astype(bf16)
        lo = (terms - hi.astype(f32)).astype(bf16)
        pair = lax.dot_general(chooser, hi, nt, preferred_element_type=f32)
        pair = pair + lax.dot_general(chooser, lo, nt, preferred_element_type=f32)
        hi = pair.astype(bf16)
        table_ref[row : row + count, 0:cells] = hi
        table_ref[row : row + count, cells:] = (pair - hi.astype(f32)).astype(bf16)

    for dz in range(2):
        row = lax.broadcasted_iota(jnp.int32, (LOW, 256), 0)
        col = lanes_of((LOW, 256))
        chooser = ((col == row) | (col == row + 128 + dz)).astype(f32).astype(bf16)
        for i, d in enumerate(CANON):
            dx, dy, climb = DIRS[d]
            if climb == dz:
                own = pad[d, 1 : 1 + size_x, 8 : 8 + size_y, :]
                other = pad[
                    OPP[d], 1 + dx : 1 + dx + size_x, 8 + dy : 8 + dy + size_y, :
                ]
                terms = [v.reshape(cells, 128) for v in (own, other)]
                put(LOW * i, LOW, jnp.concatenate(terms, axis=1), chooser)
    row = lax.broadcasted_iota(jnp.int32, (16, 640), 0)
    chooser = jnp.where(lanes_of((16, 640)) == 128 * row, 2.0, 0.0).astype(bf16)
    terms = [pad[d, 1 : 1 + size_x, 8 : 8 + size_y, :].reshape(cells, 128) for d in WALL]
    put(LOW * len(CANON), 16, jnp.concatenate(terms, axis=1), chooser)
    for i in range(PIECES):
        leaving(i).wait()


def collide(populations, relax_matrix):
    _, size_x, size_y, size_z = populations.shape
    face = jax.ShapeDtypeStruct((5 * size_y, size_z), f32)
    table = jax.ShapeDtypeStruct((LOW * len(CANON) + 16, 2 * size_x * size_y), bf16)
    return pl.pallas_call(
        collide_kernel,
        in_specs=[pl.BlockSpec(memory_space=pltpu.HBM)] * 2,
        out_specs=[pl.BlockSpec(memory_space=pltpu.HBM)] + [pl.BlockSpec(memory_space=VMEM)] * 5,
        out_shape=[jax.ShapeDtypeStruct(populations.shape, f32), table] + [face] * 4,
        scratch_shapes=[
            VMEM((19, 19), f32),
            VMEM((19, 19, 8, 128), f32),
            VMEM(populations.shape, f32),
            VMEM((19, size_x + 2, size_y + 16, size_z), f32),
            pltpu.SemaphoreType.DMA((PIECES + 1,)),
            pltpu.SemaphoreType.DMA((PIECES,)),
        ],
        compiler_params=pltpu.CompilerParams(vmem_limit_bytes=51 << 20),
        cost_estimate=pl.CostEstimate(flops=40_000_000, bytes_accessed=6_000_000, transcendentals=0),
        name="collide",
    )(relax_matrix, populations)


CHUNK = 512


def hot_rows(count, line):
    shape = (16, line.shape[1])
    offset = jnp.broadcast_to(line, shape) - lax.broadcasted_iota(jnp.int32, shape, 0)
    offset = offset.astype(jnp.int16)
    one, zero = jnp.ones(shape, bf16), jnp.zeros(shape, bf16)
    return jnp.concatenate(
        [jnp.where(offset == jnp.int16(b), one, zero) for b in range(0, count, 16)], axis=0
    )


def pick(table_ref, column, entry):
    rows, depth = table_ref.shape[0], table_ref.shape[1] // 2
    chunk = column.shape[1]
    hot = hot_rows(depth, column)
    hot = jnp.concatenate([hot, hot], axis=0)
    offset = entry - lax.broadcasted_iota(jnp.int32, (8, chunk), 0)
    acc = jnp.zeros((8, chunk), f32)
    found = jnp.dot(table_ref[...], hot, preferred_element_type=f32)
    for j in range(0, rows, 8):
        acc = jnp.where(offset == j, found[j : j + 8], acc)
    return jnp.sum(acc, axis=0, keepdims=True)


def member(direction, dirs, first=1, step=1):
    out = jnp.zeros(direction.shape, jnp.int32)
    for k, d in enumerate(dirs):
        out = jnp.where(direction == d, first + step * k, out)
    return out


def sides(direction):
    return (
        member(direction, XP),
        member(direction, XM),
        member(direction, YP),
        member(direction, YM),
    )


def tile_of(ref, k):
    start = pl.multiple_of(k * 1024, 1024)
    return jnp.concatenate(
        [ref[0, :, pl.ds(start + 128 * s, 128)] for s in range(8)], axis=0
    )


def line_of(ref, i):
    return jnp.concatenate([ref[pl.ds(4 * i + k, 1), :] for k in range(4)], axis=1)


def link_kernel(half, table_ref, cell_ref, dir_ref, value_ref, column, entry):
    def index(k, carry):
        cell, direction = tile_of(cell_ref, 8 * half + k), tile_of(dir_ref, 8 * half + k)
        xup, xdown, yup, ydown = sides(direction)
        forward = member(direction, CANON)
        backward = member(direction, [OPP[d] for d in CANON])
        wall = member(direction, WALL)
        back = (backward > 0).astype(jnp.int32)
        x = (cell >> 11) + back * ((xup > 0).astype(jnp.int32) - (xdown > 0).astype(jnp.int32))
        y = ((cell >> 7) & 15) + back * (
            (yup > 0).astype(jnp.int32) - (ydown > 0).astype(jnp.int32)
        )
        z = cell & 31
        bottom = (wall > 0) & (z == 0)
        z = z - (wall > 0).astype(jnp.int32)
        which = forward + backward - 1
        inside = (x >= 0) & (x < 16) & (y >= 0) & (y < 16) & (which >= 0)
        rows = pl.ds(pl.multiple_of(k * 8, 8), 8)
        column[rows, :] = jnp.where(bottom, cell >> 7, x * 16 + y)
        entry[rows, :] = jnp.where(bottom, 287 + wall, jnp.where(inside, which * 32 + z, -8))
        return carry

    lax.fori_loop(0, 8, index, 0)

    def one_chunk(i, carry):
        found = pick(table_ref, line_of(column, i), line_of(entry, i))
        for k in range(4):
            value_ref[pl.ds(4 * i + k, 1), :] = found[:, 128 * k : 128 * k + 128]
        return carry

    lax.fori_loop(0, 16, one_chunk, 0, unroll=True)


def interior_links(half, table, cells, dirs):
    shape = (64, 128)
    return pl.pallas_call(
        functools.partial(link_kernel, half),
        in_specs=[pl.BlockSpec(memory_space=VMEM)] * 3,
        out_specs=pl.BlockSpec(memory_space=VMEM),
        out_shape=jax.ShapeDtypeStruct(shape, f32),
        scratch_shapes=[VMEM(shape, jnp.int32)] * 2,
        compiler_params=pltpu.CompilerParams(vmem_limit_bytes=24 << 20),
        cost_estimate=pl.CostEstimate(
            flops=6_000_000_000, bytes_accessed=1_000_000, transcendentals=0
        ),
        name="interior_links",
    )(table, cells, dirs)


def scatter_kernel(
    first_ref, second_ref, cell_ref, dir_ref, grain_ref,
    xlow_ref, xhigh_ref, ylow_ref, yhigh_ref,
    ownx_low_ref, ownx_high_ref, owny_low_ref, owny_high_ref,
    self_ref, peer_ref, normal_ref, gap_ref, state_ref,
    mine_ref, to_low_ref, to_high_ref,
    table, column, entry, frames, slots, signs,
):
    size = 16
    lane = lanes_of((size, 128))
    for side in range(2):
        for group in range(3):
            acc = jnp.zeros((size, 128), f32)
            for j in range(4 * group, min(4 * group + 4, 10)):
                d = (XP + XM)[j] if side == 0 else (YP + YM)[j]
                q = OPP[d]
                dx, dy, dz = DIRS[d]
                high = j < 5
                if side == 0:
                    along = dy
                    ref = xhigh_ref if high else xlow_ref
                    mine = ownx_high_ref if high else ownx_low_ref
                    k = (XM if high else XP).index(q)
                    ends = ref[5 * size : 5 * size + 1], ref[5 * size + 1 : 5 * size + 2]
                else:
                    along = dx
                    ref = yhigh_ref if high else ylow_ref
                    mine = owny_high_ref if high else owny_low_ref
                    k = (YM if high else YP).index(q)
                    ends = (jnp.zeros((1, 128), f32),) * 2
                face = ref[k * size : (k + 1) * size]
                if along == 1:
                    face = jnp.concatenate([face[1:], ends[1]], axis=0)
                elif along == -1:
                    face = jnp.concatenate([ends[0], face[:-1]], axis=0)
                if dz:
                    face = pltpu.roll(face, (-dz) % 128, 1)
                if d not in CANON:
                    face = face + mine[(j % 5) * size : (j % 5 + 1) * size]
                if dz == -1:
                    face = jnp.where(lane == 0, 0.0, face)
                shift = (j % 4) * LOW
                if shift:
                    face = pltpu.roll(face, shift, 1)
                acc = jnp.where((lane >= shift) & (lane < shift + LOW), face, acc)
            hi = acc.astype(bf16)
            lo = (acc - hi.astype(f32)).astype(bf16)
            row = 16 * (3 * side + group)
            table[row : row + 16, 0:128] = hi
            table[row : row + 16, 128:256] = lo

    def index(k, carry):
        cell, direction, grain = tile_of(cell_ref, k), tile_of(dir_ref, k), tile_of(grain_ref, k)
        xup, xdown, yup, ydown = sides(direction)
        zup = member(direction, [5, 11, 14, 15, 18], 1, 0)
        zdown = member(direction, WALL, 1, 0)
        x, y, z = cell >> 11, (cell >> 7) & 15, cell & 31
        jx = jnp.where(
            (x == 15) & (xup > 0), xup, jnp.where((x == 0) & (xdown > 0), xdown + 5, 0)
        )
        jy = jnp.where(
            (y == 15) & (yup > 0), yup, jnp.where((y == 0) & (ydown > 0), ydown + 5, 0)
        )
        which = jnp.where(jx > 0, jx, jy) - 1
        rows = pl.ds(pl.multiple_of(k * 8, 8), 8)
        column[rows, :] = (which & 3) * 32 + z
        place = (which >> 2) * 16 + jnp.where(jx > 0, y, 48 + x)
        entry[rows, :] = jnp.where(which >= 0, place, -8)
        frames[rows, :] = grain >> 7
        slots[rows, :] = grain & 127
        for c, (up, down) in enumerate(((xup, xdown), (yup, ydown), (zup, zdown))):
            signs[c, rows, :] = (up > 0).astype(f32) - (down > 0).astype(f32)
        return carry

    lax.fori_loop(0, 16, index, 0)
    frames_of = lax.broadcasted_iota(jnp.int32, (16, CHUNK), 0)

    def one_chunk(value_ref, before, k, acc):
        i = before + k
        value = line_of(value_ref, k) + pick(table, line_of(column, i), line_of(entry, i))
        hit = frames_of == line_of(frames, i)
        sign = [line_of(signs.at[c], i) for c in range(3)]
        terms = []
        for part in split3(value):
            part = part.astype(f32)
            for c in range(3):
                terms.append(jnp.where(hit, part * sign[c], 0.0).astype(bf16))
        hot = hot_rows(128, line_of(slots, i))
        return acc + lax.dot_general(
            jnp.concatenate(terms, axis=0), hot, (((1,), (1,)), ((), ())), preferred_element_type=f32
        )

    acc = jnp.zeros((144, 128), f32)
    for before, value_ref in ((0, first_ref), (16, second_ref)):
        acc = lax.fori_loop(
            0, 16, functools.partial(one_chunk, value_ref, before), acc, unroll=True
        )
    total = acc[0:48] + (acc[48:96] + acc[96:144])
    for ref, dxi in ((to_low_ref, 0), (mine_ref, 1), (to_high_ref, 2)):
        parts = [total[16 * c + 3 * dxi : 16 * c + 3 * dxi + 3] for c in range(3)]
        ref[0:9] = jnp.concatenate(parts, axis=0)
    rows = []
    for ref in (self_ref, peer_ref):
        rows += [ref[0, :, 128 * t : 128 * t + 128].astype(f32) for t in range(4)]
    for c in range(3):
        rows += [normal_ref[0, c, :, 128 * t : 128 * t + 128] for t in range(4)]
    rows += [gap_ref[0, :, 128 * t : 128 * t + 128] for t in range(4)]
    rows += [state_ref[0, 0]]
    mine_ref[9:37] = jnp.concatenate(rows, axis=0)
    mine_ref[37:40] = jnp.zeros((3, 128), f32)


def link_sums(values, links, halos, faces, contacts):
    args = values + links + halos + faces + contacts
    square = (128, 128)
    return pl.pallas_call(
        scatter_kernel,
        in_specs=[pl.BlockSpec(memory_space=VMEM)] * len(args),
        out_specs=[pl.BlockSpec(memory_space=VMEM)] * 3,
        out_shape=[jax.ShapeDtypeStruct((n, 128), f32) for n in (40, 9, 9)],
        scratch_shapes=[VMEM((96, 256), bf16)]
        + [VMEM(square, jnp.int32)] * 4
        + [VMEM((3,) + square, f32)],
        compiler_params=pltpu.CompilerParams(vmem_limit_bytes=24 << 20),
        cost_estimate=pl.CostEstimate(
            flops=2_000_000_000, bytes_accessed=500_000, transcendentals=0
        ),
        name="link_sums",
    )(*args)


def stream_kernel(centre_ref, xlow_ref, xhigh_ref, ylow_ref, yhigh_ref, out_ref, pad):
    step = pl.program_id(0)
    block_x = out_ref.shape[1]
    size_x, size_y = centre_ref.shape[1], centre_ref.shape[2]

    @pl.when(step == 0)
    def _():
        for q in range(19):
            pad[q, 1 : 1 + size_x, 8 : 8 + size_y] = centre_ref[q]
        for k in range(5):
            pad[YP[k], 1 : 1 + size_x, 7, :] = ylow_ref[k * size_x : (k + 1) * size_x]
            pad[YM[k], 1 : 1 + size_x, 8 + size_y, :] = yhigh_ref[k * size_x : (k + 1) * size_x]
            pad[XP[k], 0, 8 : 8 + size_y, :] = xlow_ref[k * size_y : (k + 1) * size_y]
            pad[XM[k], 1 + size_x, 8 : 8 + size_y, :] = xhigh_ref[k * size_y : (k + 1) * size_y]
        base = 5 * size_y
        for q, row in ((7, 7), (9, 8 + size_y)):
            pad[q, 0, row : row + 1, :] = xlow_ref[base + (row > 8) : base + (row > 8) + 1]
        for q, row in ((10, 7), (8, 8 + size_y)):
            pad[q, 1 + size_x, row : row + 1, :] = xhigh_ref[base + (row > 8) : base + (row > 8) + 1]

    lane = lanes_of((size_y, 128))

    def one_row(i, carry):
        x = step * block_x + i
        for q in range(19):
            dx, dy, dz = DIRS[q]
            moved = pad[q, 1 + x - dx, 8 - dy : 8 - dy + size_y, :]
            if dz:
                moved = pltpu.roll(moved, dz % 128, 1)
                wall = 0 if dz == 1 else 127
                moved = jnp.where(lane == wall, pad[OPP[q], 1 + x, 8 : 8 + size_y, :], moved)
            out_ref[q, i] = moved
        return carry

    lax.fori_loop(0, block_x, one_row, 0)


def passed(centre, xlow, xhigh, ylow, yhigh):
    _, size_x, size_y, size_z = centre.shape
    block_x = 4
    return pl.pallas_call(
        stream_kernel,
        grid=(size_x // block_x,),
        in_specs=[whole(a.shape) for a in (centre, xlow, xhigh, ylow, yhigh)],
        out_specs=pl.BlockSpec((19, block_x, size_y, size_z), lambda i: (0, i, 0, 0)),
        out_shape=jax.ShapeDtypeStruct(centre.shape, f32),
        scratch_shapes=[VMEM((19, size_x + 2, size_y + 16, size_z), f32)],
        compiler_params=pltpu.CompilerParams(vmem_limit_bytes=40 << 20),
        cost_estimate=pl.CostEstimate(flops=10_000_000, bytes_accessed=6_000_000, transcendentals=0),
        name="passed",
    )(centre, xlow, xhigh, ylow, yhigh)


def across(v, by):
    return pltpu.roll(v, by % 8, 0) if by % 8 else v


def look_up(table, index):
    return jnp.take_along_axis(table, index, axis=1)


def fold(sums_ref, stride, dxs):
    out = []
    for k in range(len(dxs)):
        for c in range(3):
            total = None
            for dyi in range(3):
                row = sums_ref[:, c * stride + 3 * k + dyi, :]
                row = across(row, dyi - 1)
                total = row if total is None else total + row
            out.append(total)
    return out


def column_index(contact, t):
    own = contact(0, t).astype(jnp.int32)
    peer = contact(1, t).astype(jnp.int32)
    return own, peer & 127, peer >> 7


def peer_tables(read, dxs):
    tables = {}
    for dxi in dxs:
        base = read(dxi - 1)
        for dyi in range(3):
            tables[3 * dxi + dyi] = across(base, 1 - dyi)
    return tables


def pick_peer(tables, slot, frame):
    found = jnp.zeros(slot.shape, f32)
    for k, table in tables.items():
        found = jnp.where(frame == k, look_up(table, slot), found)
    return found


def one_column(contact, vel, denom, impulse, store_impulse, sums_ref, dxs):
    indices = [column_index(contact, t) for t in range(4)]
    closing = [contact(5, t) for t in range(4)]
    for c in range(3):
        tables = peer_tables(lambda j: vel(j, c), dxs)
        for t in range(4):
            own, slot, frame = indices[t]
            gap = pick_peer(tables, slot, frame) - look_up(vel(0, c), jnp.minimum(own, 127))
            closing[t] = closing[t] + contact(2 + c, t) * gap
    kicks = []
    for t in range(4):
        new = jnp.maximum(0.0, impulse(t) - 0.5 * closing[t] / denom(t))
        new = jnp.where(indices[t][0] < 128, new, 0.0)
        store_impulse(t, new)
        kicks.append([[p.astype(f32) for p in split3(new * contact(2 + c, t))] for c in range(3)])
    every = len(dxs) == 3
    height = 16 if every else 8
    frames_of = lax.broadcasted_iota(jnp.int32, (height, 512), 0) + 3 * dxs[0]
    nt = (((1,), (1,)), ((), ()))

    def line(parts, y):
        return jnp.concatenate([p[y : y + 1, :] for p in parts], axis=1)

    for y in range(8):
        hit = frames_of == line([indices[t][2] for t in range(4)], y)
        hot_peer = hot_rows(128, line([indices[t][1] for t in range(4)], y))
        rows = [
            line([kicks[t][c][piece] for t in range(4)], y) for piece in range(3) for c in range(3)
        ]
        terms = [jnp.where(hit, r, 0.0) for r in rows]
        if not every:
            terms.append(jnp.zeros((8, 512), f32))
        terms = jnp.concatenate(terms, axis=0).astype(bf16)
        found = lax.dot_general(terms, hot_peer, nt, preferred_element_type=f32)
        step = 3 * height
        sums_ref[y, 0:step] = found[0:step] + (found[step : 2 * step] + found[2 * step : 3 * step])
        if every:
            hot_own = hot_rows(128, line([indices[t][0] for t in range(4)], y))
            mine = jnp.concatenate(rows + [jnp.zeros((7, 512), f32)], axis=0).astype(bf16)
            mine = lax.dot_general(mine, hot_own, nt, preferred_element_type=f32)
            mine = mine[0:3] + (mine[3:6] + mine[6:9])
            for c in range(3):
                sums_ref[y, 16 * c + 9 : 16 * c + 10] = mine[c : c + 1]


def spread_kernel(mine_ref, low_ref, high_ref, out_ref):
    total = mine_ref[0:9] + (low_ref[...] + high_ref[...])
    for k in range(8):
        out_ref[k, 0:9] = total
        out_ref[k, 9:40] = mine_ref[9:40]


def free_kernel(place_ref, column_ref, force_ref, send_ref):
    y = place_ref[0]
    for r in range(24):
        send_ref[3 + r] = column_ref[:, 9 + r, :]
    mass = column_ref[:, 36, :]
    send_ref[27] = mass
    for c in range(3):
        total = None
        for dyi in range(3):
            row = across(column_ref[:, 3 * c + dyi, :], dyi - 1)
            total = row if total is None else total + row
        force_ref[0, c] = row_of(total, y)
        free = column_ref[:, 33 + c, :] + mass * total
        send_ref[c] = free


def reach(j):
    return ((2,), (0, 1, 2), (0,))[j]


def prep_kernel(mine_ref, low_ref, high_ref, contact_ref, mass_ref, denom_ref):
    for j, ref in enumerate((low_ref, mine_ref, high_ref)):
        contact_ref[j] = ref[3:27]
        mass_ref[j] = ref[27]
    for j in range(3):
        contact = lambda f, t: contact_ref[j, 4 * f + t]
        mass = lambda k: mass_ref[j + k]
        tables = peer_tables(mass, reach(j))
        for t in range(4):
            own, slot, frame = column_index(contact, t)
            denom_ref[j, t] = pick_peer(tables, slot, frame) + look_up(
                mass(0), jnp.minimum(own, 127)
            )


def row_of(v, y):
    hit = lax.broadcasted_iota(jnp.int32, (8, 128), 0) == y
    return jnp.sum(jnp.where(hit, v, 0.0), axis=0, keepdims=True)


def sweep_kernel(
    step, place_ref, vel_ref, low_ref, high_ref, free_ref, contact_ref, mass_ref, denom_ref, *refs
):
    before = refs[0] if step else None
    moved_ref, impulse_ref, sums, kick = refs[1 if step else 0 :]
    last = step == SWEEPS - 1
    y = place_ref[0]
    speeds = (low_ref, vel_ref, high_ref)

    def store(j, t, value):
        if not last:
            impulse_ref[j, t] = value
        elif j == 1:
            impulse_ref[0, :, 128 * t : 128 * t + 128] = row_of(value, y)

    for j in range(3):
        dxs = reach(j)
        one_column(
            lambda f, t: contact_ref[j, 4 * f + t],
            lambda k, c: speeds[j + k][c],
            lambda t: denom_ref[j, t],
            lambda t: before[j, t] if step else jnp.zeros((8, 128), f32),
            lambda t, v: store(j, t, v),
            sums.at[j],
            dxs,
        )
        rows = fold(sums.at[j], 16 if len(dxs) == 3 else 8, dxs)
        for c in range(3):
            if j == 1:
                kick[j, c] = rows[3 + c] - sums[j, :, 16 * c + 9, :]
            else:
                kick[j, c] = rows[c]
    for c in range(3):
        moved = free_ref[c] + mass_ref[1] * (kick[1, c] + (kick[0, c] + kick[2, c]))
        if last:
            moved_ref[0, c] = row_of(moved, y)
        else:
            moved_ref[c] = moved


def edge_kernel(xhi_ref, xlo_ref, ylow_ref, yhigh_ref, after_ref, to_low_ref, to_high_ref):
    size = 16
    last = size - 1
    for out_ref, face_ref, first, second in (
        (to_high_ref, xhi_ref, size + last, 2 * size + last),
        (to_low_ref, xlo_ref, 2 * size, size),
    ):
        out_ref[0:80] = face_ref[...]
        corners = [ylow_ref[first : first + 1], yhigh_ref[second : second + 1]]
        out_ref[80:88] = jnp.concatenate(corners + [jnp.zeros((6, 128), f32)], axis=0)


def vmem_call(kernel, outs, args, scratch=(), flops=1_000_000, place=None):
    specs = [pl.BlockSpec(memory_space=VMEM) for _ in args]
    if place is not None:
        args = (place,) + tuple(args)
        specs = [pl.BlockSpec(memory_space=pltpu.SMEM)] + specs
    return pl.pallas_call(
        kernel,
        in_specs=specs,
        out_specs=[pl.BlockSpec(memory_space=VMEM) for _ in outs],
        out_shape=[jax.ShapeDtypeStruct(s, f32) for s in outs],
        scratch_shapes=list(scratch),
        compiler_params=pltpu.CompilerParams(vmem_limit_bytes=24 << 20),
        cost_estimate=pl.CostEstimate(flops=flops, bytes_accessed=500_000, transcendentals=0),
        name=getattr(kernel, "func", kernel).__name__,
    )(*args)


def shift(value, axis, by):
    size = lax.axis_size(axis)
    return lax.ppermute(value, axis, [(i, (i + by) % size) for i in range(size)])


def both_ways(to_low, to_high, axis, by):
    return shift(to_high, axis, by), shift(to_low, axis, -by)


def per_device(
    populations,
    relax_matrix,
    grain_state,
    link_cell,
    link_dir,
    link_grain,
    contact_self,
    contact_peer,
    contact_normal,
    contact_gap,
):
    place = lax.axis_index("gy").astype(jnp.int32).reshape(1)
    links = (link_cell, link_dir, link_grain)
    contacts = (
        contact_self,
        contact_peer,
        contact_normal.transpose(0, 2, 1, 3),
        contact_gap,
        grain_state,
    )

    centre, table, yhi, ylo, xhi, xlo = collide(populations, relax_matrix)
    ylow, yhigh = both_ways(ylo, yhi, "gy", 1)
    first = interior_links(0, table, link_cell, link_dir)
    to_low, to_high = vmem_call(edge_kernel, [(88, 128)] * 2, (xhi, xlo, ylow, yhigh, first))
    xlow, xhigh = both_ways(to_low, to_high, "gx", 1)
    second = interior_links(1, table, link_cell, link_dir)
    halos = (xlow, xhigh, ylow, yhigh)
    mine, *ends = link_sums((first, second), links, halos, (xlo, xhi, ylo, yhi), contacts)
    populations_next = passed(centre, *halos)

    near = both_ways(*ends, "gx", 1)
    (spread,) = vmem_call(spread_kernel, [(8, 40, 128)], (mine, *near))
    column = lax.all_to_all(spread, "gy", 0, 0)
    force, mine = vmem_call(
        free_kernel, [(1, 3, 1, 128), (28, 8, 128)], (column,), place=place
    )

    near = both_ways(mine, mine, "gx", 1)
    static = vmem_call(
        prep_kernel, [(3, 24, 8, 128), (3, 8, 128), (3, 4, 8, 128)], (mine, *near)
    )
    scratch = [VMEM((3, 8, 48, 128), f32), VMEM((3, 3, 8, 128), f32)]
    moved, impulse = mine, ()
    for step in range(SWEEPS):
        last = step == SWEEPS - 1
        if step:
            near = both_ways(moved, moved, "gx", 1)
        moved, impulse = vmem_call(
            functools.partial(sweep_kernel, step),
            [(1, 3, 1, 128), (1, 1, 512)] if last else [(3, 8, 128), (3, 4, 8, 128)],
            (moved, *near, mine, *static) + ((impulse,) if step else ()),
            scratch,
            place=place,
        )
    velocity = moved
    return (
        populations_next,
        force.transpose(0, 2, 1, 3),
        velocity.transpose(0, 2, 1, 3),
        impulse,
    )


def solution(mesh):
    placed = (
        P(None, "gx", "gy", None),
        P(),
        P("gx", "gy", None, None),
        P("gx", "gy", None),
        P("gx", "gy", None),
        P("gx", "gy", None),
        P("gx", "gy", None),
        P("gx", "gy", None),
        P("gx", "gy", None, None),
        P("gx", "gy", None),
    )
    return jax.shard_map(
        per_device,
        mesh=mesh,
        in_specs=placed,
        out_specs=(
            P(None, "gx", "gy", None),
            P("gx", "gy", None, None),
            P("gx", "gy", None, None),
            P("gx", "gy", None),
        ),
        check_vma=False,
    )
```

```python
import functools

import jax
import jax.numpy as jnp
from jax import lax
from jax.experimental import pallas as pl
from jax.experimental.pallas import tpu as pltpu
from jax.sharding import PartitionSpec as P

SWEEPS = 4
DIRS = [
    [0, 0, 0],
    [1, 0, 0],
    [-1, 0, 0],
    [0, 1, 0],
    [0, -1, 0],
    [0, 0, 1],
    [0, 0, -1],
    [1, 1, 0],
    [-1, -1, 0],
    [1, -1, 0],
    [-1, 1, 0],
    [1, 0, 1],
    [-1, 0, -1],
    [1, 0, -1],
    [-1, 0, 1],
    [0, 1, 1],
    [0, -1, -1],
    [0, 1, -1],
    [0, -1, 1],
]
OPP = [0, 2, 1, 4, 3, 6, 5, 8, 7, 10, 9, 12, 11, 14, 13, 16, 15, 18, 17]
WEIGHT = [1.0 / 3.0] + [1.0 / 18.0] * 6 + [1.0 / 36.0] * 12
XP = [1, 7, 9, 11, 13]
XM = [2, 8, 10, 12, 14]
YP = [3, 7, 10, 15, 17]
YM = [4, 8, 9, 16, 18]
CANON = [1, 3, 5, 7, 9, 11, 14, 15, 18]
WALL = [6, 12, 13, 16, 17]
LOW = 32
highest = lax.Precision.HIGHEST
f32 = jnp.float32
bf16 = jnp.bfloat16
VMEM = pltpu.VMEM


def whole(shape):
    return pl.BlockSpec(shape, lambda *_: (0,) * len(shape))


def lanes_of(shape):
    return lax.broadcasted_iota(jnp.int32, shape, len(shape) - 1)


def split3(v):
    hi = v.astype(bf16)
    rest = v - hi.astype(f32)
    mid = rest.astype(bf16)
    low = (rest - mid.astype(f32)).astype(bf16)
    return hi, mid, low


PIECES = 4


def collide_kernel(
    relax_hbm, pop_hbm, centre_hbm, table_ref, yhi_ref, ylo_ref, xhi_ref, xlo_ref,
    relax, left, pop, pad, in_sem, out_sem,
):
    size_x, size_y = pop.shape[1], pop.shape[2]
    piece_x = size_x // PIECES

    def arriving(i):
        part = pl.ds(i * piece_x, piece_x)
        return pltpu.make_async_copy(pop_hbm.at[:, part], pop.at[:, part], in_sem.at[i])

    def leaving(i):
        part = pl.ds(i * piece_x, piece_x)
        inner = pl.ds(1 + i * piece_x, piece_x)
        return pltpu.make_async_copy(
            pad.at[:, inner, 8 : 8 + size_y], centre_hbm.at[:, part], out_sem.at[i]
        )

    matrix = pltpu.make_async_copy(relax_hbm, relax, in_sem.at[PIECES])
    matrix.start()
    for i in range(PIECES):
        arriving(i).start()
    zero = jnp.zeros((size_x + 2, 8, 128), f32)
    for q in YP + YM:
        pad[q, :, 0:8] = zero
        pad[q, :, 8 + size_y :] = zero
    for q in XP + XM:
        pad[q, 0] = jnp.zeros(pad.shape[2:], f32)
        pad[q, size_x + 1] = jnp.zeros(pad.shape[2:], f32)
    matrix.wait()
    hi = relax[...].astype(bf16)
    lo = (relax[...] - hi.astype(f32)).astype(bf16)
    row = lax.broadcasted_iota(jnp.int32, (160, 19), 0)
    rows_of = (row >> 3 == lanes_of((160, 19))).astype(f32).astype(bf16)
    col = lanes_of((19, 480))
    col = col - 160 * ((col >= 160).astype(jnp.int32) + (col >= 320).astype(jnp.int32))
    cols_of = (lax.broadcasted_iota(jnp.int32, (19, 480), 0) == col >> 3).astype(f32).astype(bf16)
    spread = []
    for part in (hi, lo):
        tall = jnp.dot(rows_of, part, preferred_element_type=f32).astype(bf16)
        spread.append(jnp.dot(tall, cols_of, preferred_element_type=f32))
    row = lax.broadcasted_iota(jnp.int32, (160, 480), 0)
    col = lanes_of((160, 480))
    value = jnp.where(col < 320, spread[0], spread[1])
    left[...] = jnp.where(row & 7 == col & 7, value, 0.0).astype(bf16)

    def one_row(x, carry):
        f = [pop[q, x] for q in range(19)]
        rho = f[0]
        for q in range(1, 19):
            rho = rho + f[q]
        speeds = []
        inverse = 1.0 / rho
        for axis in range(3):
            total = None
            for q in range(1, 19, 2):
                sign = DIRS[q][axis]
                if sign:
                    diff = f[q] - f[q + 1] if sign > 0 else f[q + 1] - f[q]
                    total = diff if total is None else total + diff
            speeds.append(total * inverse)
        ux, uy, uz = speeds
        base = 1.0 - 1.5 * (ux * ux + uy * uy + uz * uz)
        neq = [f[0] - WEIGHT[0] * rho * base]
        for q in range(1, 19, 2):
            along = None
            for axis in range(3):
                sign = DIRS[q][axis]
                if sign:
                    if along is None:
                        along = speeds[axis]
                    else:
                        along = along + speeds[axis] if sign > 0 else along - speeds[axis]
            scale = WEIGHT[q] * rho
            even = scale * (base + 4.5 * (along * along))
            odd = scale * (3.0 * along)
            neq.append(f[q] - (even + odd))
            neq.append(f[q + 1] - (even - odd))
        tall = [jnp.concatenate([v[:8], v[8:]], axis=1) for v in neq]
        tall = jnp.concatenate(tall + [jnp.zeros((8, 256), f32)], axis=0)
        hi = tall.astype(bf16)
        lo = (tall - hi.astype(f32)).astype(bf16)
        relaxed = jnp.dot(
            left[...], jnp.concatenate([hi, lo, hi], axis=0), preferred_element_type=f32
        )
        for q in range(19):
            change = relaxed[8 * q : 8 * q + 8]
            out = f[q] - jnp.concatenate([change[:, :128], change[:, 128:]], axis=0)
            pad[q, 1 + x, 8 : 8 + size_y] = out
        return carry

    def one_piece(i, carry):
        arriving(i).wait()
        lax.fori_loop(0, piece_x, lambda k, c: one_row(i * piece_x + k, c), 0, unroll=True)
        leaving(i).start()
        return carry

    lax.fori_loop(0, PIECES, one_piece, 0)
    for k in range(5):
        yhi_ref[k * size_x : (k + 1) * size_x] = pad[YP[k], 1 : 1 + size_x, 7 + size_y, :]
        ylo_ref[k * size_x : (k + 1) * size_x] = pad[YM[k], 1 : 1 + size_x, 8, :]
        xhi_ref[k * size_y : (k + 1) * size_y] = pad[XP[k], size_x, 8 : 8 + size_y, :]
        xlo_ref[k * size_y : (k + 1) * size_y] = pad[XM[k], 1, 8 : 8 + size_y, :]

    cells = size_x * size_y
    nt = (((1,), (1,)), ((), ()))

    def put(row, count, terms, chooser):
        hi = terms.astype(bf16)
        lo = (terms - hi.astype(f32)).astype(bf16)
        pair = lax.dot_general(chooser, hi, nt, preferred_element_type=f32)
        pair = pair + lax.dot_general(chooser, lo, nt, preferred_element_type=f32)
        hi = pair.astype(bf16)
        table_ref[row : row + count, 0:cells] = hi
        table_ref[row : row + count, cells:] = (pair - hi.astype(f32)).astype(bf16)

    for dz in range(2):
        row = lax.broadcasted_iota(jnp.int32, (LOW, 256), 0)
        col = lanes_of((LOW, 256))
        chooser = ((col == row) | (col == row + 128 + dz)).astype(f32).astype(bf16)
        for i, d in enumerate(CANON):
            dx, dy, climb = DIRS[d]
            if climb == dz:
                own = pad[d, 1 : 1 + size_x, 8 : 8 + size_y, :]
                other = pad[
                    OPP[d], 1 + dx : 1 + dx + size_x, 8 + dy : 8 + dy + size_y, :
                ]
                terms = [v.reshape(cells, 128) for v in (own, other)]
                put(LOW * i, LOW, jnp.concatenate(terms, axis=1), chooser)
    row = lax.broadcasted_iota(jnp.int32, (16, 640), 0)
    chooser = jnp.where(lanes_of((16, 640)) == 128 * row, 2.0, 0.0).astype(bf16)
    terms = [pad[d, 1 : 1 + size_x, 8 : 8 + size_y, :].reshape(cells, 128) for d in WALL]
    put(LOW * len(CANON), 16, jnp.concatenate(terms, axis=1), chooser)
    for i in range(PIECES):
        leaving(i).wait()


def collide(populations, relax_matrix):
    _, size_x, size_y, size_z = populations.shape
    face = jax.ShapeDtypeStruct((5 * size_y, size_z), f32)
    table = jax.ShapeDtypeStruct((LOW * len(CANON) + 16, 2 * size_x * size_y), bf16)
    return pl.pallas_call(
        collide_kernel,
        in_specs=[pl.BlockSpec(memory_space=pltpu.HBM)] * 2,
        out_specs=[pl.BlockSpec(memory_space=pltpu.HBM)] + [pl.BlockSpec(memory_space=VMEM)] * 5,
        out_shape=[jax.ShapeDtypeStruct(populations.shape, f32), table] + [face] * 4,
        scratch_shapes=[
            VMEM((19, 19), f32),
            VMEM((160, 480), bf16),
            VMEM(populations.shape, f32),
            VMEM((19, size_x + 2, size_y + 16, size_z), f32),
            pltpu.SemaphoreType.DMA((PIECES + 1,)),
            pltpu.SemaphoreType.DMA((PIECES,)),
        ],
        compiler_params=pltpu.CompilerParams(vmem_limit_bytes=51 << 20),
        cost_estimate=pl.CostEstimate(flops=40_000_000, bytes_accessed=6_000_000, transcendentals=0),
        name="collide",
    )(relax_matrix, populations)


CHUNK = 512


def hot_rows(count, line):
    shape = (16, line.shape[1])
    offset = jnp.broadcast_to(line, shape) - lax.broadcasted_iota(jnp.int32, shape, 0)
    offset = offset.astype(jnp.int16)
    one, zero = jnp.ones(shape, bf16), jnp.zeros(shape, bf16)
    return jnp.concatenate(
        [jnp.where(offset == jnp.int16(b), one, zero) for b in range(0, count, 16)], axis=0
    )


def pick(table_ref, column, entry):
    rows, depth = table_ref.shape[0], table_ref.shape[1] // 2
    chunk = column.shape[1]
    hot = hot_rows(depth, column)
    hot = jnp.concatenate([hot, hot], axis=0)
    offset = entry - lax.broadcasted_iota(jnp.int32, (8, chunk), 0)
    acc = jnp.zeros((8, chunk), f32)
    found = jnp.dot(table_ref[...], hot, preferred_element_type=f32)
    for j in range(0, rows, 8):
        acc = jnp.where(offset == j, found[j : j + 8], acc)
    return jnp.sum(acc, axis=0, keepdims=True)


def member(direction, dirs, first=1, step=1):
    out = jnp.zeros(direction.shape, jnp.int32)
    for k, d in enumerate(dirs):
        out = jnp.where(direction == d, first + step * k, out)
    return out


def sides(direction):
    return (
        member(direction, XP),
        member(direction, XM),
        member(direction, YP),
        member(direction, YM),
    )


def tile_of(ref, k):
    start = pl.multiple_of(k * 1024, 1024)
    return jnp.concatenate(
        [ref[0, :, pl.ds(start + 128 * s, 128)] for s in range(8)], axis=0
    )


def line_of(ref, i):
    return jnp.concatenate([ref[pl.ds(4 * i + k, 1), :] for k in range(4)], axis=1)


def link_kernel(half, table_ref, cell_ref, dir_ref, value_ref, column, entry):
    def index(k, carry):
        cell, direction = tile_of(cell_ref, 8 * half + k), tile_of(dir_ref, 8 * half + k)
        xup, xdown, yup, ydown = sides(direction)
        forward = member(direction, CANON)
        backward = member(direction, [OPP[d] for d in CANON])
        wall = member(direction, WALL)
        back = (backward > 0).astype(jnp.int32)
        x = (cell >> 11) + back * ((xup > 0).astype(jnp.int32) - (xdown > 0).astype(jnp.int32))
        y = ((cell >> 7) & 15) + back * (
            (yup > 0).astype(jnp.int32) - (ydown > 0).astype(jnp.int32)
        )
        z = cell & 31
        bottom = (wall > 0) & (z == 0)
        z = z - (wall > 0).astype(jnp.int32)
        which = forward + backward - 1
        inside = (x >= 0) & (x < 16) & (y >= 0) & (y < 16) & (which >= 0)
        rows = pl.ds(pl.multiple_of(k * 8, 8), 8)
        column[rows, :] = jnp.where(bottom, cell >> 7, x * 16 + y)
        entry[rows, :] = jnp.where(bottom, 287 + wall, jnp.where(inside, which * 32 + z, -8))
        return carry

    lax.fori_loop(0, 8, index, 0)

    def one_chunk(i, carry):
        found = pick(table_ref, line_of(column, i), line_of(entry, i))
        for k in range(4):
            value_ref[pl.ds(4 * i + k, 1), :] = found[:, 128 * k : 128 * k + 128]
        return carry

    lax.fori_loop(0, 16, one_chunk, 0, unroll=True)


def interior_links(half, table, cells, dirs):
    shape = (64, 128)
    return pl.pallas_call(
        functools.partial(link_kernel, half),
        in_specs=[pl.BlockSpec(memory_space=VMEM)] * 3,
        out_specs=pl.BlockSpec(memory_space=VMEM),
        out_shape=jax.ShapeDtypeStruct(shape, f32),
        scratch_shapes=[VMEM(shape, jnp.int32)] * 2,
        compiler_params=pltpu.CompilerParams(vmem_limit_bytes=24 << 20),
        cost_estimate=pl.CostEstimate(
            flops=6_000_000_000, bytes_accessed=1_000_000, transcendentals=0
        ),
        name="interior_links",
    )(table, cells, dirs)


def scatter_kernel(
    first_ref, second_ref, cell_ref, dir_ref, grain_ref,
    xlow_ref, xhigh_ref, ylow_ref, yhigh_ref,
    ownx_low_ref, ownx_high_ref, owny_low_ref, owny_high_ref,
    self_ref, peer_ref, normal_ref, gap_ref, state_ref,
    mine_ref, to_low_ref, to_high_ref,
    table, column, entry, frames, slots, signs,
):
    size = 16
    lane = lanes_of((size, 128))
    for side in range(2):
        for group in range(3):
            acc = jnp.zeros((size, 128), f32)
            for j in range(4 * group, min(4 * group + 4, 10)):
                d = (XP + XM)[j] if side == 0 else (YP + YM)[j]
                q = OPP[d]
                dx, dy, dz = DIRS[d]
                high = j < 5
                if side == 0:
                    along = dy
                    ref = xhigh_ref if high else xlow_ref
                    mine = ownx_high_ref if high else ownx_low_ref
                    k = (XM if high else XP).index(q)
                    ends = ref[5 * size : 5 * size + 1], ref[5 * size + 1 : 5 * size + 2]
                else:
                    along = dx
                    ref = yhigh_ref if high else ylow_ref
                    mine = owny_high_ref if high else owny_low_ref
                    k = (YM if high else YP).index(q)
                    ends = (jnp.zeros((1, 128), f32),) * 2
                face = ref[k * size : (k + 1) * size]
                if along == 1:
                    face = jnp.concatenate([face[1:], ends[1]], axis=0)
                elif along == -1:
                    face = jnp.concatenate([ends[0], face[:-1]], axis=0)
                if dz:
                    face = pltpu.roll(face, (-dz) % 128, 1)
                if d not in CANON:
                    face = face + mine[(j % 5) * size : (j % 5 + 1) * size]
                if dz == -1:
                    face = jnp.where(lane == 0, 0.0, face)
                shift = (j % 4) * LOW
                if shift:
                    face = pltpu.roll(face, shift, 1)
                acc = jnp.where((lane >= shift) & (lane < shift + LOW), face, acc)
            hi = acc.astype(bf16)
            lo = (acc - hi.astype(f32)).astype(bf16)
            row = 16 * (3 * side + group)
            table[row : row + 16, 0:128] = hi
            table[row : row + 16, 128:256] = lo

    def index(k, carry):
        cell, direction, grain = tile_of(cell_ref, k), tile_of(dir_ref, k), tile_of(grain_ref, k)
        xup, xdown, yup, ydown = sides(direction)
        zup = member(direction, [5, 11, 14, 15, 18], 1, 0)
        zdown = member(direction, WALL, 1, 0)
        x, y, z = cell >> 11, (cell >> 7) & 15, cell & 31
        jx = jnp.where(
            (x == 15) & (xup > 0), xup, jnp.where((x == 0) & (xdown > 0), xdown + 5, 0)
        )
        jy = jnp.where(
            (y == 15) & (yup > 0), yup, jnp.where((y == 0) & (ydown > 0), ydown + 5, 0)
        )
        which = jnp.where(jx > 0, jx, jy) - 1
        rows = pl.ds(pl.multiple_of(k * 8, 8), 8)
        column[rows, :] = (which & 3) * 32 + z
        place = (which >> 2) * 16 + jnp.where(jx > 0, y, 48 + x)
        entry[rows, :] = jnp.where(which >= 0, place, -8)
        frames[rows, :] = grain >> 7
        slots[rows, :] = grain & 127
        for c, (up, down) in enumerate(((xup, xdown), (yup, ydown), (zup, zdown))):
            signs[c, rows, :] = (up > 0).astype(f32) - (down > 0).astype(f32)
        return carry

    lax.fori_loop(0, 16, index, 0)
    frames_of = lax.broadcasted_iota(jnp.int32, (16, CHUNK), 0)

    def one_chunk(value_ref, before, k, acc):
        i = before + k
        value = line_of(value_ref, k) + pick(table, line_of(column, i), line_of(entry, i))
        hit = frames_of == line_of(frames, i)
        sign = [line_of(signs.at[c], i) for c in range(3)]
        terms = []
        for part in split3(value):
            part = part.astype(f32)
            for c in range(3):
                terms.append(jnp.where(hit, part * sign[c], 0.0).astype(bf16))
        hot = hot_rows(128, line_of(slots, i))
        return acc + lax.dot_general(
            jnp.concatenate(terms, axis=0), hot, (((1,), (1,)), ((), ())), preferred_element_type=f32
        )

    acc = jnp.zeros((144, 128), f32)
    for before, value_ref in ((0, first_ref), (16, second_ref)):
        acc = lax.fori_loop(
            0, 16, functools.partial(one_chunk, value_ref, before), acc, unroll=True
        )
    total = acc[0:48] + (acc[48:96] + acc[96:144])
    for ref, dxi in ((to_low_ref, 0), (mine_ref, 1), (to_high_ref, 2)):
        parts = [total[16 * c + 3 * dxi : 16 * c + 3 * dxi + 3] for c in range(3)]
        ref[0:9] = jnp.concatenate(parts, axis=0)
    rows = []
    for ref in (self_ref, peer_ref):
        rows += [ref[0, :, 128 * t : 128 * t + 128].astype(f32) for t in range(4)]
    for c in range(3):
        rows += [normal_ref[0, c, :, 128 * t : 128 * t + 128] for t in range(4)]
    rows += [gap_ref[0, :, 128 * t : 128 * t + 128] for t in range(4)]
    rows += [state_ref[0, 0]]
    mine_ref[9:37] = jnp.concatenate(rows, axis=0)
    mine_ref[37:40] = jnp.zeros((3, 128), f32)


def link_sums(values, links, halos, faces, contacts):
    args = values + links + halos + faces + contacts
    square = (128, 128)
    return pl.pallas_call(
        scatter_kernel,
        in_specs=[pl.BlockSpec(memory_space=VMEM)] * len(args),
        out_specs=[pl.BlockSpec(memory_space=VMEM)] * 3,
        out_shape=[jax.ShapeDtypeStruct((n, 128), f32) for n in (40, 9, 9)],
        scratch_shapes=[VMEM((96, 256), bf16)]
        + [VMEM(square, jnp.int32)] * 4
        + [VMEM((3,) + square, f32)],
        compiler_params=pltpu.CompilerParams(vmem_limit_bytes=24 << 20),
        cost_estimate=pl.CostEstimate(
            flops=2_000_000_000, bytes_accessed=500_000, transcendentals=0
        ),
        name="link_sums",
    )(*args)


def stream_kernel(centre_ref, xlow_ref, xhigh_ref, ylow_ref, yhigh_ref, out_ref, pad):
    step = pl.program_id(0)
    block_x = out_ref.shape[1]
    size_x, size_y = centre_ref.shape[1], centre_ref.shape[2]

    @pl.when(step == 0)
    def _():
        for q in range(19):
            pad[q, 1 : 1 + size_x, 8 : 8 + size_y] = centre_ref[q]
        for k in range(5):
            pad[YP[k], 1 : 1 + size_x, 7, :] = ylow_ref[k * size_x : (k + 1) * size_x]
            pad[YM[k], 1 : 1 + size_x, 8 + size_y, :] = yhigh_ref[k * size_x : (k + 1) * size_x]
            pad[XP[k], 0, 8 : 8 + size_y, :] = xlow_ref[k * size_y : (k + 1) * size_y]
            pad[XM[k], 1 + size_x, 8 : 8 + size_y, :] = xhigh_ref[k * size_y : (k + 1) * size_y]
        base = 5 * size_y
        for q, row in ((7, 7), (9, 8 + size_y)):
            pad[q, 0, row : row + 1, :] = xlow_ref[base + (row > 8) : base + (row > 8) + 1]
        for q, row in ((10, 7), (8, 8 + size_y)):
            pad[q, 1 + size_x, row : row + 1, :] = xhigh_ref[base + (row > 8) : base + (row > 8) + 1]

    lane = lanes_of((size_y, 128))

    def one_row(i, carry):
        x = step * block_x + i
        for q in range(19):
            dx, dy, dz = DIRS[q]
            moved = pad[q, 1 + x - dx, 8 - dy : 8 - dy + size_y, :]
            if dz:
                moved = pltpu.roll(moved, dz % 128, 1)
                wall = 0 if dz == 1 else 127
                moved = jnp.where(lane == wall, pad[OPP[q], 1 + x, 8 : 8 + size_y, :], moved)
            out_ref[q, i] = moved
        return carry

    lax.fori_loop(0, block_x, one_row, 0)


def passed(centre, xlow, xhigh, ylow, yhigh):
    _, size_x, size_y, size_z = centre.shape
    block_x = 4
    return pl.pallas_call(
        stream_kernel,
        grid=(size_x // block_x,),
        in_specs=[whole(a.shape) for a in (centre, xlow, xhigh, ylow, yhigh)],
        out_specs=pl.BlockSpec((19, block_x, size_y, size_z), lambda i: (0, i, 0, 0)),
        out_shape=jax.ShapeDtypeStruct(centre.shape, f32),
        scratch_shapes=[VMEM((19, size_x + 2, size_y + 16, size_z), f32)],
        compiler_params=pltpu.CompilerParams(vmem_limit_bytes=40 << 20),
        cost_estimate=pl.CostEstimate(flops=10_000_000, bytes_accessed=6_000_000, transcendentals=0),
        name="passed",
    )(centre, xlow, xhigh, ylow, yhigh)


def across(v, by):
    return pltpu.roll(v, by % 8, 0) if by % 8 else v


def look_up(table, index):
    return jnp.take_along_axis(table, index, axis=1)


def fold(sums_ref, stride, dxs):
    out = []
    for k in range(len(dxs)):
        for c in range(3):
            total = None
            for dyi in range(3):
                row = sums_ref[:, c * stride + 3 * k + dyi, :]
                row = across(row, dyi - 1)
                total = row if total is None else total + row
            out.append(total)
    return out


def column_index(contact, t):
    own = contact(0, t).astype(jnp.int32)
    peer = contact(1, t).astype(jnp.int32)
    return own, peer & 127, peer >> 7


def peer_tables(read, dxs):
    tables = {}
    for dxi in dxs:
        base = read(dxi - 1)
        for dyi in range(3):
            tables[3 * dxi + dyi] = across(base, 1 - dyi)
    return tables


def pick_peer(tables, slot, frame):
    found = jnp.zeros(slot.shape, f32)
    for k, table in tables.items():
        found = jnp.where(frame == k, look_up(table, slot), found)
    return found


def one_column(contact, vel, denom, impulse, store_impulse, sums_ref, dxs):
    indices = [column_index(contact, t) for t in range(4)]
    closing = [contact(5, t) for t in range(4)]
    for c in range(3):
        tables = peer_tables(lambda j: vel(j, c), dxs)
        for t in range(4):
            own, slot, frame = indices[t]
            gap = pick_peer(tables, slot, frame) - look_up(vel(0, c), jnp.minimum(own, 127))
            closing[t] = closing[t] + contact(2 + c, t) * gap
    kicks = []
    for t in range(4):
        new = jnp.maximum(0.0, impulse(t) - 0.5 * closing[t] / denom(t))
        new = jnp.where(indices[t][0] < 128, new, 0.0)
        store_impulse(t, new)
        kicks.append([[p.astype(f32) for p in split3(new * contact(2 + c, t))] for c in range(3)])
    every = len(dxs) == 3
    height = 16 if every else 8
    frames_of = lax.broadcasted_iota(jnp.int32, (height, 512), 0) + 3 * dxs[0]
    nt = (((1,), (1,)), ((), ()))

    def line(parts, y):
        return jnp.concatenate([p[y : y + 1, :] for p in parts], axis=1)

    for y in range(8):
        hit = frames_of == line([indices[t][2] for t in range(4)], y)
        hot_peer = hot_rows(128, line([indices[t][1] for t in range(4)], y))
        rows = [
            line([kicks[t][c][piece] for t in range(4)], y) for piece in range(3) for c in range(3)
        ]
        terms = [jnp.where(hit, r, 0.0) for r in rows]
        if not every:
            terms.append(jnp.zeros((8, 512), f32))
        terms = jnp.concatenate(terms, axis=0).astype(bf16)
        found = lax.dot_general(terms, hot_peer, nt, preferred_element_type=f32)
        step = 3 * height
        sums_ref[y, 0:step] = found[0:step] + (found[step : 2 * step] + found[2 * step : 3 * step])
        if every:
            hot_own = hot_rows(128, line([indices[t][0] for t in range(4)], y))
            mine = jnp.concatenate(rows + [jnp.zeros((7, 512), f32)], axis=0).astype(bf16)
            mine = lax.dot_general(mine, hot_own, nt, preferred_element_type=f32)
            mine = mine[0:3] + (mine[3:6] + mine[6:9])
            for c in range(3):
                sums_ref[y, 16 * c + 9 : 16 * c + 10] = mine[c : c + 1]


def spread_kernel(mine_ref, low_ref, high_ref, out_ref):
    total = mine_ref[0:9] + (low_ref[...] + high_ref[...])
    for k in range(8):
        out_ref[k, 0:9] = total
        out_ref[k, 9:40] = mine_ref[9:40]


def free_kernel(place_ref, column_ref, force_ref, send_ref):
    y = place_ref[0]
    for r in range(24):
        send_ref[3 + r] = column_ref[:, 9 + r, :]
    mass = column_ref[:, 36, :]
    send_ref[27] = mass
    for c in range(3):
        total = None
        for dyi in range(3):
            row = across(column_ref[:, 3 * c + dyi, :], dyi - 1)
            total = row if total is None else total + row
        force_ref[0, c] = row_of(total, y)
        free = column_ref[:, 33 + c, :] + mass * total
        send_ref[c] = free


def reach(j):
    return ((2,), (0, 1, 2), (0,))[j]


def prep_kernel(mine_ref, low_ref, high_ref, contact_ref, mass_ref, denom_ref):
    for j, ref in enumerate((low_ref, mine_ref, high_ref)):
        contact_ref[j] = ref[3:27]
        mass_ref[j] = ref[27]
    for j in range(3):
        contact = lambda f, t: contact_ref[j, 4 * f + t]
        mass = lambda k: mass_ref[j + k]
        tables = peer_tables(mass, reach(j))
        for t in range(4):
            own, slot, frame = column_index(contact, t)
            denom_ref[j, t] = pick_peer(tables, slot, frame) + look_up(
                mass(0), jnp.minimum(own, 127)
            )


def row_of(v, y):
    hit = lax.broadcasted_iota(jnp.int32, (8, 128), 0) == y
    return jnp.sum(jnp.where(hit, v, 0.0), axis=0, keepdims=True)


def sweep_kernel(
    step, place_ref, vel_ref, low_ref, high_ref, free_ref, contact_ref, mass_ref, denom_ref, *refs
):
    before = refs[0] if step else None
    moved_ref, impulse_ref, sums, kick = refs[1 if step else 0 :]
    last = step == SWEEPS - 1
    y = place_ref[0]
    speeds = (low_ref, vel_ref, high_ref)

    def store(j, t, value):
        if not last:
            impulse_ref[j, t] = value
        elif j == 1:
            impulse_ref[0, :, 128 * t : 128 * t + 128] = row_of(value, y)

    for j in range(3):
        dxs = reach(j)
        one_column(
            lambda f, t: contact_ref[j, 4 * f + t],
            lambda k, c: speeds[j + k][c],
            lambda t: denom_ref[j, t],
            lambda t: before[j, t] if step else jnp.zeros((8, 128), f32),
            lambda t, v: store(j, t, v),
            sums.at[j],
            dxs,
        )
        rows = fold(sums.at[j], 16 if len(dxs) == 3 else 8, dxs)
        for c in range(3):
            if j == 1:
                kick[j, c] = rows[3 + c] - sums[j, :, 16 * c + 9, :]
            else:
                kick[j, c] = rows[c]
    for c in range(3):
        moved = free_ref[c] + mass_ref[1] * (kick[1, c] + (kick[0, c] + kick[2, c]))
        if last:
            moved_ref[0, c] = row_of(moved, y)
        else:
            moved_ref[c] = moved


def edge_kernel(xhi_ref, xlo_ref, ylow_ref, yhigh_ref, after_ref, to_low_ref, to_high_ref):
    size = 16
    last = size - 1
    for out_ref, face_ref, first, second in (
        (to_high_ref, xhi_ref, size + last, 2 * size + last),
        (to_low_ref, xlo_ref, 2 * size, size),
    ):
        out_ref[0:80] = face_ref[...]
        corners = [ylow_ref[first : first + 1], yhigh_ref[second : second + 1]]
        out_ref[80:88] = jnp.concatenate(corners + [jnp.zeros((6, 128), f32)], axis=0)


def vmem_call(kernel, outs, args, scratch=(), flops=1_000_000, place=None):
    specs = [pl.BlockSpec(memory_space=VMEM) for _ in args]
    if place is not None:
        args = (place,) + tuple(args)
        specs = [pl.BlockSpec(memory_space=pltpu.SMEM)] + specs
    return pl.pallas_call(
        kernel,
        in_specs=specs,
        out_specs=[pl.BlockSpec(memory_space=VMEM) for _ in outs],
        out_shape=[jax.ShapeDtypeStruct(s, f32) for s in outs],
        scratch_shapes=list(scratch),
        compiler_params=pltpu.CompilerParams(vmem_limit_bytes=24 << 20),
        cost_estimate=pl.CostEstimate(flops=flops, bytes_accessed=500_000, transcendentals=0),
        name=getattr(kernel, "func", kernel).__name__,
    )(*args)


def shift(value, axis, by):
    size = lax.axis_size(axis)
    return lax.ppermute(value, axis, [(i, (i + by) % size) for i in range(size)])


def both_ways(to_low, to_high, axis, by):
    return shift(to_high, axis, by), shift(to_low, axis, -by)


def per_device(
    populations,
    relax_matrix,
    grain_state,
    link_cell,
    link_dir,
    link_grain,
    contact_self,
    contact_peer,
    contact_normal,
    contact_gap,
):
    place = lax.axis_index("gy").astype(jnp.int32).reshape(1)
    links = (link_cell, link_dir, link_grain)
    contacts = (
        contact_self,
        contact_peer,
        contact_normal.transpose(0, 2, 1, 3),
        contact_gap,
        grain_state,
    )

    centre, table, yhi, ylo, xhi, xlo = collide(populations, relax_matrix)
    ylow, yhigh = both_ways(ylo, yhi, "gy", 1)
    first = interior_links(0, table, link_cell, link_dir)
    to_low, to_high = vmem_call(edge_kernel, [(88, 128)] * 2, (xhi, xlo, ylow, yhigh, first))
    xlow, xhigh = both_ways(to_low, to_high, "gx", 1)
    second = interior_links(1, table, link_cell, link_dir)
    halos = (xlow, xhigh, ylow, yhigh)
    mine, *ends = link_sums((first, second), links, halos, (xlo, xhi, ylo, yhi), contacts)
    populations_next = passed(centre, *halos)

    near = both_ways(*ends, "gx", 1)
    (spread,) = vmem_call(spread_kernel, [(8, 40, 128)], (mine, *near))
    column = lax.all_to_all(spread, "gy", 0, 0)
    force, mine = vmem_call(
        free_kernel, [(1, 3, 1, 128), (28, 8, 128)], (column,), place=place
    )

    near = both_ways(mine, mine, "gx", 1)
    static = vmem_call(
        prep_kernel, [(3, 24, 8, 128), (3, 8, 128), (3, 4, 8, 128)], (mine, *near)
    )
    scratch = [VMEM((3, 8, 48, 128), f32), VMEM((3, 3, 8, 128), f32)]
    moved, impulse = mine, ()
    for step in range(SWEEPS):
        last = step == SWEEPS - 1
        if step:
            near = both_ways(moved, moved, "gx", 1)
        moved, impulse = vmem_call(
            functools.partial(sweep_kernel, step),
            [(1, 3, 1, 128), (1, 1, 512)] if last else [(3, 8, 128), (3, 4, 8, 128)],
            (moved, *near, mine, *static) + ((impulse,) if step else ()),
            scratch,
            place=place,
        )
    velocity = moved
    return (
        populations_next,
        force.transpose(0, 2, 1, 3),
        velocity.transpose(0, 2, 1, 3),
        impulse,
    )


def solution(mesh):
    placed = (
        P(None, "gx", "gy", None),
        P(),
        P("gx", "gy", None, None),
        P("gx", "gy", None),
        P("gx", "gy", None),
        P("gx", "gy", None),
        P("gx", "gy", None),
        P("gx", "gy", None),
        P("gx", "gy", None, None),
        P("gx", "gy", None),
    )
    return jax.shard_map(
        per_device,
        mesh=mesh,
        in_specs=placed,
        out_specs=(
            P(None, "gx", "gy", None),
            P("gx", "gy", None, None),
            P("gx", "gy", None, None),
            P("gx", "gy", None),
        ),
        check_vma=False,
    )
```

```python
import functools

import jax
import jax.numpy as jnp
from jax import lax
from jax.experimental import pallas as pl
from jax.experimental.pallas import tpu as pltpu
from jax.sharding import PartitionSpec as P

SWEEPS = 4
DIRS = [
    [0, 0, 0],
    [1, 0, 0],
    [-1, 0, 0],
    [0, 1, 0],
    [0, -1, 0],
    [0, 0, 1],
    [0, 0, -1],
    [1, 1, 0],
    [-1, -1, 0],
    [1, -1, 0],
    [-1, 1, 0],
    [1, 0, 1],
    [-1, 0, -1],
    [1, 0, -1],
    [-1, 0, 1],
    [0, 1, 1],
    [0, -1, -1],
    [0, 1, -1],
    [0, -1, 1],
]
OPP = [0, 2, 1, 4, 3, 6, 5, 8, 7, 10, 9, 12, 11, 14, 13, 16, 15, 18, 17]
WEIGHT = [1.0 / 3.0] + [1.0 / 18.0] * 6 + [1.0 / 36.0] * 12
XP = [1, 7, 9, 11, 13]
XM = [2, 8, 10, 12, 14]
YP = [3, 7, 10, 15, 17]
YM = [4, 8, 9, 16, 18]
CANON = [1, 3, 5, 7, 9, 11, 14, 15, 18]
WALL = [6, 12, 13, 16, 17]
LOW = 32
highest = lax.Precision.HIGHEST
f32 = jnp.float32
bf16 = jnp.bfloat16
VMEM = pltpu.VMEM


def whole(shape):
    return pl.BlockSpec(shape, lambda *_: (0,) * len(shape))


def lanes_of(shape):
    return lax.broadcasted_iota(jnp.int32, shape, len(shape) - 1)


def split3(v):
    hi = v.astype(bf16)
    rest = v - hi.astype(f32)
    mid = rest.astype(bf16)
    low = (rest - mid.astype(f32)).astype(bf16)
    return hi, mid, low


PIECES = 4


def collide_kernel(
    relax_hbm, pop_hbm, centre_hbm, table_ref, yhi_ref, ylo_ref, xhi_ref, xlo_ref,
    relax, left, pop, pad, in_sem, out_sem,
):
    size_x, size_y = pop.shape[1], pop.shape[2]
    piece_x = size_x // PIECES

    def arriving(i):
        part = pl.ds(i * piece_x, piece_x)
        return pltpu.make_async_copy(pop_hbm.at[:, part], pop.at[:, part], in_sem.at[i])

    def leaving(i):
        part = pl.ds(i * piece_x, piece_x)
        inner = pl.ds(1 + i * piece_x, piece_x)
        return pltpu.make_async_copy(
            pad.at[:, inner, 8 : 8 + size_y], centre_hbm.at[:, part], out_sem.at[i]
        )

    matrix = pltpu.make_async_copy(relax_hbm, relax, in_sem.at[PIECES])
    matrix.start()
    for i in range(PIECES):
        arriving(i).start()
    zero = jnp.zeros((size_x + 2, 8, 128), f32)
    for q in YP + YM:
        pad[q, :, 0:8] = zero
        pad[q, :, 8 + size_y :] = zero
    for q in XP + XM:
        pad[q, 0] = jnp.zeros(pad.shape[2:], f32)
        pad[q, size_x + 1] = jnp.zeros(pad.shape[2:], f32)
    matrix.wait()
    hi = relax[...].astype(bf16)
    lo = (relax[...] - hi.astype(f32)).astype(bf16)
    row = lax.broadcasted_iota(jnp.int32, (160, 19), 0)
    rows_of = (row >> 3 == lanes_of((160, 19))).astype(f32).astype(bf16)
    col = lanes_of((19, 480))
    col = col - 160 * ((col >= 160).astype(jnp.int32) + (col >= 320).astype(jnp.int32))
    cols_of = (lax.broadcasted_iota(jnp.int32, (19, 480), 0) == col >> 3).astype(f32).astype(bf16)
    spread = []
    for part in (hi, lo):
        tall = jnp.dot(rows_of, part, preferred_element_type=f32).astype(bf16)
        spread.append(jnp.dot(tall, cols_of, preferred_element_type=f32))
    row = lax.broadcasted_iota(jnp.int32, (160, 480), 0)
    col = lanes_of((160, 480))
    value = jnp.where(col < 320, spread[0], spread[1])
    left[...] = jnp.where(row & 7 == col & 7, value, 0.0).astype(bf16)

    def one_row(x, carry):
        f = [pop[q, x] for q in range(19)]
        rho = f[0]
        for q in range(1, 19):
            rho = rho + f[q]
        speeds = []
        inverse = 1.0 / rho
        for axis in range(3):
            total = None
            for q in range(1, 19, 2):
                sign = DIRS[q][axis]
                if sign:
                    diff = f[q] - f[q + 1] if sign > 0 else f[q + 1] - f[q]
                    total = diff if total is None else total + diff
            speeds.append(total * inverse)
        ux, uy, uz = speeds
        base = 1.0 - 1.5 * (ux * ux + uy * uy + uz * uz)
        neq = [f[0] - WEIGHT[0] * rho * base]
        for q in range(1, 19, 2):
            along = None
            for axis in range(3):
                sign = DIRS[q][axis]
                if sign:
                    if along is None:
                        along = speeds[axis]
                    else:
                        along = along + speeds[axis] if sign > 0 else along - speeds[axis]
            scale = WEIGHT[q] * rho
            even = scale * (base + 4.5 * (along * along))
            odd = scale * (3.0 * along)
            neq.append(f[q] - (even + odd))
            neq.append(f[q + 1] - (even - odd))
        tall = [jnp.concatenate([v[:8], v[8:]], axis=1) for v in neq]
        tall = jnp.concatenate(tall + [jnp.zeros((8, 256), f32)], axis=0)
        hi = tall.astype(bf16)
        lo = (tall - hi.astype(f32)).astype(bf16)
        relaxed = jnp.dot(
            left[...], jnp.concatenate([hi, lo, hi], axis=0), preferred_element_type=f32
        )
        for q in range(19):
            change = relaxed[8 * q : 8 * q + 8]
            out = f[q] - jnp.concatenate([change[:, :128], change[:, 128:]], axis=0)
            pad[q, 1 + x, 8 : 8 + size_y] = out
        return carry

    def one_piece(i, carry):
        arriving(i).wait()
        lax.fori_loop(0, piece_x, lambda k, c: one_row(i * piece_x + k, c), 0, unroll=True)
        leaving(i).start()
        return carry

    lax.fori_loop(0, PIECES, one_piece, 0)
    for k in range(5):
        yhi_ref[k * size_x : (k + 1) * size_x] = pad[YP[k], 1 : 1 + size_x, 7 + size_y, :]
        ylo_ref[k * size_x : (k + 1) * size_x] = pad[YM[k], 1 : 1 + size_x, 8, :]
        xhi_ref[k * size_y : (k + 1) * size_y] = pad[XP[k], size_x, 8 : 8 + size_y, :]
        xlo_ref[k * size_y : (k + 1) * size_y] = pad[XM[k], 1, 8 : 8 + size_y, :]

    cells = size_x * size_y
    nt = (((1,), (1,)), ((), ()))

    def put(row, count, terms, chooser):
        hi = terms.astype(bf16)
        lo = (terms - hi.astype(f32)).astype(bf16)
        pair = lax.dot_general(chooser, hi, nt, preferred_element_type=f32)
        pair = pair + lax.dot_general(chooser, lo, nt, preferred_element_type=f32)
        hi = pair.astype(bf16)
        table_ref[row : row + count, 0:cells] = hi
        table_ref[row : row + count, cells:] = (pair - hi.astype(f32)).astype(bf16)

    for dz in range(2):
        row = lax.broadcasted_iota(jnp.int32, (LOW, 256), 0)
        col = lanes_of((LOW, 256))
        chooser = ((col == row) | (col == row + 128 + dz)).astype(f32).astype(bf16)
        for i, d in enumerate(CANON):
            dx, dy, climb = DIRS[d]
            if climb == dz:
                own = pad[d, 1 : 1 + size_x, 8 : 8 + size_y, :]
                other = pad[
                    OPP[d], 1 + dx : 1 + dx + size_x, 8 + dy : 8 + dy + size_y, :
                ]
                terms = [v.reshape(cells, 128) for v in (own, other)]
                put(LOW * i, LOW, jnp.concatenate(terms, axis=1), chooser)
    row = lax.broadcasted_iota(jnp.int32, (16, 640), 0)
    chooser = jnp.where(lanes_of((16, 640)) == 128 * row, 2.0, 0.0).astype(bf16)
    terms = [pad[d, 1 : 1 + size_x, 8 : 8 + size_y, :].reshape(cells, 128) for d in WALL]
    put(LOW * len(CANON), 16, jnp.concatenate(terms, axis=1), chooser)
    for i in range(PIECES):
        leaving(i).wait()


def collide(populations, relax_matrix):
    _, size_x, size_y, size_z = populations.shape
    face = jax.ShapeDtypeStruct((5 * size_y, size_z), f32)
    table = jax.ShapeDtypeStruct((LOW * len(CANON) + 16, 2 * size_x * size_y), bf16)
    return pl.pallas_call(
        collide_kernel,
        in_specs=[pl.BlockSpec(memory_space=pltpu.HBM)] * 2,
        out_specs=[pl.BlockSpec(memory_space=pltpu.HBM)] + [pl.BlockSpec(memory_space=VMEM)] * 5,
        out_shape=[jax.ShapeDtypeStruct(populations.shape, f32), table] + [face] * 4,
        scratch_shapes=[
            VMEM((19, 19), f32),
            VMEM((160, 480), bf16),
            VMEM(populations.shape, f32),
            VMEM((19, size_x + 2, size_y + 16, size_z), f32),
            pltpu.SemaphoreType.DMA((PIECES + 1,)),
            pltpu.SemaphoreType.DMA((PIECES,)),
        ],
        compiler_params=pltpu.CompilerParams(vmem_limit_bytes=51 << 20),
        cost_estimate=pl.CostEstimate(flops=40_000_000, bytes_accessed=6_000_000, transcendentals=0),
        name="collide",
    )(relax_matrix, populations)


CHUNK = 512


def hot_rows(count, line):
    shape = (16, line.shape[1])
    offset = jnp.broadcast_to(line, shape) - lax.broadcasted_iota(jnp.int32, shape, 0)
    offset = offset.astype(jnp.int16)
    one, zero = jnp.ones(shape, bf16), jnp.zeros(shape, bf16)
    return jnp.concatenate(
        [jnp.where(offset == jnp.int16(b), one, zero) for b in range(0, count, 16)], axis=0
    )


def pick(table_ref, column, entry):
    rows, depth = table_ref.shape[0], table_ref.shape[1] // 2
    chunk = column.shape[1]
    hot = hot_rows(depth, column)
    hot = jnp.concatenate([hot, hot], axis=0)
    offset = entry - lax.broadcasted_iota(jnp.int32, (8, chunk), 0)
    acc = jnp.zeros((8, chunk), f32)
    found = jnp.dot(table_ref[...], hot, preferred_element_type=f32)
    for j in range(0, rows, 8):
        acc = jnp.where(offset == j, found[j : j + 8], acc)
    return jnp.sum(acc, axis=0, keepdims=True)


def member(direction, dirs, first=1, step=1):
    out = jnp.zeros(direction.shape, jnp.int32)
    for k, d in enumerate(dirs):
        out = jnp.where(direction == d, first + step * k, out)
    return out


def sides(direction):
    return (
        member(direction, XP),
        member(direction, XM),
        member(direction, YP),
        member(direction, YM),
    )


def tile_of(ref, k):
    start = pl.multiple_of(k * 1024, 1024)
    return jnp.concatenate(
        [ref[0, :, pl.ds(start + 128 * s, 128)] for s in range(8)], axis=0
    )


def line_of(ref, i):
    return jnp.concatenate([ref[pl.ds(4 * i + k, 1), :] for k in range(4)], axis=1)


def link_kernel(half, table_ref, cell_ref, dir_ref, value_ref, column, entry):
    def index(k, carry):
        cell, direction = tile_of(cell_ref, 8 * half + k), tile_of(dir_ref, 8 * half + k)
        xup, xdown, yup, ydown = sides(direction)
        forward = member(direction, CANON)
        backward = member(direction, [OPP[d] for d in CANON])
        wall = member(direction, WALL)
        back = (backward > 0).astype(jnp.int32)
        x = (cell >> 11) + back * ((xup > 0).astype(jnp.int32) - (xdown > 0).astype(jnp.int32))
        y = ((cell >> 7) & 15) + back * (
            (yup > 0).astype(jnp.int32) - (ydown > 0).astype(jnp.int32)
        )
        z = cell & 31
        bottom = (wall > 0) & (z == 0)
        z = z - (wall > 0).astype(jnp.int32)
        which = forward + backward - 1
        inside = (x >= 0) & (x < 16) & (y >= 0) & (y < 16) & (which >= 0)
        rows = pl.ds(pl.multiple_of(k * 8, 8), 8)
        column[rows, :] = jnp.where(bottom, cell >> 7, x * 16 + y)
        entry[rows, :] = jnp.where(bottom, 287 + wall, jnp.where(inside, which * 32 + z, -8))
        return carry

    lax.fori_loop(0, 8, index, 0)

    def one_chunk(i, carry):
        found = pick(table_ref, line_of(column, i), line_of(entry, i))
        for k in range(4):
            value_ref[pl.ds(4 * i + k, 1), :] = found[:, 128 * k : 128 * k + 128]
        return carry

    lax.fori_loop(0, 16, one_chunk, 0, unroll=True)


def interior_links(half, table, cells, dirs):
    shape = (64, 128)
    return pl.pallas_call(
        functools.partial(link_kernel, half),
        in_specs=[pl.BlockSpec(memory_space=VMEM)] * 3,
        out_specs=pl.BlockSpec(memory_space=VMEM),
        out_shape=jax.ShapeDtypeStruct(shape, f32),
        scratch_shapes=[VMEM(shape, jnp.int32)] * 2,
        compiler_params=pltpu.CompilerParams(vmem_limit_bytes=24 << 20),
        cost_estimate=pl.CostEstimate(
            flops=6_000_000_000, bytes_accessed=1_000_000, transcendentals=0
        ),
        name="interior_links",
    )(table, cells, dirs)


def scatter_kernel(
    first_ref, second_ref, cell_ref, dir_ref, grain_ref,
    xlow_ref, xhigh_ref, ylow_ref, yhigh_ref,
    ownx_low_ref, ownx_high_ref, owny_low_ref, owny_high_ref,
    self_ref, peer_ref, normal_ref, gap_ref, state_ref,
    out_ref,
    table, column, entry, frames, slots, signs,
):
    size = 16
    lane = lanes_of((size, 128))
    for side in range(2):
        for group in range(3):
            acc = jnp.zeros((size, 128), f32)
            for j in range(4 * group, min(4 * group + 4, 10)):
                d = (XP + XM)[j] if side == 0 else (YP + YM)[j]
                q = OPP[d]
                dx, dy, dz = DIRS[d]
                high = j < 5
                if side == 0:
                    along = dy
                    ref = xhigh_ref if high else xlow_ref
                    mine = ownx_high_ref if high else ownx_low_ref
                    k = (XM if high else XP).index(q)
                    ends = ref[5 * size : 5 * size + 1], ref[5 * size + 1 : 5 * size + 2]
                else:
                    along = dx
                    ref = yhigh_ref if high else ylow_ref
                    mine = owny_high_ref if high else owny_low_ref
                    k = (YM if high else YP).index(q)
                    ends = (jnp.zeros((1, 128), f32),) * 2
                face = ref[k * size : (k + 1) * size]
                if along == 1:
                    face = jnp.concatenate([face[1:], ends[1]], axis=0)
                elif along == -1:
                    face = jnp.concatenate([ends[0], face[:-1]], axis=0)
                if dz:
                    face = pltpu.roll(face, (-dz) % 128, 1)
                if d not in CANON:
                    face = face + mine[(j % 5) * size : (j % 5 + 1) * size]
                if dz == -1:
                    face = jnp.where(lane == 0, 0.0, face)
                shift = (j % 4) * LOW
                if shift:
                    face = pltpu.roll(face, shift, 1)
                acc = jnp.where((lane >= shift) & (lane < shift + LOW), face, acc)
            hi = acc.astype(bf16)
            lo = (acc - hi.astype(f32)).astype(bf16)
            row = 16 * (3 * side + group)
            table[row : row + 16, 0:128] = hi
            table[row : row + 16, 128:256] = lo

    def index(k, carry):
        cell, direction, grain = tile_of(cell_ref, k), tile_of(dir_ref, k), tile_of(grain_ref, k)
        xup, xdown, yup, ydown = sides(direction)
        zup = member(direction, [5, 11, 14, 15, 18], 1, 0)
        zdown = member(direction, WALL, 1, 0)
        x, y, z = cell >> 11, (cell >> 7) & 15, cell & 31
        jx = jnp.where(
            (x == 15) & (xup > 0), xup, jnp.where((x == 0) & (xdown > 0), xdown + 5, 0)
        )
        jy = jnp.where(
            (y == 15) & (yup > 0), yup, jnp.where((y == 0) & (ydown > 0), ydown + 5, 0)
        )
        which = jnp.where(jx > 0, jx, jy) - 1
        rows = pl.ds(pl.multiple_of(k * 8, 8), 8)
        column[rows, :] = (which & 3) * 32 + z
        place = (which >> 2) * 16 + jnp.where(jx > 0, y, 48 + x)
        entry[rows, :] = jnp.where(which >= 0, place, -8)
        frames[rows, :] = grain >> 7
        slots[rows, :] = grain & 127
        for c, (up, down) in enumerate(((xup, xdown), (yup, ydown), (zup, zdown))):
            signs[c, rows, :] = (up > 0).astype(f32) - (down > 0).astype(f32)
        return carry

    lax.fori_loop(0, 16, index, 0)
    row = lax.broadcasted_iota(jnp.int32, (32, CHUNK), 0)
    group = (row >= 9).astype(jnp.int32) + (row >= 18).astype(jnp.int32)
    frames_of = jnp.where(row < 27, row - 9 * group, -1)

    def one_chunk(value_ref, before, k, acc):
        i = before + k
        value = line_of(value_ref, k) + pick(table, line_of(column, i), line_of(entry, i))
        hit = frames_of == line_of(frames, i)
        sign = [line_of(signs.at[c], i) for c in range(3)]
        sign = jnp.where(group == 0, sign[0], jnp.where(group == 1, sign[1], sign[2]))
        sign = jnp.where(hit, sign, 0.0)
        terms = [(sign * part.astype(f32)).astype(bf16) for part in split3(value)]
        hot = hot_rows(128, line_of(slots, i))
        return acc + lax.dot_general(
            jnp.concatenate(terms, axis=0), hot, (((1,), (1,)), ((), ())), preferred_element_type=f32
        )

    acc = jnp.zeros((96, 128), f32)
    for before, value_ref in ((0, first_ref), (16, second_ref)):
        acc = lax.fori_loop(
            0, 16, functools.partial(one_chunk, value_ref, before), acc, unroll=True
        )
    rows = [acc[0:32] + (acc[32:64] + acc[64:96])]
    for ref in (self_ref, peer_ref):
        rows += [ref[0, :, 128 * t : 128 * t + 128].astype(f32) for t in range(4)]
    for c in range(3):
        rows += [normal_ref[0, c, :, 128 * t : 128 * t + 128] for t in range(4)]
    rows += [gap_ref[0, :, 128 * t : 128 * t + 128] for t in range(4)]
    rows += [state_ref[0, 0], jnp.zeros((4, 128), f32)]
    message = jnp.concatenate(rows, axis=0)
    for k in range(8):
        out_ref[k] = message


def link_sums(values, links, halos, faces, contacts):
    args = values + links + halos + faces + contacts
    square = (128, 128)
    return pl.pallas_call(
        scatter_kernel,
        in_specs=[pl.BlockSpec(memory_space=VMEM)] * len(args),
        out_specs=pl.BlockSpec(memory_space=VMEM),
        out_shape=jax.ShapeDtypeStruct((8, 64, 128), f32),
        scratch_shapes=[VMEM((96, 256), bf16)]
        + [VMEM(square, jnp.int32)] * 4
        + [VMEM((3,) + square, f32)],
        compiler_params=pltpu.CompilerParams(vmem_limit_bytes=24 << 20),
        cost_estimate=pl.CostEstimate(
            flops=2_000_000_000, bytes_accessed=500_000, transcendentals=0
        ),
        name="link_sums",
    )(*args)


def stream_kernel(centre_ref, xlow_ref, xhigh_ref, ylow_ref, yhigh_ref, out_ref, pad):
    step = pl.program_id(0)
    block_x = out_ref.shape[1]
    size_x, size_y = centre_ref.shape[1], centre_ref.shape[2]

    @pl.when(step == 0)
    def _():
        for q in range(19):
            pad[q, 1 : 1 + size_x, 8 : 8 + size_y] = centre_ref[q]
        for k in range(5):
            pad[YP[k], 1 : 1 + size_x, 7, :] = ylow_ref[k * size_x : (k + 1) * size_x]
            pad[YM[k], 1 : 1 + size_x, 8 + size_y, :] = yhigh_ref[k * size_x : (k + 1) * size_x]
            pad[XP[k], 0, 8 : 8 + size_y, :] = xlow_ref[k * size_y : (k + 1) * size_y]
            pad[XM[k], 1 + size_x, 8 : 8 + size_y, :] = xhigh_ref[k * size_y : (k + 1) * size_y]
        base = 5 * size_y
        for q, row in ((7, 7), (9, 8 + size_y)):
            pad[q, 0, row : row + 1, :] = xlow_ref[base + (row > 8) : base + (row > 8) + 1]
        for q, row in ((10, 7), (8, 8 + size_y)):
            pad[q, 1 + size_x, row : row + 1, :] = xhigh_ref[base + (row > 8) : base + (row > 8) + 1]

    lane = lanes_of((size_y, 128))

    def one_row(i, carry):
        x = step * block_x + i
        for q in range(19):
            dx, dy, dz = DIRS[q]
            moved = pad[q, 1 + x - dx, 8 - dy : 8 - dy + size_y, :]
            if dz:
                moved = pltpu.roll(moved, dz % 128, 1)
                wall = 0 if dz == 1 else 127
                moved = jnp.where(lane == wall, pad[OPP[q], 1 + x, 8 : 8 + size_y, :], moved)
            out_ref[q, i] = moved
        return carry

    lax.fori_loop(0, block_x, one_row, 0, unroll=True)


def passed(centre, xlow, xhigh, ylow, yhigh):
    _, size_x, size_y, size_z = centre.shape
    block_x = 8
    return pl.pallas_call(
        stream_kernel,
        grid=(size_x // block_x,),
        in_specs=[whole(a.shape) for a in (centre, xlow, xhigh, ylow, yhigh)],
        out_specs=pl.BlockSpec((19, block_x, size_y, size_z), lambda i: (0, i, 0, 0)),
        out_shape=jax.ShapeDtypeStruct(centre.shape, f32),
        scratch_shapes=[VMEM((19, size_x + 2, size_y + 16, size_z), f32)],
        compiler_params=pltpu.CompilerParams(vmem_limit_bytes=40 << 20),
        cost_estimate=pl.CostEstimate(flops=10_000_000, bytes_accessed=6_000_000, transcendentals=0),
        name="passed",
    )(centre, xlow, xhigh, ylow, yhigh)


def across(v, by):
    return pltpu.roll(v, by % 8, 0) if by % 8 else v


def look_up(table, index):
    return jnp.take_along_axis(table, index, axis=1)


def fold(sums_ref, stride, dxs):
    out = []
    for k in range(len(dxs)):
        for c in range(3):
            total = None
            for dyi in range(3):
                row = sums_ref[:, c * stride + 3 * k + dyi, :]
                row = across(row, dyi - 1)
                total = row if total is None else total + row
            out.append(total)
    return out


def column_index(contact, t):
    own = contact(0, t).astype(jnp.int32)
    peer = contact(1, t).astype(jnp.int32)
    return own, peer & 127, peer >> 7


def peer_tables(read, dxs):
    tables = {}
    for dxi in dxs:
        base = read(dxi - 1)
        for dyi in range(3):
            tables[3 * dxi + dyi] = across(base, 1 - dyi)
    return tables


def pick_peer(tables, slot, frame):
    found = jnp.zeros(slot.shape, f32)
    for k, table in tables.items():
        found = jnp.where(frame == k, look_up(table, slot), found)
    return found


def one_column(contact, vel, denom, impulse, store_impulse, sums_ref, dxs):
    indices = [column_index(contact, t) for t in range(4)]
    closing = [contact(5, t) for t in range(4)]
    for c in range(3):
        tables = peer_tables(lambda j: vel(j, c), dxs)
        for t in range(4):
            own, slot, frame = indices[t]
            gap = pick_peer(tables, slot, frame) - look_up(vel(0, c), jnp.minimum(own, 127))
            closing[t] = closing[t] + contact(2 + c, t) * gap
    kicks = []
    for t in range(4):
        new = jnp.maximum(0.0, impulse(t) - 0.5 * closing[t] / denom(t))
        new = jnp.where(indices[t][0] < 128, new, 0.0)
        store_impulse(t, new)
        kicks.append([[p.astype(f32) for p in split3(new * contact(2 + c, t))] for c in range(3)])
    every = len(dxs) == 3
    height = 16 if every else 8
    frames_of = lax.broadcasted_iota(jnp.int32, (height, 512), 0) + 3 * dxs[0]
    nt = (((1,), (1,)), ((), ()))

    def line(parts, y):
        return jnp.concatenate([p[y : y + 1, :] for p in parts], axis=1)

    for y in range(8):
        hit = frames_of == line([indices[t][2] for t in range(4)], y)
        hot_peer = hot_rows(128, line([indices[t][1] for t in range(4)], y))
        rows = [
            line([kicks[t][c][piece] for t in range(4)], y) for piece in range(3) for c in range(3)
        ]
        terms = [jnp.where(hit, r, 0.0) for r in rows]
        if not every:
            terms.append(jnp.zeros((8, 512), f32))
        terms = jnp.concatenate(terms, axis=0).astype(bf16)
        found = lax.dot_general(terms, hot_peer, nt, preferred_element_type=f32)
        step = 3 * height
        sums_ref[y, 0:step] = found[0:step] + (found[step : 2 * step] + found[2 * step : 3 * step])
        if every:
            hot_own = hot_rows(128, line([indices[t][0] for t in range(4)], y))
            mine = jnp.concatenate(rows + [jnp.zeros((7, 512), f32)], axis=0).astype(bf16)
            mine = lax.dot_general(mine, hot_own, nt, preferred_element_type=f32)
            mine = mine[0:3] + (mine[3:6] + mine[6:9])
            for c in range(3):
                sums_ref[y, 16 * c + 9 : 16 * c + 10] = mine[c : c + 1]


def fold_kernel(frames_ref, mine_ref, to_low_ref, to_high_ref):
    force = fold(frames_ref, 9, (0, 1, 2))
    for c in range(3):
        to_low_ref[c] = force[c]
        mine_ref[c] = force[3 + c]
        to_high_ref[c] = force[6 + c]
    for r in range(28):
        row = frames_ref[:, 32 + r, :]
        mine_ref[3 + r] = row
        if r < 24 or r == 27:
            k = 3 + min(r, 24)
            to_low_ref[k] = row
            to_high_ref[k] = row


def reach(j):
    return ((2,), (0, 1, 2), (0,))[j]


def prep_kernel(mine_ref, low_ref, high_ref, contact_ref, mass_ref, denom_ref):
    for j, ref in enumerate((low_ref, mine_ref, high_ref)):
        contact_ref[j] = ref[3:27]
        mass_ref[j] = ref[ref.shape[0] - 1]
    for j in range(3):
        contact = lambda f, t: contact_ref[j, 4 * f + t]
        mass = lambda k: mass_ref[j + k]
        tables = peer_tables(mass, reach(j))
        for t in range(4):
            own, slot, frame = column_index(contact, t)
            denom_ref[j, t] = pick_peer(tables, slot, frame) + look_up(
                mass(0), jnp.minimum(own, 127)
            )


def row_of(v, y):
    hit = lax.broadcasted_iota(jnp.int32, (8, 128), 0) == y
    return jnp.sum(jnp.where(hit, v, 0.0), axis=0, keepdims=True)


def free_kernel(place_ref, mine_ref, low_ref, high_ref, force_ref, free_ref):
    y = place_ref[0]
    for c in range(3):
        total = mine_ref[c] + (low_ref[c] + high_ref[c])
        force_ref[0, c] = row_of(total, y)
        free_ref[c] = mine_ref[27 + c] + mine_ref[30] * total


def sweep_kernel(
    step, place_ref, vel_ref, low_ref, high_ref, free_ref, contact_ref, mass_ref, denom_ref, *refs
):
    before = refs[0] if step else None
    moved_ref, impulse_ref, sums, kick = refs[1 if step else 0 :]
    last = step == SWEEPS - 1
    y = place_ref[0]
    speeds = (low_ref, vel_ref, high_ref)

    def store(j, t, value):
        if not last:
            impulse_ref[j, t] = value
        elif j == 1:
            impulse_ref[0, :, 128 * t : 128 * t + 128] = row_of(value, y)

    for j in range(3):
        dxs = reach(j)
        one_column(
            lambda f, t: contact_ref[j, 4 * f + t],
            lambda k, c: speeds[j + k][c],
            lambda t: denom_ref[j, t],
            lambda t: before[j, t] if step else jnp.zeros((8, 128), f32),
            lambda t, v: store(j, t, v),
            sums.at[j],
            dxs,
        )
        rows = fold(sums.at[j], 16 if len(dxs) == 3 else 8, dxs)
        for c in range(3):
            if j == 1:
                kick[j, c] = rows[3 + c] - sums[j, :, 16 * c + 9, :]
            else:
                kick[j, c] = rows[c]
    for c in range(3):
        moved = free_ref[c] + mass_ref[1] * (kick[1, c] + (kick[0, c] + kick[2, c]))
        if last:
            moved_ref[0, c] = row_of(moved, y)
        else:
            moved_ref[c] = moved


def edge_kernel(xhi_ref, xlo_ref, ylow_ref, yhigh_ref, after_ref, to_low_ref, to_high_ref):
    size = 16
    last = size - 1
    for out_ref, face_ref, first, second in (
        (to_high_ref, xhi_ref, size + last, 2 * size + last),
        (to_low_ref, xlo_ref, 2 * size, size),
    ):
        out_ref[0:80] = face_ref[...]
        corners = [ylow_ref[first : first + 1], yhigh_ref[second : second + 1]]
        out_ref[80:88] = jnp.concatenate(corners + [jnp.zeros((6, 128), f32)], axis=0)


def vmem_call(kernel, outs, args, scratch=(), flops=1_000_000, place=None):
    specs = [pl.BlockSpec(memory_space=VMEM) for _ in args]
    if place is not None:
        args = (place,) + tuple(args)
        specs = [pl.BlockSpec(memory_space=pltpu.SMEM)] + specs
    return pl.pallas_call(
        kernel,
        in_specs=specs,
        out_specs=[pl.BlockSpec(memory_space=VMEM) for _ in outs],
        out_shape=[jax.ShapeDtypeStruct(s, f32) for s in outs],
        scratch_shapes=list(scratch),
        compiler_params=pltpu.CompilerParams(vmem_limit_bytes=24 << 20),
        cost_estimate=pl.CostEstimate(flops=flops, bytes_accessed=500_000, transcendentals=0),
        name=getattr(kernel, "func", kernel).__name__,
    )(*args)


def shift(value, axis, by):
    size = lax.axis_size(axis)
    return lax.ppermute(value, axis, [(i, (i + by) % size) for i in range(size)])


def both_ways(to_low, to_high, axis, by):
    return shift(to_high, axis, by), shift(to_low, axis, -by)


def per_device(
    populations,
    relax_matrix,
    grain_state,
    link_cell,
    link_dir,
    link_grain,
    contact_self,
    contact_peer,
    contact_normal,
    contact_gap,
):
    place = lax.axis_index("gy").astype(jnp.int32).reshape(1)
    links = (link_cell, link_dir, link_grain)
    contacts = (
        contact_self,
        contact_peer,
        contact_normal.transpose(0, 2, 1, 3),
        contact_gap,
        grain_state,
    )

    centre, table, yhi, ylo, xhi, xlo = collide(populations, relax_matrix)
    ylow, yhigh = both_ways(ylo, yhi, "gy", 1)
    first = interior_links(0, table, link_cell, link_dir)
    to_low, to_high = vmem_call(edge_kernel, [(88, 128)] * 2, (xhi, xlo, ylow, yhigh, first))
    xlow, xhigh = both_ways(to_low, to_high, "gx", 1)
    second = interior_links(1, table, link_cell, link_dir)
    halos = (xlow, xhigh, ylow, yhigh)
    spread = link_sums((first, second), links, halos, (xlo, xhi, ylo, yhi), contacts)
    populations_next = passed(centre, *halos)

    spread = lax.all_to_all(spread, "gy", 0, 0)
    mine, *ends = vmem_call(
        fold_kernel, [(31, 8, 128), (28, 8, 128), (28, 8, 128)], (spread,)
    )
    near = both_ways(*ends, "gx", 1)
    force, free = vmem_call(
        free_kernel, [(1, 3, 1, 128), (3, 8, 128)], (mine, *near), place=place
    )

    static = vmem_call(
        prep_kernel, [(3, 24, 8, 128), (3, 8, 128), (3, 4, 8, 128)], (mine, *near)
    )
    scratch = [VMEM((3, 8, 48, 128), f32), VMEM((3, 3, 8, 128), f32)]
    moved, impulse = free, ()
    for step in range(SWEEPS):
        last = step == SWEEPS - 1
        moved, impulse = vmem_call(
            functools.partial(sweep_kernel, step),
            [(1, 3, 1, 128), (1, 1, 512)] if last else [(3, 8, 128), (3, 4, 8, 128)],
            (moved, *both_ways(moved, moved, "gx", 1), free, *static)
            + ((impulse,) if step else ()),
            scratch,
            place=place,
        )
    velocity = moved
    return (
        populations_next,
        force.transpose(0, 2, 1, 3),
        velocity.transpose(0, 2, 1, 3),
        impulse,
    )


def solution(mesh):
    placed = (
        P(None, "gx", "gy", None),
        P(),
        P("gx", "gy", None, None),
        P("gx", "gy", None),
        P("gx", "gy", None),
        P("gx", "gy", None),
        P("gx", "gy", None),
        P("gx", "gy", None),
        P("gx", "gy", None, None),
        P("gx", "gy", None),
    )
    return jax.shard_map(
        per_device,
        mesh=mesh,
        in_specs=placed,
        out_specs=(
            P(None, "gx", "gy", None),
            P("gx", "gy", None, None),
            P("gx", "gy", None, None),
            P("gx", "gy", None),
        ),
        check_vma=False,
    )
```

```python
import functools

import jax
import jax.numpy as jnp
from jax import lax
from jax.experimental import pallas as pl
from jax.experimental.pallas import tpu as pltpu
from jax.sharding import PartitionSpec as P

SWEEPS = 4
DIRS = [
    [0, 0, 0],
    [1, 0, 0],
    [-1, 0, 0],
    [0, 1, 0],
    [0, -1, 0],
    [0, 0, 1],
    [0, 0, -1],
    [1, 1, 0],
    [-1, -1, 0],
    [1, -1, 0],
    [-1, 1, 0],
    [1, 0, 1],
    [-1, 0, -1],
    [1, 0, -1],
    [-1, 0, 1],
    [0, 1, 1],
    [0, -1, -1],
    [0, 1, -1],
    [0, -1, 1],
]
OPP = [0, 2, 1, 4, 3, 6, 5, 8, 7, 10, 9, 12, 11, 14, 13, 16, 15, 18, 17]
WEIGHT = [1.0 / 3.0] + [1.0 / 18.0] * 6 + [1.0 / 36.0] * 12
XP = [1, 7, 9, 11, 13]
XM = [2, 8, 10, 12, 14]
YP = [3, 7, 10, 15, 17]
YM = [4, 8, 9, 16, 18]
CANON = [1, 3, 5, 7, 9, 11, 14, 15, 18]
WALL = [6, 12, 13, 16, 17]
LOW = 32
highest = lax.Precision.HIGHEST
f32 = jnp.float32
bf16 = jnp.bfloat16
VMEM = pltpu.VMEM


def whole(shape):
    return pl.BlockSpec(shape, lambda *_: (0,) * len(shape))


def lanes_of(shape):
    return lax.broadcasted_iota(jnp.int32, shape, len(shape) - 1)


def split3(v):
    hi = v.astype(bf16)
    rest = v - hi.astype(f32)
    mid = rest.astype(bf16)
    low = (rest - mid.astype(f32)).astype(bf16)
    return hi, mid, low


PIECES = 2


def collide_kernel(
    relax_hbm, pop_hbm, centre_hbm, table_ref, yhi_ref, ylo_ref, xhi_ref, xlo_ref,
    relax, left, pop, pad, in_sem, out_sem,
):
    size_x, size_y = pop.shape[1], pop.shape[2]
    piece_x = size_x // PIECES

    def arriving(i):
        part = pl.ds(i * piece_x, piece_x)
        return pltpu.make_async_copy(pop_hbm.at[:, part], pop.at[:, part], in_sem.at[i])

    def leaving(i):
        part = pl.ds(i * piece_x, piece_x)
        inner = pl.ds(1 + i * piece_x, piece_x)
        return pltpu.make_async_copy(
            pad.at[:, inner, 8 : 8 + size_y], centre_hbm.at[:, part], out_sem.at[i]
        )

    matrix = pltpu.make_async_copy(relax_hbm, relax, in_sem.at[PIECES])
    matrix.start()
    for i in range(PIECES):
        arriving(i).start()
    zero = jnp.zeros((size_x + 2, 8, 128), f32)
    for q in YP + YM:
        pad[q, :, 0:8] = zero
        pad[q, :, 8 + size_y :] = zero
    for q in XP + XM:
        pad[q, 0] = jnp.zeros(pad.shape[2:], f32)
        pad[q, size_x + 1] = jnp.zeros(pad.shape[2:], f32)
    matrix.wait()
    hi = relax[...].astype(bf16)
    lo = (relax[...] - hi.astype(f32)).astype(bf16)
    row = lax.broadcasted_iota(jnp.int32, (160, 19), 0)
    rows_of = (row >> 3 == lanes_of((160, 19))).astype(f32).astype(bf16)
    col = lanes_of((19, 480))
    col = col - 160 * ((col >= 160).astype(jnp.int32) + (col >= 320).astype(jnp.int32))
    cols_of = (lax.broadcasted_iota(jnp.int32, (19, 480), 0) == col >> 3).astype(f32).astype(bf16)
    spread = []
    for part in (hi, lo):
        tall = jnp.dot(rows_of, part, preferred_element_type=f32).astype(bf16)
        spread.append(jnp.dot(tall, cols_of, preferred_element_type=f32))
    row = lax.broadcasted_iota(jnp.int32, (160, 480), 0)
    col = lanes_of((160, 480))
    value = jnp.where(col < 320, spread[0], spread[1])
    left[...] = jnp.where(row & 7 == col & 7, value, 0.0).astype(bf16)

    def one_row(x, carry):
        f = [pop[q, x] for q in range(19)]
        rho = f[0]
        for q in range(1, 19):
            rho = rho + f[q]
        speeds = []
        inverse = 1.0 / rho
        for axis in range(3):
            total = None
            for q in range(1, 19, 2):
                sign = DIRS[q][axis]
                if sign:
                    diff = f[q] - f[q + 1] if sign > 0 else f[q + 1] - f[q]
                    total = diff if total is None else total + diff
            speeds.append(total * inverse)
        ux, uy, uz = speeds
        base = 1.0 - 1.5 * (ux * ux + uy * uy + uz * uz)
        neq = [f[0] - WEIGHT[0] * rho * base]
        for q in range(1, 19, 2):
            along = None
            for axis in range(3):
                sign = DIRS[q][axis]
                if sign:
                    if along is None:
                        along = speeds[axis]
                    else:
                        along = along + speeds[axis] if sign > 0 else along - speeds[axis]
            scale = WEIGHT[q] * rho
            even = scale * (base + 4.5 * (along * along))
            odd = scale * (3.0 * along)
            neq.append(f[q] - (even + odd))
            neq.append(f[q + 1] - (even - odd))
        tall = [jnp.concatenate([v[:8], v[8:]], axis=1) for v in neq]
        tall = jnp.concatenate(tall + [jnp.zeros((8, 256), f32)], axis=0)
        hi = tall.astype(bf16)
        lo = (tall - hi.astype(f32)).astype(bf16)
        relaxed = jnp.dot(
            left[...], jnp.concatenate([hi, lo, hi], axis=0), preferred_element_type=f32
        )
        for q in range(19):
            change = relaxed[8 * q : 8 * q + 8]
            out = f[q] - jnp.concatenate([change[:, :128], change[:, 128:]], axis=0)
            pad[q, 1 + x, 8 : 8 + size_y] = out
        return carry

    def one_piece(i, carry):
        arriving(i).wait()
        lax.fori_loop(0, piece_x, lambda k, c: one_row(i * piece_x + k, c), 0, unroll=True)
        leaving(i).start()
        return carry

    lax.fori_loop(0, PIECES, one_piece, 0)
    for k in range(5):
        yhi_ref[k * size_x : (k + 1) * size_x] = pad[YP[k], 1 : 1 + size_x, 7 + size_y, :]
        ylo_ref[k * size_x : (k + 1) * size_x] = pad[YM[k], 1 : 1 + size_x, 8, :]
        xhi_ref[k * size_y : (k + 1) * size_y] = pad[XP[k], size_x, 8 : 8 + size_y, :]
        xlo_ref[k * size_y : (k + 1) * size_y] = pad[XM[k], 1, 8 : 8 + size_y, :]

    cells = size_x * size_y
    nt = (((1,), (1,)), ((), ()))

    def put(row, count, terms, chooser):
        hi = terms.astype(bf16)
        lo = (terms - hi.astype(f32)).astype(bf16)
        pair = lax.dot_general(chooser, hi, nt, preferred_element_type=f32)
        pair = pair + lax.dot_general(chooser, lo, nt, preferred_element_type=f32)
        hi = pair.astype(bf16)
        table_ref[row : row + count, 0:cells] = hi
        table_ref[row : row + count, cells:] = (pair - hi.astype(f32)).astype(bf16)

    for dz in range(2):
        row = lax.broadcasted_iota(jnp.int32, (LOW, 256), 0)
        col = lanes_of((LOW, 256))
        chooser = ((col == row) | (col == row + 128 + dz)).astype(f32).astype(bf16)
        for i, d in enumerate(CANON):
            dx, dy, climb = DIRS[d]
            if climb == dz:
                own = pad[d, 1 : 1 + size_x, 8 : 8 + size_y, :]
                other = pad[
                    OPP[d], 1 + dx : 1 + dx + size_x, 8 + dy : 8 + dy + size_y, :
                ]
                terms = [v.reshape(cells, 128) for v in (own, other)]
                put(LOW * i, LOW, jnp.concatenate(terms, axis=1), chooser)
    row = lax.broadcasted_iota(jnp.int32, (16, 640), 0)
    chooser = jnp.where(lanes_of((16, 640)) == 128 * row, 2.0, 0.0).astype(bf16)
    terms = [pad[d, 1 : 1 + size_x, 8 : 8 + size_y, :].reshape(cells, 128) for d in WALL]
    put(LOW * len(CANON), 16, jnp.concatenate(terms, axis=1), chooser)
    for i in range(PIECES):
        leaving(i).wait()


def collide(populations, relax_matrix):
    _, size_x, size_y, size_z = populations.shape
    face = jax.ShapeDtypeStruct((5 * size_y, size_z), f32)
    table = jax.ShapeDtypeStruct((LOW * len(CANON) + 16, 2 * size_x * size_y), bf16)
    return pl.pallas_call(
        collide_kernel,
        in_specs=[pl.BlockSpec(memory_space=pltpu.HBM)] * 2,
        out_specs=[pl.BlockSpec(memory_space=pltpu.HBM)] + [pl.BlockSpec(memory_space=VMEM)] * 5,
        out_shape=[jax.ShapeDtypeStruct(populations.shape, f32), table] + [face] * 4,
        scratch_shapes=[
            VMEM((19, 19), f32),
            VMEM((160, 480), bf16),
            VMEM(populations.shape, f32),
            VMEM((19, size_x + 2, size_y + 16, size_z), f32),
            pltpu.SemaphoreType.DMA((PIECES + 1,)),
            pltpu.SemaphoreType.DMA((PIECES,)),
        ],
        compiler_params=pltpu.CompilerParams(vmem_limit_bytes=51 << 20),
        cost_estimate=pl.CostEstimate(flops=40_000_000, bytes_accessed=6_000_000, transcendentals=0),
        name="collide",
    )(relax_matrix, populations)


CHUNK = 512


def hot_rows(count, line):
    shape = (16, line.shape[1])
    offset = jnp.broadcast_to(line, shape) - lax.broadcasted_iota(jnp.int32, shape, 0)
    offset = offset.astype(jnp.int16)
    one, zero = jnp.ones(shape, bf16), jnp.zeros(shape, bf16)
    return jnp.concatenate(
        [jnp.where(offset == jnp.int16(b), one, zero) for b in range(0, count, 16)], axis=0
    )


def pick(table_ref, column, entry):
    rows, depth = table_ref.shape[0], table_ref.shape[1] // 2
    chunk = column.shape[1]
    hot = hot_rows(depth, column)
    hot = jnp.concatenate([hot, hot], axis=0)
    offset = entry - lax.broadcasted_iota(jnp.int32, (8, chunk), 0)
    acc = jnp.zeros((8, chunk), f32)
    found = jnp.dot(table_ref[...], hot, preferred_element_type=f32)
    for j in range(0, rows, 8):
        acc = jnp.where(offset == j, found[j : j + 8], acc)
    return jnp.sum(acc, axis=0, keepdims=True)


def member(direction, dirs, first=1, step=1):
    out = jnp.zeros(direction.shape, jnp.int32)
    for k, d in enumerate(dirs):
        out = jnp.where(direction == d, first + step * k, out)
    return out


def sides(direction):
    return (
        member(direction, XP),
        member(direction, XM),
        member(direction, YP),
        member(direction, YM),
    )


def tile_of(ref, k):
    start = pl.multiple_of(k * 1024, 1024)
    return jnp.concatenate(
        [ref[0, :, pl.ds(start + 128 * s, 128)] for s in range(8)], axis=0
    )


def line_of(ref, i):
    return jnp.concatenate([ref[pl.ds(4 * i + k, 1), :] for k in range(4)], axis=1)


def link_kernel(half, table_ref, cell_ref, dir_ref, value_ref, column, entry):
    def index(k, carry):
        cell, direction = tile_of(cell_ref, 8 * half + k), tile_of(dir_ref, 8 * half + k)
        xup, xdown, yup, ydown = sides(direction)
        forward = member(direction, CANON)
        backward = member(direction, [OPP[d] for d in CANON])
        wall = member(direction, WALL)
        back = (backward > 0).astype(jnp.int32)
        x = (cell >> 11) + back * ((xup > 0).astype(jnp.int32) - (xdown > 0).astype(jnp.int32))
        y = ((cell >> 7) & 15) + back * (
            (yup > 0).astype(jnp.int32) - (ydown > 0).astype(jnp.int32)
        )
        z = cell & 31
        bottom = (wall > 0) & (z == 0)
        z = z - (wall > 0).astype(jnp.int32)
        which = forward + backward - 1
        inside = (x >= 0) & (x < 16) & (y >= 0) & (y < 16) & (which >= 0)
        rows = pl.ds(pl.multiple_of(k * 8, 8), 8)
        column[rows, :] = jnp.where(bottom, cell >> 7, x * 16 + y)
        entry[rows, :] = jnp.where(bottom, 287 + wall, jnp.where(inside, which * 32 + z, -8))
        return carry

    lax.fori_loop(0, 8, index, 0)

    def one_chunk(i, carry):
        found = pick(table_ref, line_of(column, i), line_of(entry, i))
        for k in range(4):
            value_ref[pl.ds(4 * i + k, 1), :] = found[:, 128 * k : 128 * k + 128]
        return carry

    lax.fori_loop(0, 16, one_chunk, 0, unroll=True)


def interior_links(half, table, cells, dirs):
    shape = (64, 128)
    return pl.pallas_call(
        functools.partial(link_kernel, half),
        in_specs=[pl.BlockSpec(memory_space=VMEM)] * 3,
        out_specs=pl.BlockSpec(memory_space=VMEM),
        out_shape=jax.ShapeDtypeStruct(shape, f32),
        scratch_shapes=[VMEM(shape, jnp.int32)] * 2,
        compiler_params=pltpu.CompilerParams(vmem_limit_bytes=24 << 20),
        cost_estimate=pl.CostEstimate(
            flops=6_000_000_000, bytes_accessed=1_000_000, transcendentals=0
        ),
        name="interior_links",
    )(table, cells, dirs)


def scatter_kernel(
    first_ref, second_ref, cell_ref, dir_ref, grain_ref,
    xlow_ref, xhigh_ref, ylow_ref, yhigh_ref,
    ownx_low_ref, ownx_high_ref, owny_low_ref, owny_high_ref,
    self_ref, peer_ref, normal_ref, gap_ref, state_ref,
    out_ref,
    table, column, entry, frames, slots, signs,
):
    size = 16
    lane = lanes_of((size, 128))
    for side in range(2):
        for group in range(3):
            acc = jnp.zeros((size, 128), f32)
            for j in range(4 * group, min(4 * group + 4, 10)):
                d = (XP + XM)[j] if side == 0 else (YP + YM)[j]
                q = OPP[d]
                dx, dy, dz = DIRS[d]
                high = j < 5
                if side == 0:
                    along = dy
                    ref = xhigh_ref if high else xlow_ref
                    mine = ownx_high_ref if high else ownx_low_ref
                    k = (XM if high else XP).index(q)
                    ends = ref[5 * size : 5 * size + 1], ref[5 * size + 1 : 5 * size + 2]
                else:
                    along = dx
                    ref = yhigh_ref if high else ylow_ref
                    mine = owny_high_ref if high else owny_low_ref
                    k = (YM if high else YP).index(q)
                    ends = (jnp.zeros((1, 128), f32),) * 2
                face = ref[k * size : (k + 1) * size]
                if along == 1:
                    face = jnp.concatenate([face[1:], ends[1]], axis=0)
                elif along == -1:
                    face = jnp.concatenate([ends[0], face[:-1]], axis=0)
                if dz:
                    face = pltpu.roll(face, (-dz) % 128, 1)
                if d not in CANON:
                    face = face + mine[(j % 5) * size : (j % 5 + 1) * size]
                if dz == -1:
                    face = jnp.where(lane == 0, 0.0, face)
                shift = (j % 4) * LOW
                if shift:
                    face = pltpu.roll(face, shift, 1)
                acc = jnp.where((lane >= shift) & (lane < shift + LOW), face, acc)
            hi = acc.astype(bf16)
            lo = (acc - hi.astype(f32)).astype(bf16)
            row = 16 * (3 * side + group)
            table[row : row + 16, 0:128] = hi
            table[row : row + 16, 128:256] = lo

    def index(k, carry):
        cell, direction, grain = tile_of(cell_ref, k), tile_of(dir_ref, k), tile_of(grain_ref, k)
        xup, xdown, yup, ydown = sides(direction)
        zup = member(direction, [5, 11, 14, 15, 18], 1, 0)
        zdown = member(direction, WALL, 1, 0)
        x, y, z = cell >> 11, (cell >> 7) & 15, cell & 31
        jx = jnp.where(
            (x == 15) & (xup > 0), xup, jnp.where((x == 0) & (xdown > 0), xdown + 5, 0)
        )
        jy = jnp.where(
            (y == 15) & (yup > 0), yup, jnp.where((y == 0) & (ydown > 0), ydown + 5, 0)
        )
        which = jnp.where(jx > 0, jx, jy) - 1
        rows = pl.ds(pl.multiple_of(k * 8, 8), 8)
        column[rows, :] = (which & 3) * 32 + z
        place = (which >> 2) * 16 + jnp.where(jx > 0, y, 48 + x)
        entry[rows, :] = jnp.where(which >= 0, place, -8)
        frames[rows, :] = grain >> 7
        slots[rows, :] = grain & 127
        for c, (up, down) in enumerate(((xup, xdown), (yup, ydown), (zup, zdown))):
            signs[c, rows, :] = (up > 0).astype(f32) - (down > 0).astype(f32)
        return carry

    lax.fori_loop(0, 16, index, 0)
    row = lax.broadcasted_iota(jnp.int32, (32, CHUNK), 0)
    group = (row >= 9).astype(jnp.int32) + (row >= 18).astype(jnp.int32)
    frames_of = jnp.where(row < 27, row - 9 * group, -1)

    def one_chunk(value_ref, before, k, acc):
        i = before + k
        value = line_of(value_ref, k) + pick(table, line_of(column, i), line_of(entry, i))
        hit = frames_of == line_of(frames, i)
        sign = [line_of(signs.at[c], i) for c in range(3)]
        sign = jnp.where(group == 0, sign[0], jnp.where(group == 1, sign[1], sign[2]))
        sign = jnp.where(hit, sign, 0.0)
        terms = [(sign * part.astype(f32)).astype(bf16) for part in split3(value)]
        hot = hot_rows(128, line_of(slots, i))
        return acc + lax.dot_general(
            jnp.concatenate(terms, axis=0), hot, (((1,), (1,)), ((), ())), preferred_element_type=f32
        )

    acc = jnp.zeros((96, 128), f32)
    for before, value_ref in ((0, first_ref), (16, second_ref)):
        acc = lax.fori_loop(
            0, 16, functools.partial(one_chunk, value_ref, before), acc, unroll=True
        )
    rows = [acc[0:27] + (acc[32:59] + acc[64:91])]
    for ref in (self_ref, peer_ref):
        rows += [ref[0, :, 128 * t : 128 * t + 128].astype(f32) for t in range(4)]
    for c in range(3):
        rows += [normal_ref[0, c, :, 128 * t : 128 * t + 128] for t in range(4)]
    rows += [gap_ref[0, :, 128 * t : 128 * t + 128] for t in range(4)]
    rows += [state_ref[0, 0], jnp.zeros((1, 128), f32)]
    message = jnp.concatenate(rows, axis=0)
    for k in range(8):
        out_ref[k] = message


def link_sums(values, links, halos, faces, contacts):
    args = values + links + halos + faces + contacts
    square = (128, 128)
    return pl.pallas_call(
        scatter_kernel,
        in_specs=[pl.BlockSpec(memory_space=VMEM)] * len(args),
        out_specs=pl.BlockSpec(memory_space=VMEM),
        out_shape=jax.ShapeDtypeStruct((8, 56, 128), f32),
        scratch_shapes=[VMEM((96, 256), bf16)]
        + [VMEM(square, jnp.int32)] * 4
        + [VMEM((3,) + square, f32)],
        compiler_params=pltpu.CompilerParams(vmem_limit_bytes=24 << 20),
        cost_estimate=pl.CostEstimate(
            flops=2_000_000_000, bytes_accessed=500_000, transcendentals=0
        ),
        name="link_sums",
    )(*args)


def stream_kernel(centre_ref, xlow_ref, xhigh_ref, ylow_ref, yhigh_ref, out_ref, pad):
    step = pl.program_id(0)
    block_x = out_ref.shape[1]
    size_x, size_y = centre_ref.shape[1], centre_ref.shape[2]

    @pl.when(step == 0)
    def _():
        for q in range(19):
            pad[q, 1 : 1 + size_x, 8 : 8 + size_y] = centre_ref[q]
        for k in range(5):
            pad[YP[k], 1 : 1 + size_x, 7, :] = ylow_ref[k * size_x : (k + 1) * size_x]
            pad[YM[k], 1 : 1 + size_x, 8 + size_y, :] = yhigh_ref[k * size_x : (k + 1) * size_x]
            pad[XP[k], 0, 8 : 8 + size_y, :] = xlow_ref[k * size_y : (k + 1) * size_y]
            pad[XM[k], 1 + size_x, 8 : 8 + size_y, :] = xhigh_ref[k * size_y : (k + 1) * size_y]
        base = 5 * size_y
        for q, row in ((7, 7), (9, 8 + size_y)):
            pad[q, 0, row : row + 1, :] = xlow_ref[base + (row > 8) : base + (row > 8) + 1]
        for q, row in ((10, 7), (8, 8 + size_y)):
            pad[q, 1 + size_x, row : row + 1, :] = xhigh_ref[base + (row > 8) : base + (row > 8) + 1]

    lane = lanes_of((size_y, 128))

    def one_row(i, carry):
        x = step * block_x + i
        for q in range(19):
            dx, dy, dz = DIRS[q]
            moved = pad[q, 1 + x - dx, 8 - dy : 8 - dy + size_y, :]
            if dz:
                moved = pltpu.roll(moved, dz % 128, 1)
                wall = 0 if dz == 1 else 127
                moved = jnp.where(lane == wall, pad[OPP[q], 1 + x, 8 : 8 + size_y, :], moved)
            out_ref[q, i] = moved
        return carry

    lax.fori_loop(0, block_x, one_row, 0, unroll=True)


def passed(centre, xlow, xhigh, ylow, yhigh):
    _, size_x, size_y, size_z = centre.shape
    block_x = 8
    return pl.pallas_call(
        stream_kernel,
        grid=(size_x // block_x,),
        in_specs=[whole(a.shape) for a in (centre, xlow, xhigh, ylow, yhigh)],
        out_specs=pl.BlockSpec((19, block_x, size_y, size_z), lambda i: (0, i, 0, 0)),
        out_shape=jax.ShapeDtypeStruct(centre.shape, f32),
        scratch_shapes=[VMEM((19, size_x + 2, size_y + 16, size_z), f32)],
        compiler_params=pltpu.CompilerParams(vmem_limit_bytes=40 << 20),
        cost_estimate=pl.CostEstimate(flops=10_000_000, bytes_accessed=6_000_000, transcendentals=0),
        name="passed",
    )(centre, xlow, xhigh, ylow, yhigh)


def across(v, by):
    return pltpu.roll(v, by % 8, 0) if by % 8 else v


def look_up(table, index):
    return jnp.take_along_axis(table, index, axis=1)


def fold(sums_ref, stride, dxs):
    out = []
    for k in range(len(dxs)):
        for c in range(3):
            total = None
            for dyi in range(3):
                row = sums_ref[:, c * stride + 3 * k + dyi, :]
                row = across(row, dyi - 1)
                total = row if total is None else total + row
            out.append(total)
    return out


def column_index(contact, t):
    own = contact(0, t).astype(jnp.int32)
    peer = contact(1, t).astype(jnp.int32)
    return own, peer & 127, peer >> 7


def peer_tables(read, dxs):
    tables = {}
    for dxi in dxs:
        base = read(dxi - 1)
        for dyi in range(3):
            tables[3 * dxi + dyi] = across(base, 1 - dyi)
    return tables


def pick_peer(tables, slot, frame):
    found = jnp.zeros(slot.shape, f32)
    for k, table in tables.items():
        found = jnp.where(frame == k, look_up(table, slot), found)
    return found


def one_column(contact, vel, denom, impulse, store_impulse, sums_ref, dxs):
    indices = [column_index(contact, t) for t in range(4)]
    closing = [contact(5, t) for t in range(4)]
    for c in range(3):
        tables = peer_tables(lambda j: vel(j, c), dxs)
        for t in range(4):
            own, slot, frame = indices[t]
            gap = pick_peer(tables, slot, frame) - look_up(vel(0, c), jnp.minimum(own, 127))
            closing[t] = closing[t] + contact(2 + c, t) * gap
    kicks = []
    for t in range(4):
        new = jnp.maximum(0.0, impulse(t) - 0.5 * closing[t] / denom(t))
        new = jnp.where(indices[t][0] < 128, new, 0.0)
        store_impulse(t, new)
        kicks.append([[p.astype(f32) for p in split3(new * contact(2 + c, t))] for c in range(3)])
    every = len(dxs) == 3
    height = 16 if every else 8
    frames_of = lax.broadcasted_iota(jnp.int32, (height, 512), 0) + 3 * dxs[0]
    nt = (((1,), (1,)), ((), ()))

    def line(parts, y):
        return jnp.concatenate([p[y : y + 1, :] for p in parts], axis=1)

    for y in range(8):
        hit = frames_of == line([indices[t][2] for t in range(4)], y)
        hot_peer = hot_rows(128, line([indices[t][1] for t in range(4)], y))
        rows = [
            line([kicks[t][c][piece] for t in range(4)], y) for piece in range(3) for c in range(3)
        ]
        terms = [jnp.where(hit, r, 0.0) for r in rows]
        if not every:
            terms.append(jnp.zeros((8, 512), f32))
        terms = jnp.concatenate(terms, axis=0).astype(bf16)
        found = lax.dot_general(terms, hot_peer, nt, preferred_element_type=f32)
        step = 3 * height
        sums_ref[y, 0:step] = found[0:step] + (found[step : 2 * step] + found[2 * step : 3 * step])
        if every:
            hot_own = hot_rows(128, line([indices[t][0] for t in range(4)], y))
            mine = jnp.concatenate(rows + [jnp.zeros((7, 512), f32)], axis=0).astype(bf16)
            mine = lax.dot_general(mine, hot_own, nt, preferred_element_type=f32)
            mine = mine[0:3] + (mine[3:6] + mine[6:9])
            for c in range(3):
                sums_ref[y, 16 * c + 9 : 16 * c + 10] = mine[c : c + 1]


def fold_kernel(frames_ref, mine_ref, to_low_ref, to_high_ref):
    force = fold(frames_ref, 9, (0, 1, 2))
    for c in range(3):
        to_low_ref[c] = force[c]
        mine_ref[c] = force[3 + c]
        to_high_ref[c] = force[6 + c]
    for r in range(28):
        row = frames_ref[:, 27 + r, :]
        mine_ref[3 + r] = row
        if r < 24 or r == 27:
            k = 3 + min(r, 24)
            to_low_ref[k] = row
            to_high_ref[k] = row


def reach(j):
    return ((2,), (0, 1, 2), (0,))[j]


def prep_kernel(
    place_ref, mine_ref, low_ref, high_ref, force_ref, contact_ref, mass_ref, denom_ref
):
    y = place_ref[0]
    for c in range(3):
        force_ref[0, c] = row_of(mine_ref[c] + (low_ref[c] + high_ref[c]), y)
    for j, ref in enumerate((low_ref, mine_ref, high_ref)):
        contact_ref[j] = ref[3:27]
        mass_ref[j] = ref[ref.shape[0] - 1]
    for j in range(3):
        contact = lambda f, t: contact_ref[j, 4 * f + t]
        mass = lambda k: mass_ref[j + k]
        tables = peer_tables(mass, reach(j))
        for t in range(4):
            own, slot, frame = column_index(contact, t)
            denom_ref[j, t] = pick_peer(tables, slot, frame) + look_up(
                mass(0), jnp.minimum(own, 127)
            )


def row_of(v, y):
    hit = lax.broadcasted_iota(jnp.int32, (8, 128), 0) == y
    return jnp.sum(jnp.where(hit, v, 0.0), axis=0, keepdims=True)


def free_kernel(mine_ref, low_ref, high_ref, free_ref):
    for c in range(3):
        total = mine_ref[c] + (low_ref[c] + high_ref[c])
        free_ref[c] = mine_ref[27 + c] + mine_ref[30] * total


def sweep_kernel(
    step, place_ref, vel_ref, low_ref, high_ref, free_ref, contact_ref, mass_ref, denom_ref, *refs
):
    before = refs[0] if step else None
    moved_ref, impulse_ref, sums, kick = refs[1 if step else 0 :]
    last = step == SWEEPS - 1
    y = place_ref[0]
    speeds = (low_ref, vel_ref, high_ref)

    def store(j, t, value):
        if not last:
            impulse_ref[j, t] = value
        elif j == 1:
            impulse_ref[0, :, 128 * t : 128 * t + 128] = row_of(value, y)

    for j in range(3):
        dxs = reach(j)
        one_column(
            lambda f, t: contact_ref[j, 4 * f + t],
            lambda k, c: speeds[j + k][c],
            lambda t: denom_ref[j, t],
            lambda t: before[j, t] if step else jnp.zeros((8, 128), f32),
            lambda t, v: store(j, t, v),
            sums.at[j],
            dxs,
        )
        rows = fold(sums.at[j], 16 if len(dxs) == 3 else 8, dxs)
        for c in range(3):
            if j == 1:
                kick[j, c] = rows[3 + c] - sums[j, :, 16 * c + 9, :]
            else:
                kick[j, c] = rows[c]
    for c in range(3):
        moved = free_ref[c] + mass_ref[1] * (kick[1, c] + (kick[0, c] + kick[2, c]))
        if last:
            moved_ref[0, c] = row_of(moved, y)
        else:
            moved_ref[c] = moved


def edge_kernel(xhi_ref, xlo_ref, ylow_ref, yhigh_ref, after_ref, to_low_ref, to_high_ref):
    size = 16
    last = size - 1
    for out_ref, face_ref, first, second in (
        (to_high_ref, xhi_ref, size + last, 2 * size + last),
        (to_low_ref, xlo_ref, 2 * size, size),
    ):
        out_ref[0:80] = face_ref[...]
        corners = [ylow_ref[first : first + 1], yhigh_ref[second : second + 1]]
        out_ref[80:88] = jnp.concatenate(corners + [jnp.zeros((6, 128), f32)], axis=0)


def vmem_call(kernel, outs, args, scratch=(), flops=1_000_000, place=None):
    specs = [pl.BlockSpec(memory_space=VMEM) for _ in args]
    if place is not None:
        args = (place,) + tuple(args)
        specs = [pl.BlockSpec(memory_space=pltpu.SMEM)] + specs
    return pl.pallas_call(
        kernel,
        in_specs=specs,
        out_specs=[pl.BlockSpec(memory_space=VMEM) for _ in outs],
        out_shape=[jax.ShapeDtypeStruct(s, f32) for s in outs],
        scratch_shapes=list(scratch),
        compiler_params=pltpu.CompilerParams(vmem_limit_bytes=24 << 20),
        cost_estimate=pl.CostEstimate(flops=flops, bytes_accessed=500_000, transcendentals=0),
        name=getattr(kernel, "func", kernel).__name__,
    )(*args)


def shift(value, axis, by):
    size = lax.axis_size(axis)
    return lax.ppermute(value, axis, [(i, (i + by) % size) for i in range(size)])


def both_ways(to_low, to_high, axis, by):
    return shift(to_high, axis, by), shift(to_low, axis, -by)


def per_device(
    populations,
    relax_matrix,
    grain_state,
    link_cell,
    link_dir,
    link_grain,
    contact_self,
    contact_peer,
    contact_normal,
    contact_gap,
):
    place = lax.axis_index("gy").astype(jnp.int32).reshape(1)
    links = (link_cell, link_dir, link_grain)
    contacts = (
        contact_self,
        contact_peer,
        contact_normal.transpose(0, 2, 1, 3),
        contact_gap,
        grain_state,
    )

    centre, table, yhi, ylo, xhi, xlo = collide(populations, relax_matrix)
    ylow, yhigh = both_ways(ylo, yhi, "gy", 1)
    first = interior_links(0, table, link_cell, link_dir)
    to_low, to_high = vmem_call(edge_kernel, [(88, 128)] * 2, (xhi, xlo, ylow, yhigh, first))
    xlow, xhigh = both_ways(to_low, to_high, "gx", 1)
    second = interior_links(1, table, link_cell, link_dir)
    halos = (xlow, xhigh, ylow, yhigh)
    spread = link_sums((first, second), links, halos, (xlo, xhi, ylo, yhi), contacts)
    populations_next = passed(centre, *halos)

    spread = lax.all_to_all(spread, "gy", 0, 0)
    mine, *ends = vmem_call(
        fold_kernel, [(31, 8, 128), (28, 8, 128), (28, 8, 128)], (spread,)
    )
    near = both_ways(*ends, "gx", 1)
    (free,) = vmem_call(free_kernel, [(3, 8, 128)], (mine, *near))

    force, *static = vmem_call(
        prep_kernel,
        [(1, 3, 1, 128), (3, 24, 8, 128), (3, 8, 128), (3, 4, 8, 128)],
        (mine, *near),
        place=place,
    )
    scratch = [VMEM((3, 8, 48, 128), f32), VMEM((3, 3, 8, 128), f32)]
    moved, impulse = free, ()
    for step in range(SWEEPS):
        last = step == SWEEPS - 1
        moved, impulse = vmem_call(
            functools.partial(sweep_kernel, step),
            [(1, 3, 1, 128), (1, 1, 512)] if last else [(3, 8, 128), (3, 4, 8, 128)],
            (moved, *both_ways(moved, moved, "gx", 1), free, *static)
            + ((impulse,) if step else ()),
            scratch,
            place=place,
        )
    velocity = moved
    return (
        populations_next,
        force.transpose(0, 2, 1, 3),
        velocity.transpose(0, 2, 1, 3),
        impulse,
    )


def solution(mesh):
    placed = (
        P(None, "gx", "gy", None),
        P(),
        P("gx", "gy", None, None),
        P("gx", "gy", None),
        P("gx", "gy", None),
        P("gx", "gy", None),
        P("gx", "gy", None),
        P("gx", "gy", None),
        P("gx", "gy", None, None),
        P("gx", "gy", None),
    )
    return jax.shard_map(
        per_device,
        mesh=mesh,
        in_specs=placed,
        out_specs=(
            P(None, "gx", "gy", None),
            P("gx", "gy", None, None),
            P("gx", "gy", None, None),
            P("gx", "gy", None),
        ),
        check_vma=False,
    )
```

```python
import functools

import jax
import jax.numpy as jnp
from jax import lax
from jax.experimental import pallas as pl
from jax.experimental.pallas import tpu as pltpu
from jax.sharding import PartitionSpec as P

SWEEPS = 4
DIRS = [
    [0, 0, 0],
    [1, 0, 0],
    [-1, 0, 0],
    [0, 1, 0],
    [0, -1, 0],
    [0, 0, 1],
    [0, 0, -1],
    [1, 1, 0],
    [-1, -1, 0],
    [1, -1, 0],
    [-1, 1, 0],
    [1, 0, 1],
    [-1, 0, -1],
    [1, 0, -1],
    [-1, 0, 1],
    [0, 1, 1],
    [0, -1, -1],
    [0, 1, -1],
    [0, -1, 1],
]
OPP = [0, 2, 1, 4, 3, 6, 5, 8, 7, 10, 9, 12, 11, 14, 13, 16, 15, 18, 17]
WEIGHT = [1.0 / 3.0] + [1.0 / 18.0] * 6 + [1.0 / 36.0] * 12
XP = [1, 7, 9, 11, 13]
XM = [2, 8, 10, 12, 14]
YP = [3, 7, 10, 15, 17]
YM = [4, 8, 9, 16, 18]
CANON = [1, 3, 5, 7, 9, 11, 14, 15, 18]
WALL = [6, 12, 13, 16, 17]
LOW = 32
highest = lax.Precision.HIGHEST
f32 = jnp.float32
bf16 = jnp.bfloat16
VMEM = pltpu.VMEM


def whole(shape):
    return pl.BlockSpec(shape, lambda *_: (0,) * len(shape))


def lanes_of(shape):
    return lax.broadcasted_iota(jnp.int32, shape, len(shape) - 1)


def split3(v):
    hi = v.astype(bf16)
    rest = v - hi.astype(f32)
    mid = rest.astype(bf16)
    low = (rest - mid.astype(f32)).astype(bf16)
    return hi, mid, low


PIECES = 2


def collide_kernel(
    relax_hbm, pop_hbm, centre_hbm, table_ref, yhi_ref, ylo_ref, xhi_ref, xlo_ref,
    relax, left, pop, pad, in_sem, out_sem,
):
    size_x, size_y = pop.shape[1], pop.shape[2]
    piece_x = size_x // PIECES

    def arriving(i):
        part = pl.ds(i * piece_x, piece_x)
        return pltpu.make_async_copy(pop_hbm.at[:, part], pop.at[:, part], in_sem.at[i])

    def leaving(i):
        part = pl.ds(i * piece_x, piece_x)
        inner = pl.ds(1 + i * piece_x, piece_x)
        return pltpu.make_async_copy(
            pad.at[:, inner, 8 : 8 + size_y], centre_hbm.at[:, part], out_sem.at[i]
        )

    matrix = pltpu.make_async_copy(relax_hbm, relax, in_sem.at[PIECES])
    matrix.start()
    for i in range(PIECES):
        arriving(i).start()
    zero = jnp.zeros((size_x + 2, 8, 128), f32)
    for q in YP + YM:
        pad[q, :, 0:8] = zero
        pad[q, :, 8 + size_y :] = zero
    for q in XP + XM:
        pad[q, 0] = jnp.zeros(pad.shape[2:], f32)
        pad[q, size_x + 1] = jnp.zeros(pad.shape[2:], f32)
    matrix.wait()
    hi = relax[...].astype(bf16)
    lo = (relax[...] - hi.astype(f32)).astype(bf16)
    row = lax.broadcasted_iota(jnp.int32, (160, 19), 0)
    rows_of = (row >> 3 == lanes_of((160, 19))).astype(f32).astype(bf16)
    col = lanes_of((19, 480))
    col = col - 160 * ((col >= 160).astype(jnp.int32) + (col >= 320).astype(jnp.int32))
    cols_of = (lax.broadcasted_iota(jnp.int32, (19, 480), 0) == col >> 3).astype(f32).astype(bf16)
    spread = []
    for part in (hi, lo):
        tall = jnp.dot(rows_of, part, preferred_element_type=f32).astype(bf16)
        spread.append(jnp.dot(tall, cols_of, preferred_element_type=f32))
    row = lax.broadcasted_iota(jnp.int32, (160, 480), 0)
    col = lanes_of((160, 480))
    value = jnp.where(col < 320, spread[0], spread[1])
    left[...] = jnp.where(row & 7 == col & 7, value, 0.0).astype(bf16)

    def one_row(x, carry):
        f = [pop[q, x] for q in range(19)]
        rho = f[0]
        for q in range(1, 19):
            rho = rho + f[q]
        speeds = []
        inverse = 1.0 / rho
        for axis in range(3):
            total = None
            for q in range(1, 19, 2):
                sign = DIRS[q][axis]
                if sign:
                    diff = f[q] - f[q + 1] if sign > 0 else f[q + 1] - f[q]
                    total = diff if total is None else total + diff
            speeds.append(total * inverse)
        ux, uy, uz = speeds
        base = 1.0 - 1.5 * (ux * ux + uy * uy + uz * uz)
        neq = [f[0] - WEIGHT[0] * rho * base]
        for q in range(1, 19, 2):
            along = None
            for axis in range(3):
                sign = DIRS[q][axis]
                if sign:
                    if along is None:
                        along = speeds[axis]
                    else:
                        along = along + speeds[axis] if sign > 0 else along - speeds[axis]
            scale = WEIGHT[q] * rho
            even = scale * (base + 4.5 * (along * along))
            odd = scale * (3.0 * along)
            neq.append(f[q] - (even + odd))
            neq.append(f[q + 1] - (even - odd))
        tall = [jnp.concatenate([v[:8], v[8:]], axis=1) for v in neq]
        tall = jnp.concatenate(tall + [jnp.zeros((8, 256), f32)], axis=0)
        hi = tall.astype(bf16)
        lo = (tall - hi.astype(f32)).astype(bf16)
        relaxed = jnp.dot(
            left[...], jnp.concatenate([hi, lo, hi], axis=0), preferred_element_type=f32
        )
        for q in range(19):
            change = relaxed[8 * q : 8 * q + 8]
            out = f[q] - jnp.concatenate([change[:, :128], change[:, 128:]], axis=0)
            pad[q, 1 + x, 8 : 8 + size_y] = out
        return carry

    def one_piece(i, carry):
        arriving(i).wait()
        lax.fori_loop(0, piece_x, lambda k, c: one_row(i * piece_x + k, c), 0, unroll=True)
        leaving(i).start()
        return carry

    lax.fori_loop(0, PIECES, one_piece, 0)
    for k in range(5):
        yhi_ref[k * size_x : (k + 1) * size_x] = pad[YP[k], 1 : 1 + size_x, 7 + size_y, :]
        ylo_ref[k * size_x : (k + 1) * size_x] = pad[YM[k], 1 : 1 + size_x, 8, :]
        xhi_ref[k * size_y : (k + 1) * size_y] = pad[XP[k], size_x, 8 : 8 + size_y, :]
        xlo_ref[k * size_y : (k + 1) * size_y] = pad[XM[k], 1, 8 : 8 + size_y, :]

    cells = size_x * size_y
    nt = (((1,), (1,)), ((), ()))

    def put(row, count, terms, chooser):
        hi = terms.astype(bf16)
        lo = (terms - hi.astype(f32)).astype(bf16)
        pair = lax.dot_general(chooser, hi, nt, preferred_element_type=f32)
        pair = pair + lax.dot_general(chooser, lo, nt, preferred_element_type=f32)
        hi = pair.astype(bf16)
        table_ref[row : row + count, 0:cells] = hi
        table_ref[row : row + count, cells:] = (pair - hi.astype(f32)).astype(bf16)

    for dz in range(2):
        row = lax.broadcasted_iota(jnp.int32, (LOW, 256), 0)
        col = lanes_of((LOW, 256))
        chooser = ((col == row) | (col == row + 128 + dz)).astype(f32).astype(bf16)
        for i, d in enumerate(CANON):
            dx, dy, climb = DIRS[d]
            if climb == dz:
                own = pad[d, 1 : 1 + size_x, 8 : 8 + size_y, :]
                other = pad[
                    OPP[d], 1 + dx : 1 + dx + size_x, 8 + dy : 8 + dy + size_y, :
                ]
                terms = [v.reshape(cells, 128) for v in (own, other)]
                put(LOW * i, LOW, jnp.concatenate(terms, axis=1), chooser)
    row = lax.broadcasted_iota(jnp.int32, (16, 640), 0)
    chooser = jnp.where(lanes_of((16, 640)) == 128 * row, 2.0, 0.0).astype(bf16)
    terms = [pad[d, 1 : 1 + size_x, 8 : 8 + size_y, :].reshape(cells, 128) for d in WALL]
    put(LOW * len(CANON), 16, jnp.concatenate(terms, axis=1), chooser)
    for i in range(PIECES):
        leaving(i).wait()


def collide(populations, relax_matrix):
    _, size_x, size_y, size_z = populations.shape
    face = jax.ShapeDtypeStruct((5 * size_y, size_z), f32)
    table = jax.ShapeDtypeStruct((LOW * len(CANON) + 16, 2 * size_x * size_y), bf16)
    return pl.pallas_call(
        collide_kernel,
        in_specs=[pl.BlockSpec(memory_space=pltpu.HBM)] * 2,
        out_specs=[pl.BlockSpec(memory_space=pltpu.HBM)] + [pl.BlockSpec(memory_space=VMEM)] * 5,
        out_shape=[jax.ShapeDtypeStruct(populations.shape, f32), table] + [face] * 4,
        scratch_shapes=[
            VMEM((19, 19), f32),
            VMEM((160, 480), bf16),
            VMEM(populations.shape, f32),
            VMEM((19, size_x + 2, size_y + 16, size_z), f32),
            pltpu.SemaphoreType.DMA((PIECES + 1,)),
            pltpu.SemaphoreType.DMA((PIECES,)),
        ],
        compiler_params=pltpu.CompilerParams(vmem_limit_bytes=51 << 20),
        cost_estimate=pl.CostEstimate(flops=40_000_000, bytes_accessed=6_000_000, transcendentals=0),
        name="collide",
    )(relax_matrix, populations)


CHUNK = 512


def hot_rows(count, line):
    shape = (16, line.shape[1])
    offset = jnp.broadcast_to(line, shape) - lax.broadcasted_iota(jnp.int32, shape, 0)
    offset = offset.astype(jnp.int16)
    one, zero = jnp.ones(shape, bf16), jnp.zeros(shape, bf16)
    return jnp.concatenate(
        [jnp.where(offset == jnp.int16(b), one, zero) for b in range(0, count, 16)], axis=0
    )


def pick(table_ref, column, entry):
    rows, depth = table_ref.shape[0], table_ref.shape[1] // 2
    chunk = column.shape[1]
    hot = hot_rows(depth, column)
    hot = jnp.concatenate([hot, hot], axis=0)
    offset = entry - lax.broadcasted_iota(jnp.int32, (8, chunk), 0)
    acc = jnp.zeros((8, chunk), f32)
    found = jnp.dot(table_ref[...], hot, preferred_element_type=f32)
    for j in range(0, rows, 8):
        acc = jnp.where(offset == j, found[j : j + 8], acc)
    return jnp.sum(acc, axis=0, keepdims=True)


def member(direction, dirs, first=1, step=1):
    out = jnp.zeros(direction.shape, jnp.int32)
    for k, d in enumerate(dirs):
        out = jnp.where(direction == d, first + step * k, out)
    return out


def sides(direction):
    return (
        member(direction, XP),
        member(direction, XM),
        member(direction, YP),
        member(direction, YM),
    )


def tile_of(ref, k):
    start = pl.multiple_of(k * 1024, 1024)
    return jnp.concatenate(
        [ref[0, :, pl.ds(start + 128 * s, 128)] for s in range(8)], axis=0
    )


def line_of(ref, i):
    return jnp.concatenate([ref[pl.ds(4 * i + k, 1), :] for k in range(4)], axis=1)


def link_kernel(half, table_ref, cell_ref, dir_ref, value_ref, column, entry):
    def index(k, carry):
        cell, direction = tile_of(cell_ref, 8 * half + k), tile_of(dir_ref, 8 * half + k)
        xup, xdown, yup, ydown = sides(direction)
        forward = member(direction, CANON)
        backward = member(direction, [OPP[d] for d in CANON])
        wall = member(direction, WALL)
        back = (backward > 0).astype(jnp.int32)
        x = (cell >> 11) + back * ((xup > 0).astype(jnp.int32) - (xdown > 0).astype(jnp.int32))
        y = ((cell >> 7) & 15) + back * (
            (yup > 0).astype(jnp.int32) - (ydown > 0).astype(jnp.int32)
        )
        z = cell & 31
        bottom = (wall > 0) & (z == 0)
        z = z - (wall > 0).astype(jnp.int32)
        which = forward + backward - 1
        inside = (x >= 0) & (x < 16) & (y >= 0) & (y < 16) & (which >= 0)
        rows = pl.ds(pl.multiple_of(k * 8, 8), 8)
        column[rows, :] = jnp.where(bottom, cell >> 7, x * 16 + y)
        entry[rows, :] = jnp.where(bottom, 287 + wall, jnp.where(inside, which * 32 + z, -8))
        return carry

    lax.fori_loop(0, 8, index, 0)

    def one_chunk(i, carry):
        found = pick(table_ref, line_of(column, i), line_of(entry, i))
        for k in range(4):
            value_ref[pl.ds(4 * i + k, 1), :] = found[:, 128 * k : 128 * k + 128]
        return carry

    lax.fori_loop(0, 16, one_chunk, 0, unroll=True)


def interior_links(half, table, cells, dirs):
    shape = (64, 128)
    return pl.pallas_call(
        functools.partial(link_kernel, half),
        in_specs=[pl.BlockSpec(memory_space=VMEM)] * 3,
        out_specs=pl.BlockSpec(memory_space=VMEM),
        out_shape=jax.ShapeDtypeStruct(shape, f32),
        scratch_shapes=[VMEM(shape, jnp.int32)] * 2,
        compiler_params=pltpu.CompilerParams(vmem_limit_bytes=24 << 20),
        cost_estimate=pl.CostEstimate(
            flops=6_000_000_000, bytes_accessed=1_000_000, transcendentals=0
        ),
        name="interior_links",
    )(table, cells, dirs)


def scatter_kernel(
    first_ref, second_ref, cell_ref, dir_ref, grain_ref,
    xlow_ref, xhigh_ref, ylow_ref, yhigh_ref,
    ownx_low_ref, ownx_high_ref, owny_low_ref, owny_high_ref,
    self_ref, peer_ref, normal_ref, gap_ref, state_ref,
    out_ref,
    table, column, entry, frames, slots, signs,
):
    size = 16
    lane = lanes_of((size, 128))
    for side in range(2):
        for group in range(3):
            acc = jnp.zeros((size, 128), f32)
            for j in range(4 * group, min(4 * group + 4, 10)):
                d = (XP + XM)[j] if side == 0 else (YP + YM)[j]
                q = OPP[d]
                dx, dy, dz = DIRS[d]
                high = j < 5
                if side == 0:
                    along = dy
                    ref = xhigh_ref if high else xlow_ref
                    mine = ownx_high_ref if high else ownx_low_ref
                    k = (XM if high else XP).index(q)
                    ends = ref[5 * size : 5 * size + 1], ref[5 * size + 1 : 5 * size + 2]
                else:
                    along = dx
                    ref = yhigh_ref if high else ylow_ref
                    mine = owny_high_ref if high else owny_low_ref
                    k = (YM if high else YP).index(q)
                    ends = (jnp.zeros((1, 128), f32),) * 2
                face = ref[k * size : (k + 1) * size]
                if along == 1:
                    face = jnp.concatenate([face[1:], ends[1]], axis=0)
                elif along == -1:
                    face = jnp.concatenate([ends[0], face[:-1]], axis=0)
                if dz:
                    face = pltpu.roll(face, (-dz) % 128, 1)
                if d not in CANON:
                    face = face + mine[(j % 5) * size : (j % 5 + 1) * size]
                if dz == -1:
                    face = jnp.where(lane == 0, 0.0, face)
                shift = (j % 4) * LOW
                if shift:
                    face = pltpu.roll(face, shift, 1)
                acc = jnp.where((lane >= shift) & (lane < shift + LOW), face, acc)
            hi = acc.astype(bf16)
            lo = (acc - hi.astype(f32)).astype(bf16)
            row = 16 * (3 * side + group)
            table[row : row + 16, 0:128] = hi
            table[row : row + 16, 128:256] = lo

    def index(k, carry):
        cell, direction, grain = tile_of(cell_ref, k), tile_of(dir_ref, k), tile_of(grain_ref, k)
        xup, xdown, yup, ydown = sides(direction)
        zup = member(direction, [5, 11, 14, 15, 18], 1, 0)
        zdown = member(direction, WALL, 1, 0)
        x, y, z = cell >> 11, (cell >> 7) & 15, cell & 31
        jx = jnp.where(
            (x == 15) & (xup > 0), xup, jnp.where((x == 0) & (xdown > 0), xdown + 5, 0)
        )
        jy = jnp.where(
            (y == 15) & (yup > 0), yup, jnp.where((y == 0) & (ydown > 0), ydown + 5, 0)
        )
        which = jnp.where(jx > 0, jx, jy) - 1
        rows = pl.ds(pl.multiple_of(k * 8, 8), 8)
        column[rows, :] = (which & 3) * 32 + z
        place = (which >> 2) * 16 + jnp.where(jx > 0, y, 48 + x)
        entry[rows, :] = jnp.where(which >= 0, place, -8)
        frames[rows, :] = grain >> 7
        slots[rows, :] = grain & 127
        for c, (up, down) in enumerate(((xup, xdown), (yup, ydown), (zup, zdown))):
            signs[c, rows, :] = (up > 0).astype(f32) - (down > 0).astype(f32)
        return carry

    lax.fori_loop(0, 16, index, 0)
    row = lax.broadcasted_iota(jnp.int32, (32, CHUNK), 0)
    group = (row >= 9).astype(jnp.int32) + (row >= 18).astype(jnp.int32)
    frames_of = jnp.where(row < 27, row - 9 * group, -1)

    def one_chunk(value_ref, before, k, acc):
        i = before + k
        value = line_of(value_ref, k) + pick(table, line_of(column, i), line_of(entry, i))
        hit = frames_of == line_of(frames, i)
        sign = [line_of(signs.at[c], i) for c in range(3)]
        sign = jnp.where(group == 0, sign[0], jnp.where(group == 1, sign[1], sign[2]))
        sign = jnp.where(hit, sign, 0.0)
        terms = [(sign * part.astype(f32)).astype(bf16) for part in split3(value)]
        hot = hot_rows(128, line_of(slots, i))
        return acc + lax.dot_general(
            jnp.concatenate(terms, axis=0), hot, (((1,), (1,)), ((), ())), preferred_element_type=f32
        )

    acc = jnp.zeros((96, 128), f32)
    for before, value_ref in ((0, first_ref), (16, second_ref)):
        acc = lax.fori_loop(
            0, 16, functools.partial(one_chunk, value_ref, before), acc, unroll=True
        )
    rows = [acc[0:27] + (acc[32:59] + acc[64:91])]
    for ref in (self_ref, peer_ref):
        rows += [ref[0, :, 128 * t : 128 * t + 128].astype(f32) for t in range(4)]
    for c in range(3):
        rows += [normal_ref[0, c, :, 128 * t : 128 * t + 128] for t in range(4)]
    rows += [gap_ref[0, :, 128 * t : 128 * t + 128] for t in range(4)]
    rows += [state_ref[0, 0], jnp.zeros((1, 128), f32)]
    message = jnp.concatenate(rows, axis=0)
    for k in range(8):
        out_ref[k] = message


def link_sums(values, links, halos, faces, contacts):
    args = values + links + halos + faces + contacts
    square = (128, 128)
    return pl.pallas_call(
        scatter_kernel,
        in_specs=[pl.BlockSpec(memory_space=VMEM)] * len(args),
        out_specs=pl.BlockSpec(memory_space=VMEM),
        out_shape=jax.ShapeDtypeStruct((8, 56, 128), f32),
        scratch_shapes=[VMEM((96, 256), bf16)]
        + [VMEM(square, jnp.int32)] * 4
        + [VMEM((3,) + square, f32)],
        compiler_params=pltpu.CompilerParams(vmem_limit_bytes=24 << 20),
        cost_estimate=pl.CostEstimate(
            flops=2_000_000_000, bytes_accessed=500_000, transcendentals=0
        ),
        name="link_sums",
    )(*args)


def stream_kernel(centre_ref, xlow_ref, xhigh_ref, ylow_ref, yhigh_ref, out_ref, pad):
    step = pl.program_id(0)
    block_x = out_ref.shape[1]
    size_x, size_y = centre_ref.shape[1], centre_ref.shape[2]

    @pl.when(step == 0)
    def _():
        for q in range(19):
            pad[q, 1 : 1 + size_x, 8 : 8 + size_y] = centre_ref[q]
        for k in range(5):
            pad[YP[k], 1 : 1 + size_x, 7, :] = ylow_ref[k * size_x : (k + 1) * size_x]
            pad[YM[k], 1 : 1 + size_x, 8 + size_y, :] = yhigh_ref[k * size_x : (k + 1) * size_x]
            pad[XP[k], 0, 8 : 8 + size_y, :] = xlow_ref[k * size_y : (k + 1) * size_y]
            pad[XM[k], 1 + size_x, 8 : 8 + size_y, :] = xhigh_ref[k * size_y : (k + 1) * size_y]
        base = 5 * size_y
        for q, row in ((7, 7), (9, 8 + size_y)):
            pad[q, 0, row : row + 1, :] = xlow_ref[base + (row > 8) : base + (row > 8) + 1]
        for q, row in ((10, 7), (8, 8 + size_y)):
            pad[q, 1 + size_x, row : row + 1, :] = xhigh_ref[base + (row > 8) : base + (row > 8) + 1]

    lane = lanes_of((size_y, 128))

    def one_row(i, carry):
        x = step * block_x + i
        for q in range(19):
            dx, dy, dz = DIRS[q]
            moved = pad[q, 1 + x - dx, 8 - dy : 8 - dy + size_y, :]
            if dz:
                moved = pltpu.roll(moved, dz % 128, 1)
                wall = 0 if dz == 1 else 127
                moved = jnp.where(lane == wall, pad[OPP[q], 1 + x, 8 : 8 + size_y, :], moved)
            out_ref[q, i] = moved
        return carry

    lax.fori_loop(0, block_x, one_row, 0, unroll=True)


def passed(centre, xlow, xhigh, ylow, yhigh):
    _, size_x, size_y, size_z = centre.shape
    block_x = 8
    return pl.pallas_call(
        stream_kernel,
        grid=(size_x // block_x,),
        in_specs=[whole(a.shape) for a in (centre, xlow, xhigh, ylow, yhigh)],
        out_specs=pl.BlockSpec((19, block_x, size_y, size_z), lambda i: (0, i, 0, 0)),
        out_shape=jax.ShapeDtypeStruct(centre.shape, f32),
        scratch_shapes=[VMEM((19, size_x + 2, size_y + 16, size_z), f32)],
        compiler_params=pltpu.CompilerParams(vmem_limit_bytes=40 << 20),
        cost_estimate=pl.CostEstimate(flops=10_000_000, bytes_accessed=6_000_000, transcendentals=0),
        name="passed",
    )(centre, xlow, xhigh, ylow, yhigh)


def across(v, by):
    return pltpu.roll(v, by % 8, 0) if by % 8 else v


def look_up(table, index):
    return jnp.take_along_axis(table, index, axis=1)


def fold(sums_ref, stride, dxs):
    out = []
    for k in range(len(dxs)):
        for c in range(3):
            total = None
            for dyi in range(3):
                row = sums_ref[:, c * stride + 3 * k + dyi, :]
                row = across(row, dyi - 1)
                total = row if total is None else total + row
            out.append(total)
    return out


def column_index(contact, t):
    own = contact(0, t).astype(jnp.int32)
    peer = contact(1, t).astype(jnp.int32)
    return own, peer & 127, peer >> 7


def peer_tables(read, dxs):
    tables = {}
    for dxi in dxs:
        base = read(dxi - 1)
        for dyi in range(3):
            tables[3 * dxi + dyi] = across(base, 1 - dyi)
    return tables


def pick_peer(tables, slot, frame):
    found = jnp.zeros(slot.shape, f32)
    for k, table in tables.items():
        found = jnp.where(frame == k, look_up(table, slot), found)
    return found


def one_column(contact, vel, denom, impulse, store_impulse, sums_ref, dxs):
    indices = [column_index(contact, t) for t in range(4)]
    closing = [contact(5, t) for t in range(4)]
    for c in range(3):
        tables = peer_tables(lambda j: vel(j, c), dxs)
        for t in range(4):
            own, slot, frame = indices[t]
            gap = pick_peer(tables, slot, frame) - look_up(vel(0, c), jnp.minimum(own, 127))
            closing[t] = closing[t] + contact(2 + c, t) * gap
    kicks = []
    for t in range(4):
        new = jnp.maximum(0.0, impulse(t) - 0.5 * closing[t] / denom(t))
        new = jnp.where(indices[t][0] < 128, new, 0.0)
        store_impulse(t, new)
        kicks.append([[p.astype(f32) for p in split3(new * contact(2 + c, t))] for c in range(3)])
    every = len(dxs) == 3
    height = 32 if every else 16
    each = 9 if every else 3
    row = lax.broadcasted_iota(jnp.int32, (height, 512), 0)
    group = (row >= each).astype(jnp.int32) + (row >= 2 * each).astype(jnp.int32)
    frames_of = jnp.where(row < 3 * each, row - each * group + 3 * dxs[0], -1)
    nt = (((1,), (1,)), ((), ()))

    def line(parts, y):
        return jnp.concatenate([p[y : y + 1, :] for p in parts], axis=1)

    for y in range(8):
        hit = frames_of == line([indices[t][2] for t in range(4)], y)
        hot_peer = hot_rows(128, line([indices[t][1] for t in range(4)], y))
        rows = [
            line([kicks[t][c][piece] for t in range(4)], y) for piece in range(3) for c in range(3)
        ]
        terms = []
        for piece in range(3):
            kx, ky, kz = rows[3 * piece : 3 * piece + 3]
            term = jnp.where(group == 0, kx, jnp.where(group == 1, ky, kz))
            terms.append(jnp.where(hit, term, 0.0).astype(bf16))
        terms = jnp.concatenate(terms, axis=0)
        found = lax.dot_general(terms, hot_peer, nt, preferred_element_type=f32)
        sums_ref[y, 0:height] = found[0:height] + (
            found[height : 2 * height] + found[2 * height : 3 * height]
        )
        if every:
            hot_own = hot_rows(128, line([indices[t][0] for t in range(4)], y))
            mine = jnp.concatenate(rows + [jnp.zeros((7, 512), f32)], axis=0).astype(bf16)
            mine = lax.dot_general(mine, hot_own, nt, preferred_element_type=f32)
            mine = mine[0:3] + (mine[3:6] + mine[6:9])
            for c in range(3):
                sums_ref[y, 32 + c : 33 + c] = mine[c : c + 1]


def fold_kernel(frames_ref, mine_ref, to_low_ref, to_high_ref):
    force = fold(frames_ref, 9, (0, 1, 2))
    for c in range(3):
        to_low_ref[c] = force[c]
        mine_ref[c] = force[3 + c]
        to_high_ref[c] = force[6 + c]
    for r in range(28):
        row = frames_ref[:, 27 + r, :]
        mine_ref[3 + r] = row
        if r < 24 or r == 27:
            k = 3 + min(r, 24)
            to_low_ref[k] = row
            to_high_ref[k] = row


def reach(j):
    return ((2,), (0, 1, 2), (0,))[j]


def prep_kernel(
    place_ref, mine_ref, low_ref, high_ref, force_ref, contact_ref, mass_ref, denom_ref
):
    y = place_ref[0]
    for c in range(3):
        force_ref[0, c] = row_of(mine_ref[c] + (low_ref[c] + high_ref[c]), y)
    for j, ref in enumerate((low_ref, mine_ref, high_ref)):
        contact_ref[j] = ref[3:27]
        mass_ref[j] = ref[ref.shape[0] - 1]
    for j in range(3):
        contact = lambda f, t: contact_ref[j, 4 * f + t]
        mass = lambda k: mass_ref[j + k]
        tables = peer_tables(mass, reach(j))
        for t in range(4):
            own, slot, frame = column_index(contact, t)
            denom_ref[j, t] = pick_peer(tables, slot, frame) + look_up(
                mass(0), jnp.minimum(own, 127)
            )


def row_of(v, y):
    hit = lax.broadcasted_iota(jnp.int32, (8, 128), 0) == y
    return jnp.sum(jnp.where(hit, v, 0.0), axis=0, keepdims=True)


def free_kernel(mine_ref, low_ref, high_ref, free_ref):
    for c in range(3):
        total = mine_ref[c] + (low_ref[c] + high_ref[c])
        free_ref[c] = mine_ref[27 + c] + mine_ref[30] * total


def sweep_kernel(
    step, place_ref, vel_ref, low_ref, high_ref, free_ref, contact_ref, mass_ref, denom_ref, *refs
):
    before = refs[0] if step else None
    moved_ref, impulse_ref, sums, kick = refs[1 if step else 0 :]
    last = step == SWEEPS - 1
    y = place_ref[0]
    speeds = (low_ref, vel_ref, high_ref)

    def store(j, t, value):
        if not last:
            impulse_ref[j, t] = value
        elif j == 1:
            impulse_ref[0, :, 128 * t : 128 * t + 128] = row_of(value, y)

    for j in range(3):
        dxs = reach(j)
        one_column(
            lambda f, t: contact_ref[j, 4 * f + t],
            lambda k, c: speeds[j + k][c],
            lambda t: denom_ref[j, t],
            lambda t: before[j, t] if step else jnp.zeros((8, 128), f32),
            lambda t, v: store(j, t, v),
            sums.at[j],
            dxs,
        )
        rows = fold(sums.at[j], 3 * len(dxs), dxs)
        for c in range(3):
            if j == 1:
                kick[j, c] = rows[3 + c] - sums[j, :, 32 + c, :]
            else:
                kick[j, c] = rows[c]
    for c in range(3):
        moved = free_ref[c] + mass_ref[1] * (kick[1, c] + (kick[0, c] + kick[2, c]))
        if last:
            moved_ref[0, c] = row_of(moved, y)
        else:
            moved_ref[c] = moved


def edge_kernel(xhi_ref, xlo_ref, ylow_ref, yhigh_ref, after_ref, to_low_ref, to_high_ref):
    size = 16
    last = size - 1
    for out_ref, face_ref, first, second in (
        (to_high_ref, xhi_ref, size + last, 2 * size + last),
        (to_low_ref, xlo_ref, 2 * size, size),
    ):
        out_ref[0:80] = face_ref[...]
        corners = [ylow_ref[first : first + 1], yhigh_ref[second : second + 1]]
        out_ref[80:88] = jnp.concatenate(corners + [jnp.zeros((6, 128), f32)], axis=0)


def vmem_call(kernel, outs, args, scratch=(), flops=1_000_000, place=None):
    specs = [pl.BlockSpec(memory_space=VMEM) for _ in args]
    if place is not None:
        args = (place,) + tuple(args)
        specs = [pl.BlockSpec(memory_space=pltpu.SMEM)] + specs
    return pl.pallas_call(
        kernel,
        in_specs=specs,
        out_specs=[pl.BlockSpec(memory_space=VMEM) for _ in outs],
        out_shape=[jax.ShapeDtypeStruct(s, f32) for s in outs],
        scratch_shapes=list(scratch),
        compiler_params=pltpu.CompilerParams(vmem_limit_bytes=24 << 20),
        cost_estimate=pl.CostEstimate(flops=flops, bytes_accessed=500_000, transcendentals=0),
        name=getattr(kernel, "func", kernel).__name__,
    )(*args)


def shift(value, axis, by):
    size = lax.axis_size(axis)
    return lax.ppermute(value, axis, [(i, (i + by) % size) for i in range(size)])


def both_ways(to_low, to_high, axis, by):
    return shift(to_high, axis, by), shift(to_low, axis, -by)


def per_device(
    populations,
    relax_matrix,
    grain_state,
    link_cell,
    link_dir,
    link_grain,
    contact_self,
    contact_peer,
    contact_normal,
    contact_gap,
):
    place = lax.axis_index("gy").astype(jnp.int32).reshape(1)
    links = (link_cell, link_dir, link_grain)
    contacts = (
        contact_self,
        contact_peer,
        contact_normal.transpose(0, 2, 1, 3),
        contact_gap,
        grain_state,
    )

    centre, table, yhi, ylo, xhi, xlo = collide(populations, relax_matrix)
    ylow, yhigh = both_ways(ylo, yhi, "gy", 1)
    first = interior_links(0, table, link_cell, link_dir)
    to_low, to_high = vmem_call(edge_kernel, [(88, 128)] * 2, (xhi, xlo, ylow, yhigh, first))
    xlow, xhigh = both_ways(to_low, to_high, "gx", 1)
    second = interior_links(1, table, link_cell, link_dir)
    halos = (xlow, xhigh, ylow, yhigh)
    spread = link_sums((first, second), links, halos, (xlo, xhi, ylo, yhi), contacts)
    populations_next = passed(centre, *halos)

    spread = lax.all_to_all(spread, "gy", 0, 0)
    mine, *ends = vmem_call(
        fold_kernel, [(31, 8, 128), (28, 8, 128), (28, 8, 128)], (spread,)
    )
    near = both_ways(*ends, "gx", 1)
    (free,) = vmem_call(free_kernel, [(3, 8, 128)], (mine, *near))

    force, *static = vmem_call(
        prep_kernel,
        [(1, 3, 1, 128), (3, 24, 8, 128), (3, 8, 128), (3, 4, 8, 128)],
        (mine, *near),
        place=place,
    )
    scratch = [VMEM((3, 8, 48, 128), f32), VMEM((3, 3, 8, 128), f32)]
    moved, impulse = free, ()
    for step in range(SWEEPS):
        last = step == SWEEPS - 1
        moved, impulse = vmem_call(
            functools.partial(sweep_kernel, step),
            [(1, 3, 1, 128), (1, 1, 512)] if last else [(3, 8, 128), (3, 4, 8, 128)],
            (moved, *both_ways(moved, moved, "gx", 1), free, *static)
            + ((impulse,) if step else ()),
            scratch,
            place=place,
        )
    velocity = moved
    return (
        populations_next,
        force.transpose(0, 2, 1, 3),
        velocity.transpose(0, 2, 1, 3),
        impulse,
    )


def solution(mesh):
    placed = (
        P(None, "gx", "gy", None),
        P(),
        P("gx", "gy", None, None),
        P("gx", "gy", None),
        P("gx", "gy", None),
        P("gx", "gy", None),
        P("gx", "gy", None),
        P("gx", "gy", None),
        P("gx", "gy", None, None),
        P("gx", "gy", None),
    )
    return jax.shard_map(
        per_device,
        mesh=mesh,
        in_specs=placed,
        out_specs=(
            P(None, "gx", "gy", None),
            P("gx", "gy", None, None),
            P("gx", "gy", None, None),
            P("gx", "gy", None),
        ),
        check_vma=False,
    )
```
